32 devices in a mesh: batch: 8 (over z, x), head: 4 (over y, core).
Axes of the slice: x: 2, y: 2, z: 4, core: 2. Of those that a mesh axis runs over, the one named last changes fastest.
Arguments:
- patches: bfloat16 [8, 3136, 768], P('batch', 'head'), may hold values from -8 to 8
- bucket: int32 [8], P('batch'), may hold values from 0 to 1
- labels: int32 [8], P('batch'), may hold values from 0 to 399
- partner: int32 [8], P('batch'), may hold values from 0 to 7, as said below
- patch_weight: float32 [768, 768], P(('batch', 'head')), may hold values from -0.21875 to 0.21875
- norm_params: float32 [8, 768], P(None, ('batch', 'head')), may hold values from -2.5 to 2.5
- head_weight: float32 [768, 400], P(('batch', 'head')), may hold values from -0.4375 to 0.4375
- proj_weight: float32 [768, 256], P(('batch', 'head')), may hold values from -0.21875 to 0.21875
- attn_in: float32 [2, 768, 3, 768], P(None, 'batch', None, 'head'), may hold values from -0.21875 to 0.21875
- attn_out: float32 [2, 768, 768], P(None, 'head', 'batch'), may hold values from -0.875 to 0.875
- mlp_up: float32 [768, 3072], P('batch', 'head'), may hold values from -0.21875 to 0.21875
- mlp_down: float32 [3072, 768], P('head', 'batch'), may hold values from -0.109375 to 0.109375
- first_patch: float32 [768, 768], P(('batch', 'head')), may hold values from -0.001953125 to 0.001953125
- first_norms: float32 [8, 768], P(None, ('batch', 'head')), may hold values from -0.009765625 to 0.009765625
- first_head: float32 [768, 400], P(('batch', 'head')), may hold values from -0.001953125 to 0.001953125
- first_proj: float32 [768, 256], P(('batch', 'head')), may hold values from -0.001953125 to 0.001953125
- first_qkv: float32 [2, 768, 3, 768], P(None, 'batch', None, 'head'), may hold values from -0.001953125 to 0.001953125
- first_out: float32 [2, 768, 768], P(None, 'head', 'batch'), may hold values from -0.001953125 to 0.001953125
- first_up: float32 [768, 3072], P('batch', 'head'), may hold values from -0.00036621094 to 0.00036621094
- first_down: float32 [3072, 768], P('head', 'batch'), may hold values from -0.001953125 to 0.001953125
- second_patch: float32 [768, 768], P(('batch', 'head')), may hold values from 9.490403e-08 to 3.7961613e-07
- second_norms: float32 [8, 768], P(None, ('batch', 'head')), may hold values from 2.3726009e-06 to 9.4904035e-06
- second_head: float32 [768, 400], P(('batch', 'head')), may hold values from 9.490403e-08 to 3.7961613e-07
- second_proj: float32 [768, 256], P(('batch', 'head')), may hold values from 9.490403e-08 to 3.7961613e-07
- second_qkv: float32 [2, 768, 3, 768], P(None, 'batch', None, 'head'), may hold values from 9.490403e-08 to 3.7961613e-07
- second_out: float32 [2, 768, 768], P(None, 'head', 'batch'), may hold values from 9.490403e-08 to 3.7961613e-07
- second_up: float32 [768, 3072], P('batch', 'head'), may hold values from 4.7452016e-09 to 1.8980806e-08
- second_down: float32 [3072, 768], P('head', 'batch'), may hold values from 9.490403e-08 to 3.7961613e-07
Outputs:
- loss_sum: float32 [], replicated
- grad_norm: float32 [], replicated
- new_patch: float32 [768, 768], P(('batch', 'head'))
- new_first_patch: float32 [768, 768], P(('batch', 'head'))
- new_second_patch: float32 [768, 768], P(('batch', 'head'))
- new_norms: float32 [8, 768], P(None, ('batch', 'head'))
- new_first_norms: float32 [8, 768], P(None, ('batch', 'head'))
- new_second_norms: float32 [8, 768], P(None, ('batch', 'head'))
- new_head: float32 [768, 400], P(('batch', 'head'))
- new_first_head: float32 [768, 400], P(('batch', 'head'))
- new_second_head: float32 [768, 400], P(('batch', 'head'))
- new_proj: float32 [768, 256], P(('batch', 'head'))
- new_first_proj: float32 [768, 256], P(('batch', 'head'))
- new_second_proj: float32 [768, 256], P(('batch', 'head'))
- new_qkv: float32 [2, 768, 3, 768], P(None, 'batch', None, 'head')
- new_first_qkv: float32 [2, 768, 3, 768], P(None, 'batch', None, 'head')
- new_second_qkv: float32 [2, 768, 3, 768], P(None, 'batch', None, 'head')
- new_out: float32 [2, 768, 768], P(None, 'head', 'batch')
- new_first_out: float32 [2, 768, 768], P(None, 'head', 'batch')
- new_second_out: float32 [2, 768, 768], P(None, 'head', 'batch')
- new_up: float32 [768, 3072], P('batch', 'head')
- new_first_up: float32 [768, 3072], P('batch', 'head')
- new_second_up: float32 [768, 3072], P('batch', 'head')
- new_down: float32 [3072, 768], P('head', 'batch')
- new_first_down: float32 [3072, 768], P('head', 'batch')
- new_second_down: float32 [3072, 768], P('head', 'batch')
The draws below stay inside these ranges and needn't reach their ends.
Inputs may be any that keep to these rules, and one draw needn't show every extreme that they name: partner[partner[c]] = c and partner[c] != c: the clips form 8 // 2 pairs.
All inputs are finite; a program needn't handle non-finite values.
Results may differ from the reference program's by a relative error of at most 0.012.
The reference program's roundings to bfloat16 on the way (of `copies`) count: a program that leaves them out, or rounds other values in their place, can miss the bound.
Values may be sent and summed in bfloat16 or wider, within the bound.
No kernel may reach another device: no remote copies, remote signals or barrier semaphores. Data moves between devices by JAX's collectives and lax.ppermute only.
A program may use at most 192 MiB of HBM per device.

```python
import math
import jax
import jax.numpy as jnp
from jax import lax

D = 768
HEADS = 12
HD = 64
FF = 3072
CLASSES = 400
PROJ = 256
PATCH_IN = 768
FRAMES = 4
PMAX = 784
PSMALL = 196
STEP = 5
ROWS = 3136
CLIPS = 8
PARAMS = 10536960


def draw_patches(key, part):
    key = jax.random.fold_in(key, 11)
    noise_key, clip_key = jax.random.split(key)
    noise = jax.random.normal(noise_key, (CLIPS, ROWS, PATCH_IN), jnp.float32)
    common = jax.random.normal(clip_key, (CLIPS, 1, PATCH_IN), jnp.float32)
    return jnp.clip(noise + common, -8.0, 8.0).astype(jnp.bfloat16)


def draw_partner(key, part):
    key = jax.random.fold_in(key, 23)
    order = jax.random.permutation(key, CLIPS).astype(jnp.int32)
    place = jnp.argsort(order, stable=True).astype(jnp.int32)
    return order[place ^ 1].astype(jnp.int32)


def draw_norm_params(key, part):
    key = jax.random.fold_in(key, 37)
    gain_key, bias_key = jax.random.split(key)
    ramp = jnp.arange(D, dtype=jnp.float32) / D
    base = 0.5 + ramp
    gains = base[None, :] * jax.random.uniform(gain_key, (4, D), jnp.float32, 0.8, 1.25)
    biases = jnp.clip(0.3 * jax.random.normal(bias_key, (4, D), jnp.float32), -2.0, 2.0)
    return jnp.stack([gains, biases], axis=1).reshape(8, D)


def with_ends(drawn, rng, least, largest):
    longest = drawn.shape.index(max(drawn.shape))
    spots = []
    for shift in (0, 1):
        where = [jax.random.randint(jax.random.fold_in(rng, axis), (), 0, length) for axis, length in enumerate(drawn.shape)]
        where[longest] = (where[longest] + shift) % drawn.shape[longest]
        spots.append(tuple(where))
    return drawn.at[spots[0]].set(least).at[spots[1]].set(largest)


def steps_of(stream_key, dims, cuts, least, top_value):
    level = 1.0
    for position, parts in cuts:
        heights = jax.random.uniform(jax.random.fold_in(jax.random.fold_in(stream_key, 6), position), (parts,), jnp.float32, least / len(cuts), top_value / len(cuts))
        level = level * jnp.repeat(jnp.exp(heights), dims[position] // parts).reshape((-1,) + (1,) * (len(dims) - 1 - position))
    return level


def centred(stream_key, dims, deviation, reach, pieces=(), held_as=jnp.bfloat16):
    result = jax.random.normal(stream_key, dims, jnp.float32) * deviation
    if len(pieces) > 0:
        result = steps_of(stream_key, dims, pieces, -0.22, 0.18) * result
    return jnp.clip(result, min=-reach, max=reach).astype(held_as)


def setup_inputs(seed: int = 0) -> dict:
    splits = jax.random.split(jax.random.key(seed), 29)
    patches = draw_patches(jax.random.fold_in(splits[28], 71), 0)
    bucket = with_ends(jax.random.randint(splits[1], (CLIPS,), 0, 2), jax.random.fold_in(splits[1], 1), 0, 1).astype(jnp.int32)
    labels = with_ends(jax.random.randint(splits[2], (CLIPS,), 0, CLASSES), jax.random.fold_in(splits[2], 1), 0, CLASSES - 1).astype(jnp.int32)
    partner = draw_partner(jax.random.fold_in(splits[28], 71), 0)
    patch_weight = centred(splits[4], (PATCH_IN, D), PATCH_IN ** -0.5, 0.21875, ((0, 32),), jnp.float32)
    norm_params = draw_norm_params(jax.random.fold_in(splits[28], 71), 0)
    head_weight = centred(splits[6], (D, CLASSES), (D // 4) ** -0.5, 0.4375, ((0, 32),), jnp.float32)
    proj_weight = centred(splits[7], (D, PROJ), D ** -0.5, 0.21875, ((0, 32),), jnp.float32)
    attn_in = centred(splits[8], (2, D, 3, D), D ** -0.5, 0.21875, ((1, 8), (3, 4)), jnp.float32)
    attn_out = centred(splits[9], (2, D, D), (D // 16) ** -0.5, 0.875, ((1, 4), (2, 8)), jnp.float32)
    mlp_up = centred(splits[10], (D, FF), D ** -0.5, 0.21875, ((0, 8), (1, 4)), jnp.float32)
    mlp_down = centred(splits[11], (FF, D), FF ** -0.5, 0.109375, ((0, 4), (1, 8)), jnp.float32)
    first_patch = centred(splits[12], (PATCH_IN, D), (1.0 / PARAMS ** 0.5), 0.001953125, ((0, 32),), jnp.float32)
    first_norms = centred(splits[13], (8, D), (5.0 / PARAMS ** 0.5), 0.009765625, ((1, 32),), jnp.float32)
    first_head = centred(splits[14], (D, CLASSES), (1.0 / PARAMS ** 0.5), 0.001953125, ((0, 32),), jnp.float32)
    first_proj = centred(splits[15], (D, PROJ), (1.0 / PARAMS ** 0.5), 0.001953125, ((0, 32),), jnp.float32)
    first_qkv = centred(splits[16], (2, D, 3, D), (1.0 / PARAMS ** 0.5), 0.001953125, ((1, 8), (3, 4)), jnp.float32)
    first_out = centred(splits[17], (2, D, D), (1.0 / PARAMS ** 0.5), 0.001953125, ((1, 4), (2, 8)), jnp.float32)
    first_up = centred(splits[18], (D, FF), (0.2 / PARAMS ** 0.5), 0.00036621094, ((0, 8), (1, 4)), jnp.float32)
    first_down = centred(splits[19], (FF, D), (1.0 / PARAMS ** 0.5), 0.001953125, ((0, 4), (1, 8)), jnp.float32)
    second_patch = jnp.clip(jnp.exp(math.log(3.796161252012098e-07) - 1.3862944 * jax.random.uniform(splits[20], (PATCH_IN, D), jnp.float32) ** steps_of(splits[20], (PATCH_IN, D), ((0, 32),), -0.2, 0.2)), 9.490403130030245e-08, 3.796161252012098e-07)
    second_norms = jnp.clip(jnp.exp(math.log(9.490403499512468e-06) - 1.3862944 * jax.random.uniform(splits[21], (8, D), jnp.float32) ** steps_of(splits[21], (8, D), ((1, 32),), -0.2, 0.2)), 2.372600874878117e-06, 9.490403499512468e-06)
    second_head = jnp.clip(jnp.exp(math.log(3.796161252012098e-07) - 1.3862944 * jax.random.uniform(splits[22], (D, CLASSES), jnp.float32) ** steps_of(splits[22], (D, CLASSES), ((0, 32),), -0.2, 0.2)), 9.490403130030245e-08, 3.796161252012098e-07)
    second_proj = jnp.clip(jnp.exp(math.log(3.796161252012098e-07) - 1.3862944 * jax.random.uniform(splits[23], (D, PROJ), jnp.float32) ** steps_of(splits[23], (D, PROJ), ((0, 32),), -0.2, 0.2)), 9.490403130030245e-08, 3.796161252012098e-07)
    second_qkv = jnp.clip(jnp.exp(math.log(3.796161252012098e-07) - 1.3862944 * jax.random.uniform(splits[24], (2, D, 3, D), jnp.float32) ** steps_of(splits[24], (2, D, 3, D), ((1, 8), (3, 4)), -0.2, 0.2)), 9.490403130030245e-08, 3.796161252012098e-07)
    second_out = jnp.clip(jnp.exp(math.log(3.796161252012098e-07) - 1.3862944 * jax.random.uniform(splits[25], (2, D, D), jnp.float32) ** steps_of(splits[25], (2, D, D), ((1, 4), (2, 8)), -0.2, 0.2)), 9.490403130030245e-08, 3.796161252012098e-07)
    second_up = jnp.clip(jnp.exp(math.log(1.898080626006049e-08) - 1.3862944 * jax.random.uniform(splits[26], (D, FF), jnp.float32) ** steps_of(splits[26], (D, FF), ((0, 8), (1, 4)), -0.2, 0.2)), 4.7452015650151225e-09, 1.898080626006049e-08)
    second_down = jnp.clip(jnp.exp(math.log(3.796161252012098e-07) - 1.3862944 * jax.random.uniform(splits[27], (FF, D), jnp.float32) ** steps_of(splits[27], (FF, D), ((0, 4), (1, 8)), -0.2, 0.2)), 9.490403130030245e-08, 3.796161252012098e-07)
    return {"patches": patches, "bucket": bucket, "labels": labels, "partner": partner, "patch_weight": patch_weight, "norm_params": norm_params, "head_weight": head_weight, "proj_weight": proj_weight, "attn_in": attn_in, "attn_out": attn_out, "mlp_up": mlp_up, "mlp_down": mlp_down, "first_patch": first_patch, "first_norms": first_norms, "first_head": first_head, "first_proj": first_proj, "first_qkv": first_qkv, "first_out": first_out, "first_up": first_up, "first_down": first_down, "second_patch": second_patch, "second_norms": second_norms, "second_head": second_head, "second_proj": second_proj, "second_qkv": second_qkv, "second_out": second_out, "second_up": second_up, "second_down": second_down}


EXACT = lax.Precision.HIGHEST
TEMPER = 0.05
BETA_ONE = 0.5
BETA_TWO = 0.5
RATE = 0.04
NORM_RATE = 0.3
DECAY = 0.05
ADAM_EPS = 1e-08
CLIP_AT = 1.0

@jax.custom_vjp
def low(v):
    return lax.optimization_barrier(v.astype(jnp.bfloat16)).astype(jnp.float32)

@jax.custom_vjp
def low_back(v):
    return v

def low_keep(v):
    return (low(v), None)

def low_pass(kept, grad):
    return (grad,)

def back_keep(v):
    return (v, None)

def back_low(kept, grad):
    return (low(grad),)
low.defvjp(low_keep, low_pass)
low_back.defvjp(back_keep, back_low)

def product(left, right):
    return jnp.dot(left, right, precision=EXACT)

def round_both(value):
    return low(low_back(value))

def layer_norm(value, gain, bias):
    center = value - lax.optimization_barrier(jnp.mean(value, axis=-1, keepdims=True))
    spread = lax.optimization_barrier(jnp.mean(center * center, axis=-1, keepdims=True))
    return center * lax.rsqrt(spread + 1e-06) * gain + bias

def attend(query, keys, values, key_mask):
    score = jnp.einsum('blhe,bmhe->bhlm', query, keys, precision=EXACT) * HD ** (-0.5)
    score = low_back(jnp.where(key_mask[:, None, None, :], score, -1e+30))
    attn_prob = low(jax.nn.softmax(score, axis=-1))
    return jnp.einsum('bhlm,bmhe->blhe', attn_prob, values, precision=EXACT)

def attention(resid, gain, bias, w_in, w_out, key_mask, spatial):
    normed = low(layer_norm(resid, gain, bias))
    qkv_rows = round_both(jnp.einsum('rd,dkf->rkf', normed, w_in, precision=EXACT))
    query, keys, values = (qkv_rows[:, which].reshape(FRAMES, PMAX, HEADS, HD) for which in range(3))
    if spatial:
        mixed = attend(query, keys, values, jnp.broadcast_to(key_mask[None, :], (FRAMES, PMAX)))
    else:
        mixed = attend(query.transpose(1, 0, 2, 3), keys.transpose(1, 0, 2, 3), values.transpose(1, 0, 2, 3), jnp.ones((PMAX, FRAMES), bool)).transpose(1, 0, 2, 3)
    mixed = round_both(mixed.reshape(ROWS, D))
    return resid + low_back(product(mixed, w_out))

def feed_forward(resid, gain, bias, w_up, w_down):
    normed = low(layer_norm(resid, gain, bias))
    hidden = low_back(product(normed, w_up))
    activated = low(jax.nn.gelu(hidden))
    return resid + low_back(product(activated, w_down))

def clip_pool(copies, clip_rows, kind):
    patch_w, norms, attn_w, out_w, up_w, down_w = copies
    patch_count = jnp.where(kind == 1, PMAX, PSMALL)
    key_mask = jnp.arange(PMAX) < patch_count
    row_mask = jnp.tile(key_mask, FRAMES).astype(jnp.float32)[:, None]
    resid = low_back(product(clip_rows, patch_w)) * row_mask
    resid = attention(resid, norms[0], norms[1], attn_w[0], out_w[0], key_mask, False)
    resid = attention(resid, norms[2], norms[3], attn_w[1], out_w[1], key_mask, True)
    resid = feed_forward(resid, norms[4], norms[5], up_w, down_w)
    final_norm = layer_norm(resid, norms[6], norms[7])
    return lax.optimization_barrier(jnp.sum(final_norm * row_mask, axis=0)) / (FRAMES * patch_count).astype(jnp.float32)

def adam_step(master, first, second, grad, factor, rate):
    clipped = grad * factor
    first_new = BETA_ONE * first + (1.0 - BETA_ONE) * clipped
    second_new = BETA_TWO * second + (1.0 - BETA_TWO) * clipped * clipped
    first_hat = first_new / (1.0 - BETA_ONE ** STEP)
    second_hat = second_new / (1.0 - BETA_TWO ** STEP)
    master_new = master - rate * (first_hat / (jnp.sqrt(second_hat) + ADAM_EPS) + DECAY * master)
    return (master_new, first_new, second_new)

def reference(patches, bucket, labels, partner, patch_weight, norm_params, head_weight, proj_weight, attn_in, attn_out, mlp_up, mlp_down, first_patch, first_norms, first_head, first_proj, first_qkv, first_out, first_up, first_down, second_patch, second_norms, second_head, second_proj, second_qkv, second_out, second_up, second_down):
    masters = (patch_weight, norm_params, head_weight, proj_weight, attn_in, attn_out, mlp_up, mlp_down)
    firsts = (first_patch, first_norms, first_head, first_proj, first_qkv, first_out, first_up, first_down)
    seconds = (second_patch, second_norms, second_head, second_proj, second_qkv, second_out, second_up, second_down)
    video = patches.astype(jnp.float32)

    def total_loss(weights):
        patch_w, norms, head_w, proj_w, attn_w, out_w, up_w, down_w = tuple((low(weight) for weight in weights))
        copies = (patch_w, norms, attn_w, out_w, up_w, down_w)
        pooled = lax.map(jax.checkpoint(lambda block_item: clip_pool(copies, block_item[0], block_item[1])), (video, bucket))
        pooled_low = low(pooled)
        logits = low_back(product(pooled_low, head_w))
        cross_loss = jax.nn.logsumexp(logits, axis=1) - jnp.take_along_axis(logits, labels[:, None], axis=1)[:, 0]
        embedding = low_back(product(pooled_low, proj_w))
        unit_embed = embedding * lax.rsqrt(lax.optimization_barrier(jnp.sum(embedding * embedding, axis=1, keepdims=True)) + 1e-06)
        similar = product(unit_embed, unit_embed.T) / TEMPER
        clip_ids = jnp.arange(CLIPS)
        masked = jnp.where(clip_ids[:, None] == clip_ids[None, :], -1e+30, similar)
        positive = jnp.take_along_axis(similar, partner[:, None], axis=1)[:, 0]
        return jnp.sum(cross_loss) + jnp.sum(jax.nn.logsumexp(masked, axis=1) - positive)
    loss_sum, pull_back = jax.vjp(total_loss, masters)
    grad_list = pull_back(jnp.ones_like(loss_sum))[0]
    grad_norm = jnp.sqrt(sum((jnp.sum(grad * grad) for grad in grad_list)))
    factor = jnp.minimum(1.0, CLIP_AT / (grad_norm + 1e-06))
    updates = []
    for number, (master, first, second, grad) in enumerate(zip(masters, firsts, seconds, grad_list)):
        rate = NORM_RATE if number == 1 else RATE
        updates.extend(adam_step(master, first, second, grad, factor, rate))
    return (loss_sum, grad_norm, *updates)
```

```python
import functools

import jax
import jax.numpy as jnp
from jax import lax
from jax.experimental import pallas as pl
from jax.experimental.pallas import tpu as pltpu
from jax.sharding import PartitionSpec as P

HD = 64
FRAMES = 4
PMAX = 784
PSMALL = 196
STEP = 5
SLOTS = 208
ROWS = FRAMES * SLOTS
GROUP = 192
QKV = 3 * GROUP


EXACT = lax.Precision.HIGHEST
TEMPER = 0.05
BETA_ONE = 0.5
BETA_TWO = 0.5
RATE = 0.04
NORM_RATE = 0.3
DECAY = 0.05
ADAM_EPS = 1e-08
CLIP_AT = 1.0
LOWER = jnp.bfloat16
SINGLE = jnp.float32
ALL = ("batch", "head")
GRANT = 56 << 20

NN = (((1,), (0,)), ((), ()))
NT = (((1,), (1,)), ((), ()))
TN = (((0,), (0,)), ((), ()))


def dot(left, right, dims=NN):
    return lax.dot_general(left, right, dims, preferred_element_type=SINGLE)


def low(value):
    return value.astype(LOWER)


def layer_norm(value, gain, bias):
    center = value - jnp.mean(value, axis=-1, keepdims=True)
    spread = jnp.mean(center * center, axis=-1, keepdims=True)
    return center * lax.rsqrt(spread + 1e-06) * gain + bias


def three_parts(value):
    high = low(value)
    rest = value - high.astype(SINGLE)
    middle = low(rest)
    return high, middle, low(rest - middle.astype(SINGLE))


def frame_scores(left, right, heads):
    product = left.astype(SINGLE) * right.astype(SINGLE)
    high = low(product)
    rest = low(product - high.astype(SINGLE))
    return dot(high, heads) + dot(rest, heads)


def frame_probs(query, keys, heads):
    scores = [frame_scores(query, key, heads) * HD ** (-0.5) for key in keys]
    top = functools.reduce(jnp.maximum, scores)
    raised = [jnp.exp(score - top) for score in scores]
    total = functools.reduce(jnp.add, raised)
    return [value / total for value in raised]


def split_frames(rows):
    return [rows[SLOTS * f : SLOTS * (f + 1)] for f in range(FRAMES)]


def temporal_fwd_kernel(normed_ref, weight_ref, heads_ref, qkv_ref, mixed_ref):
    qkv_ref[0] = low(dot(normed_ref[...], weight_ref[0, :, :QKV]))
    heads = heads_ref[...]
    query, keys, values = (
        split_frames(qkv_ref[0, :, GROUP * i : GROUP * (i + 1)]) for i in range(3)
    )
    for f in range(FRAMES):
        probs = frame_probs(query[f], keys, heads)
        mixed = sum(
            dot(low(prob), heads, NT) * value.astype(SINGLE) for prob, value in zip(probs, values)
        )
        mixed_ref[0, SLOTS * f : SLOTS * (f + 1), :] = low(mixed)


def temporal_bwd_kernel(
    normed_ref, grad_ref, weight_ref, qkv_ref, mixed_ref, heads_ref, dweight_ref, dnormed_ref, dqkv
):
    heads = heads_ref[...]
    d_mixed = split_frames(low(dot(grad_ref[...], weight_ref[0, :, QKV:])))
    query, keys, values = (
        split_frames(qkv_ref[0, :, GROUP * i : GROUP * (i + 1)]) for i in range(3)
    )
    d_keys = [jnp.zeros((SLOTS, GROUP), SINGLE) for _ in range(FRAMES)]
    d_values = [jnp.zeros((SLOTS, GROUP), SINGLE) for _ in range(FRAMES)]
    scale = HD ** (-0.5)
    for f in range(FRAMES):
        probs = frame_probs(query[f], keys, heads)
        d_probs = [frame_scores(d_mixed[f], value, heads) for value in values]
        row = sum(prob * d_prob for prob, d_prob in zip(probs, d_probs))
        d_query = jnp.zeros((SLOTS, GROUP), SINGLE)
        for g in range(FRAMES):
            d_score = dot(low(probs[g] * (d_probs[g] - row)), heads, NT)
            d_query = d_query + d_score * keys[g].astype(SINGLE)
            d_keys[g] = d_keys[g] + d_score * query[f].astype(SINGLE)
            d_values[g] = d_values[g] + dot(low(probs[g]), heads, NT) * d_mixed[f].astype(SINGLE)
        dqkv[SLOTS * f : SLOTS * (f + 1), :GROUP] = low(d_query * scale)
    for g in range(FRAMES):
        dqkv[SLOTS * g : SLOTS * (g + 1), GROUP : 2 * GROUP] = low(d_keys[g] * scale)
        dqkv[SLOTS * g : SLOTS * (g + 1), 2 * GROUP :] = low(d_values[g])
    finish_backward(normed_ref, grad_ref, weight_ref, mixed_ref, dweight_ref, dnormed_ref, dqkv)


def finish_backward(
    normed_ref, grad_ref, weight_ref, mixed_ref, dweight_ref, dnormed_ref, dqkv
):
    dweight_ref[0, :, :QKV] = low(dot(normed_ref[...], dqkv[...], TN))
    dweight_ref[0, :, QKV:] = low(dot(grad_ref[...], mixed_ref[0], TN))
    d_normed = dot(dqkv[...], weight_ref[0, :, :QKV], NT)

    @pl.when(pl.program_id(0) == 0)
    def _():
        dnormed_ref[...] = d_normed

    @pl.when(pl.program_id(0) != 0)
    def _():
        dnormed_ref[...] += d_normed


def lane_pieces(pieces, rows):
    lane = lax.broadcasted_iota(jnp.int32, (rows, HD), 1)
    result = jnp.zeros((rows, HD), SINGLE)
    for number, piece in enumerate(pieces):
        result = jnp.where(lane == number, piece.astype(SINGLE), result)
    return low(result)


def spatial_fwd_kernel(
    normed_ref, weight_ref, key_extra_ref, qkv_ref, mixed_ref, extra_ref, branch_ref
):
    qkv_ref[0] = low(dot(normed_ref[...], weight_ref[0, :, :QKV]))
    one = jnp.ones((ROWS, 1), SINGLE)
    for head in range(GROUP // HD):
        at = HD * head
        query = qkv_ref[0, :, at : at + HD] * jnp.asarray(HD ** (-0.5), LOWER)
        query = jnp.concatenate([query, lane_pieces([one], ROWS)], axis=1)
        keys = jnp.concatenate(
            [qkv_ref[0, :, GROUP + at : GROUP + at + HD], key_extra_ref[...]], axis=1
        )
        values = jnp.concatenate(
            [qkv_ref[0, :, 2 * GROUP + at : 2 * GROUP + at + HD], lane_pieces([one], ROWS)], axis=1
        )
        for part in range(FRAMES):
            rows = slice(SLOTS * part, SLOTS * (part + 1))
            score = dot(query[rows], keys, NT)
            top = jnp.max(score, axis=1, keepdims=True)
            mixed = dot(low(jnp.exp(score - top)), values)
            total = mixed[:, HD : HD + 1]
            mixed_ref[0, rows, at : at + HD] = low(mixed[:, :HD] / total)
            logsum = -(top + jnp.log(total))
            extra_ref[0, rows, at : at + HD] = lane_pieces(
                [one[rows], *three_parts(logsum)], SLOTS
            )
    branch = dot(mixed_ref[0], weight_ref[0, :, QKV:], NT)

    @pl.when(pl.program_id(0) == 0)
    def _():
        branch_ref[...] = branch

    @pl.when(pl.program_id(0) != 0)
    def _():
        branch_ref[...] += branch


def spatial_bwd_kernel(
    normed_ref,
    grad_ref,
    weight_ref,
    qkv_ref,
    mixed_ref,
    extra_ref,
    key_extra_ref,
    dweight_ref,
    dnormed_ref,
    dqkv,
):
    scale = HD ** (-0.5)
    d_mixed_all = low(dot(grad_ref[...], weight_ref[0, :, QKV:]))
    one = jnp.ones((ROWS, 1), SINGLE)
    for head in range(GROUP // HD):
        at = HD * head
        query = qkv_ref[0, :, at : at + HD]
        query_long = jnp.concatenate(
            [query * jnp.asarray(scale, LOWER), extra_ref[0, :, at : at + HD]], axis=1
        )
        d_mixed = d_mixed_all[:, at : at + HD]
        delta = -jnp.sum(
            d_mixed.astype(SINGLE) * mixed_ref[0, :, at : at + HD].astype(SINGLE),
            axis=1,
            keepdims=True,
        )
        d_mixed_long = jnp.concatenate([d_mixed, lane_pieces(three_parts(delta), ROWS)], axis=1)
        d_query = jnp.zeros((ROWS, HD), SINGLE)
        for part in range(FRAMES):
            rows = slice(SLOTS * part, SLOTS * (part + 1))
            keys = qkv_ref[0, rows, GROUP + at : GROUP + at + HD]
            values = qkv_ref[0, rows, 2 * GROUP + at : 2 * GROUP + at + HD]
            keys_long = jnp.concatenate([keys, key_extra_ref[rows, :]], axis=1)
            values_long = jnp.concatenate(
                [values, lane_pieces([one[rows]] * 3, SLOTS)], axis=1
            )
            prob = jnp.exp(dot(keys_long, query_long, NT))
            d_score = low(prob * dot(values_long, d_mixed_long, NT))
            dqkv[rows, 2 * GROUP + at : 2 * GROUP + at + HD] = low(dot(low(prob), d_mixed))
            dqkv[rows, GROUP + at : GROUP + at + HD] = low(dot(d_score, query) * scale)
            d_query = d_query + dot(d_score, keys, TN)
        dqkv[:, at : at + HD] = low(d_query * scale)
    finish_backward(normed_ref, grad_ref, weight_ref, mixed_ref, dweight_ref, dnormed_ref, dqkv)


def whole(shape):
    return pl.BlockSpec(shape, lambda g: (0,) * len(shape))


def per_group(rows, width):
    return pl.BlockSpec((1, rows, width), lambda g: (g, 0, 0))


def call(kernel, inputs, in_specs, outputs, out_specs, scratch, flops, name):
    return pl.pallas_call(
        kernel,
        grid=(2,),
        in_specs=in_specs,
        out_specs=out_specs,
        out_shape=outputs,
        scratch_shapes=scratch,
        compiler_params=pltpu.CompilerParams(vmem_limit_bytes=GRANT),
        cost_estimate=pl.CostEstimate(flops=flops, bytes_accessed=16 << 20, transcendentals=0),
        name=name,
    )(*inputs)


def grouped(width, dtype=LOWER, rows=ROWS):
    return jax.ShapeDtypeStruct((2, rows, width), dtype)


def temporal_forward(normed, weight, heads):
    dim = normed.shape[1]
    return call(
        temporal_fwd_kernel,
        (normed, weight, heads),
        [whole(normed.shape), per_group(dim, dim), whole(heads.shape)],
        [grouped(QKV), grouped(GROUP)],
        [per_group(ROWS, QKV), per_group(ROWS, GROUP)],
        [],
        5 * 10**9,
        "temporal_forward",
    )


def temporal_backward(normed, grad, weight, qkv, mixed, heads):
    dim = normed.shape[1]
    return call(
        temporal_bwd_kernel,
        (normed, grad, weight, qkv, mixed, heads),
        [
            whole(normed.shape),
            whole(grad.shape),
            per_group(dim, dim),
            per_group(ROWS, QKV),
            per_group(ROWS, GROUP),
            whole(heads.shape),
        ],
        [grouped(dim, LOWER, dim), jax.ShapeDtypeStruct((ROWS, dim), SINGLE)],
        [per_group(dim, dim), whole((ROWS, dim))],
        [pltpu.VMEM((ROWS, QKV), LOWER)],
        12 * 10**9,
        "temporal_backward",
    )


def spatial_forward(normed, weight, key_extra):
    dim = normed.shape[1]
    return call(
        spatial_fwd_kernel,
        (normed, weight, key_extra),
        [whole(normed.shape), per_group(dim, dim), whole(key_extra.shape)],
        [
            grouped(QKV),
            grouped(GROUP),
            grouped(GROUP),
            jax.ShapeDtypeStruct((ROWS, dim), SINGLE),
        ],
        [
            per_group(ROWS, QKV),
            per_group(ROWS, GROUP),
            per_group(ROWS, GROUP),
            whole((ROWS, dim)),
        ],
        [],
        10 * 10**9,
        "spatial_forward",
    )


def spatial_backward(normed, grad, weight, qkv, mixed, extra, key_extra):
    dim = normed.shape[1]
    return call(
        spatial_bwd_kernel,
        (normed, grad, weight, qkv, mixed, extra, key_extra),
        [
            whole(normed.shape),
            whole(grad.shape),
            per_group(dim, dim),
            per_group(ROWS, QKV),
            per_group(ROWS, GROUP),
            per_group(ROWS, GROUP),
            whole(key_extra.shape),
        ],
        [grouped(dim, LOWER, dim), jax.ShapeDtypeStruct((ROWS, dim), SINGLE)],
        [per_group(dim, dim), whole((ROWS, dim))],
        [pltpu.VMEM((ROWS, QKV), LOWER)],
        30 * 10**9,
        "spatial_backward",
    )


class Cube:
    def __init__(self, sizes):
        self.count = sizes["batch"] * sizes["head"]
        self.mine = lax.axis_index(ALL)
        batch_bits = sizes["batch"].bit_length() - 1
        self.head_masks = [2, 1]
        self.batch_masks = [4 << k for k in reversed(range(batch_bits))]

    def swap(self, value, mask):
        return lax.ppermute(value, ALL, [(i, i ^ mask) for i in range(self.count)])

    def has(self, mask):
        return (self.mine & mask) != 0

    def join(self, value, mask):
        other = self.swap(value, mask)
        has = self.has(mask)
        both = jnp.stack([jnp.where(has, other, value), jnp.where(has, value, other)], axis=-3)
        shape = value.shape
        return both.reshape(*shape[:-3], 2 * shape[-3], *shape[-2:])

    def shed(self, value, mask):
        shape = value.shape
        pair = value.reshape(*shape[:-3], shape[-3] // 2, 2, *shape[-2:])
        first, last = pair[..., 0, :, :], pair[..., 1, :, :]
        has = self.has(mask)
        send = low(jnp.where(has, first, last))
        keep = jnp.where(has, last, first).astype(SINGLE)
        return keep + self.swap(send, mask).astype(SINGLE)

    def gather_block(self, shard, late):
        value = shard[None]
        for mask in self.batch_masks[:-1]:
            value = self.join(value, mask)
        if late:
            value = jnp.stack([value, self.swap(value, 2)])
            value = self.join(value, self.batch_masks[-1])
        else:
            value = self.join(value, self.batch_masks[-1])
            value = jnp.stack([value, self.swap(value, 2)])
        value = value.reshape(2, -1, shard.shape[-1])
        return value, self.swap(value, 1)

    def reduce_block(self, own, other, rows, late):
        value = own.astype(SINGLE) + self.swap(other, 1).astype(SINGLE)
        value = value.reshape(2, -1, rows, own.shape[-1])
        masks = self.batch_masks[::-1]
        if late:
            value = self.shed(value, masks[0])
        value = value[0] + self.swap(low(value[1]), 2).astype(SINGLE)
        if not late:
            value = self.shed(value, masks[0])
        for mask in masks[1:]:
            value = self.shed(value, mask)
        return value[0]

    def gather_rows(self, shard):
        value = shard[None]
        for mask in self.batch_masks + self.head_masks:
            value = self.join(value, mask)
        return value.reshape(-1, shard.shape[-1])

    def reduce_rows(self, value, rows):
        value = value.reshape(-1, rows, value.shape[-1])
        for mask in (self.batch_masks + self.head_masks)[::-1]:
            value = self.shed(value, mask)
        return value[0]

    def total(self, value):
        for mask in (self.batch_masks + self.head_masks)[::-1]:
            value = value + self.swap(value, mask)
        return value

    def swap_frames(self, parts):
        return [parts[0]] + [self.swap(parts[r], r) for r in range(1, FRAMES)]


def adam_step(master, first, second, grad, factor, rate):
    clipped = grad * factor
    first_new = BETA_ONE * first + (1.0 - BETA_ONE) * clipped
    second_new = BETA_TWO * second + (1.0 - BETA_TWO) * clipped * clipped
    first_hat = first_new / (1.0 - BETA_ONE**STEP)
    second_hat = second_new / (1.0 - BETA_TWO**STEP)
    master_new = master - rate * (first_hat / (jnp.sqrt(second_hat) + ADAM_EPS) + DECAY * master)
    return (master_new, first_new, second_new)


def gelu_slope(hidden):
    _, back = jax.vjp(jax.nn.gelu, hidden)
    return back(jnp.ones_like(hidden))[0]


def body(sizes, *args):
    patches, bucket, labels, partner = args[:4]
    masters, firsts, seconds = (args[4:12], args[12:20], args[20:28])
    patch_weight, norm_params, head_weight, proj_weight, attn_in, attn_out, up, down = masters
    cube = Cube(sizes)
    clips = sizes["batch"]
    dim = norm_params.shape[1] * cube.count
    classes, proj = head_weight.shape[1], proj_weight.shape[1]
    rows_wide, rows_small = attn_in.shape[1], patch_weight.shape[0]
    place = lax.axis_index("head")

    early = jnp.concatenate(
        [low(patch_weight), low(norm_params).T, jnp.zeros((rows_small, 120), LOWER)], axis=1
    )
    early = cube.gather_rows(early)
    patch_copy, norms = early[:, :dim], early[:, dim : dim + 8].astype(SINGLE).T
    attn_shards = [
        jnp.concatenate(
            [low(attn_in[i]).reshape(rows_wide, QKV), low(attn_out[i]).T], axis=1
        )
        for i in range(2)
    ]
    attn_w = [cube.gather_block(attn_shards[i], i == 1) for i in range(2)]
    up_w = cube.gather_block(low(up), False)
    down_w = cube.gather_block(low(down).T, True)
    small = jnp.concatenate(
        [
            low(head_weight),
            low(proj_weight),
            jnp.zeros((rows_small, -(classes + proj) % 128), LOWER),
        ],
        axis=1,
    )
    small = cube.gather_rows(small)
    head_copy, proj_copy = small[:, :classes], small[:, classes : classes + proj]

    patch_count = jnp.where(bucket == 1, PMAX, PSMALL)
    blocks = jnp.pad(patches[0], ((0, ROWS - PMAX), (0, 0))).reshape(FRAMES, SLOTS, -1)
    blocks = jnp.where((place & 1) != 0, blocks[jnp.array([1, 0, 3, 2])], blocks)
    blocks = jnp.where((place & 2) != 0, blocks[jnp.array([2, 3, 0, 1])], blocks)
    by_frame = blocks.reshape(ROWS, -1)
    by_slot = jnp.concatenate(cube.swap_frames(list(blocks)))
    offset = jnp.arange(SLOTS)[None, :]
    number = (place ^ jnp.arange(FRAMES))[:, None]
    frame_valid = ((number * SLOTS + offset) < patch_count).reshape(ROWS, 1).astype(SINGLE)
    slot_valid = (jnp.broadcast_to(place * SLOTS + offset, (FRAMES, SLOTS)) < patch_count).reshape(
        ROWS, 1
    ).astype(SINGLE)
    heads = (
        jnp.arange(GROUP)[:, None] // HD == jnp.arange(128)[None, :]
    ).astype(LOWER)
    lane = jnp.arange(HD)[None, :]
    key_extra = low(
        jnp.where(lane == 0, jnp.where(frame_valid > 0, 0.0, -1e30), (lane < 4).astype(SINGLE))
    )

    start_slot = dot(by_slot, patch_copy) * slot_valid
    start_frame = dot(by_frame, patch_copy) * frame_valid
    normed_t = low(layer_norm(start_slot, norms[0], norms[1]))
    qkv_t, mixed_t = zip(*(temporal_forward(normed_t, weight, heads) for weight in attn_w[0]))
    order = (0, 2, 1, 3)
    pieces = {m: mixed_t[m % 2][m // 2] for m in range(4)}
    parts = [
        jnp.concatenate(
            [pieces[m ^ r][SLOTS * r : SLOTS * (r + 1)] for m in order], axis=1
        )
        for r in range(FRAMES)
    ]
    mixed_frame = jnp.concatenate(cube.swap_frames(parts))
    out_first = jnp.concatenate(
        [attn_w[0][m % 2][m // 2][:, QKV:] for m in order], axis=1
    )
    resid_one = start_frame + dot(mixed_frame, out_first, NT)
    normed_s = low(layer_norm(resid_one, norms[2], norms[3]))
    qkv_s, mixed_s, extra_s, branch_s = zip(
        *(spatial_forward(normed_s, weight, key_extra) for weight in attn_w[1])
    )
    resid_two = resid_one + (branch_s[0] + branch_s[1])
    normed_m = low(layer_norm(resid_two, norms[4], norms[5]))
    hidden = [[dot(normed_m, up_w[c][y]) for y in range(2)] for c in range(2)]
    activated = [[low(jax.nn.gelu(hidden[c][y])) for y in range(2)] for c in range(2)]
    slope = [[low(gelu_slope(hidden[c][y])) for y in range(2)] for c in range(2)]
    resid_three = resid_two + sum(
        dot(activated[c][y], down_w[c][y], NT) for c in range(2) for y in range(2)
    )
    final_norm, final_back = jax.vjp(layer_norm, resid_three, norms[6], norms[7])
    sums = jnp.sum(final_norm * frame_valid, axis=0, keepdims=True)

    for mask in cube.head_masks[::-1]:
        sums = sums + cube.swap(sums, mask)
    facts = jnp.stack([labels[0], partner[0], FRAMES * patch_count[0]]).astype(SINGLE)
    gathered = jnp.concatenate([sums, jnp.pad(facts, (0, 125))[None]], axis=1)[None]
    for mask in cube.batch_masks:
        gathered = cube.join(gathered, mask)
    gathered = gathered[:, 0]
    all_labels, all_partners = (gathered[:, dim + i].astype(jnp.int32) for i in range(2))
    pooled_low = low(gathered[:, :dim] / gathered[:, dim + 2 : dim + 3])
    logits = dot(pooled_low, head_copy)
    label_hot = (jnp.arange(classes)[None, :] == all_labels[:, None]).astype(SINGLE)
    cross = jax.nn.logsumexp(logits, axis=1) - jnp.sum(logits * label_hot, axis=1)
    d_logits = low(jax.nn.softmax(logits, axis=1) - label_hot)
    embedding = dot(pooled_low, proj_copy)
    inverse = lax.rsqrt(jnp.sum(embedding * embedding, axis=1, keepdims=True) + 1e-06)
    unit = embedding * inverse
    ids = jnp.arange(clips)
    mate_hot = (ids[None, :] == all_partners[:, None]).astype(SINGLE)
    similar = jnp.dot(unit, unit.T, precision=EXACT) / TEMPER
    masked = jnp.where(ids[None, :] == ids[:, None], -1e30, similar)
    contrast = jax.nn.logsumexp(masked, axis=1) - jnp.sum(similar * mate_hot, axis=1)
    loss_sum = jnp.sum(cross + contrast)
    d_similar = (jax.nn.softmax(masked, axis=1) - mate_hot) / TEMPER
    d_unit = jnp.dot(d_similar + d_similar.T, unit, precision=EXACT)
    d_embed = low(
        inverse * d_unit
        - embedding
        * (inverse * inverse * inverse)
        * jnp.sum(embedding * d_unit, axis=1, keepdims=True)
    )
    d_head = lax.dynamic_slice_in_dim(
        dot(pooled_low, d_logits, TN), cube.mine * rows_small, rows_small, 0
    )
    d_proj = lax.dynamic_slice_in_dim(
        dot(pooled_low, d_embed, TN), cube.mine * rows_small, rows_small, 0
    )
    d_pooled = dot(d_logits, head_copy, NT) + dot(d_embed, proj_copy, NT)
    d_pooled = lax.dynamic_slice_in_dim(d_pooled, lax.axis_index("batch"), 1, 0)
    row_count = (FRAMES * patch_count[0]).astype(SINGLE)

    d_resid, d_gain_f, d_bias_f = final_back(frame_valid * (d_pooled / row_count))
    d_rows = low(d_resid)
    d_hidden = [
        [low(dot(d_rows, down_w[c][y]) * slope[c][y].astype(SINGLE)) for y in range(2)]
        for c in range(2)
    ]
    d_down = [
        jnp.stack([low(dot(d_rows, activated[c][y], TN)) for y in range(2)]) for c in range(2)
    ]
    d_down = cube.reduce_block(d_down[0], d_down[1], rows_wide, True)
    d_up = [
        jnp.stack([low(dot(normed_m, d_hidden[c][y], TN)) for y in range(2)]) for c in range(2)
    ]
    d_up = cube.reduce_block(d_up[0], d_up[1], rows_wide, False)
    d_normed = sum(dot(d_hidden[c][y], up_w[c][y], NT) for c in range(2) for y in range(2))
    _, back = jax.vjp(layer_norm, resid_two, norms[4], norms[5])
    d_local, d_gain_m, d_bias_m = back(d_normed)
    d_resid = d_resid + d_local
    d_rows = low(d_resid)
    d_second, d_normed = [None, None], []
    for c in (1, 0):
        d_second[c], part = spatial_backward(
            normed_s, d_rows, attn_w[1][c], qkv_s[c], mixed_s[c], extra_s[c], key_extra
        )
        d_normed.append(part)
    d_second = cube.reduce_block(d_second[0], d_second[1], rows_wide, True)
    _, back = jax.vjp(layer_norm, resid_one, norms[2], norms[3])
    d_local, d_gain_s, d_bias_s = back(d_normed[0] + d_normed[1])
    d_resid = d_resid + d_local
    d_rows = jnp.concatenate(cube.swap_frames(split_frames(low(d_resid))))
    d_first, d_normed = [None, None], []
    for c in (1, 0):
        d_first[c], part = temporal_backward(
            normed_t, d_rows, attn_w[0][c], qkv_t[c], mixed_t[c], heads
        )
        d_normed.append(part)
    d_first = cube.reduce_block(d_first[0], d_first[1], rows_wide, False)
    _, back = jax.vjp(layer_norm, start_slot, norms[0], norms[1])
    d_local, d_gain_t, d_bias_t = back(d_normed[0] + d_normed[1])
    d_start = low((d_rows.astype(SINGLE) + d_local) * slot_valid)
    d_patch = cube.reduce_rows(low(dot(by_slot, d_start, TN)), rows_small)
    d_norms = cube.total(
        jnp.stack(
            [d_gain_t, d_bias_t, d_gain_s, d_bias_s, d_gain_m, d_bias_m, d_gain_f, d_bias_f]
        )
    )
    d_norms = lax.dynamic_slice_in_dim(
        d_norms.reshape(8, cube.count, rows_small), cube.mine, 1, 1
    )[:, 0]
    d_in = jnp.stack([d_first[:, :QKV], d_second[:, :QKV]]).reshape(attn_in.shape)
    d_out = jnp.stack([d_first[:, QKV:].T, d_second[:, QKV:].T])
    grads = (d_patch, d_norms, d_head, d_proj, d_in, d_out, d_up, d_down.T)

    squares = sum(jnp.sum(grad * grad) for grad in grads)
    grad_norm = jnp.sqrt(cube.total(squares.reshape(1, 1)))[0, 0]
    factor = jnp.minimum(1.0, CLIP_AT / (grad_norm + 1e-06))
    updates = []
    for index, (master, first, second, grad) in enumerate(zip(masters, firsts, seconds, grads)):
        rate = NORM_RATE if index == 1 else RATE
        updates.extend(adam_step(master, first, second, grad, factor, rate))
    return (loss_sum, grad_norm, *updates)


def solution(mesh):
    placed = (
        P("batch", "head", None),
        P("batch"),
        P("batch"),
        P("batch"),
        P(("batch", "head"), None),
        P(None, ("batch", "head")),
        P(("batch", "head"), None),
        P(("batch", "head"), None),
        P(None, "batch", None, "head"),
        P(None, "head", "batch"),
        P("batch", "head"),
        P("head", "batch"),
        P(("batch", "head"), None),
        P(None, ("batch", "head")),
        P(("batch", "head"), None),
        P(("batch", "head"), None),
        P(None, "batch", None, "head"),
        P(None, "head", "batch"),
        P("batch", "head"),
        P("head", "batch"),
        P(("batch", "head"), None),
        P(None, ("batch", "head")),
        P(("batch", "head"), None),
        P(("batch", "head"), None),
        P(None, "batch", None, "head"),
        P(None, "head", "batch"),
        P("batch", "head"),
        P("head", "batch"),
    )
    return jax.shard_map(
        functools.partial(body, dict(mesh.shape)),
        mesh=mesh,
        in_specs=placed,
        out_specs=(
            P(),
            P(),
            P(("batch", "head"), None),
            P(("batch", "head"), None),
            P(("batch", "head"), None),
            P(None, ("batch", "head")),
            P(None, ("batch", "head")),
            P(None, ("batch", "head")),
            P(("batch", "head"), None),
            P(("batch", "head"), None),
            P(("batch", "head"), None),
            P(("batch", "head"), None),
            P(("batch", "head"), None),
            P(("batch", "head"), None),
            P(None, "batch", None, "head"),
            P(None, "batch", None, "head"),
            P(None, "batch", None, "head"),
            P(None, "head", "batch"),
            P(None, "head", "batch"),
            P(None, "head", "batch"),
            P("batch", "head"),
            P("batch", "head"),
            P("batch", "head"),
            P("head", "batch"),
            P("head", "batch"),
            P("head", "batch"),
        ),
        check_vma=False,
    )
```

```python
import functools

import jax
import jax.numpy as jnp
from jax import lax
from jax.experimental import pallas as pl
from jax.experimental.pallas import tpu as pltpu
from jax.sharding import PartitionSpec as P

HD = 64
FRAMES = 4
PMAX = 784
PSMALL = 196
STEP = 5
SLOTS = 208
ROWS = FRAMES * SLOTS
GROUP = 192
QKV = 3 * GROUP


EXACT = lax.Precision.HIGHEST
TEMPER = 0.05
BETA_ONE = 0.5
BETA_TWO = 0.5
RATE = 0.04
NORM_RATE = 0.3
DECAY = 0.05
ADAM_EPS = 1e-08
CLIP_AT = 1.0
LOWER = jnp.bfloat16
SINGLE = jnp.float32
ALL = ("batch", "head")
GRANT = 56 << 20

NN = (((1,), (0,)), ((), ()))
NT = (((1,), (1,)), ((), ()))
TN = (((0,), (0,)), ((), ()))


def dot(left, right, dims=NN):
    return lax.dot_general(left, right, dims, preferred_element_type=SINGLE)


def low(value):
    return value.astype(LOWER)


def layer_norm(value, gain, bias):
    center = value - jnp.mean(value, axis=-1, keepdims=True)
    spread = jnp.mean(center * center, axis=-1, keepdims=True)
    return center * lax.rsqrt(spread + 1e-06) * gain + bias


def three_parts(value):
    high = low(value)
    rest = value - high.astype(SINGLE)
    middle = low(rest)
    return high, middle, low(rest - middle.astype(SINGLE))


def frame_probs(query, keys):
    scores = [jnp.sum(query * key, axis=0, keepdims=True) * HD ** (-0.5) for key in keys]
    top = functools.reduce(jnp.maximum, scores)
    raised = [jnp.exp(score - top) for score in scores]
    total = functools.reduce(jnp.add, raised)
    return [value / total for value in raised]


def rounded(value):
    return low(value).astype(SINGLE)


def frame_rows(f):
    return slice(SLOTS * f, SLOTS * (f + 1))


def split_frames(rows):
    return [rows[frame_rows(f)] for f in range(FRAMES)]


def head_features(which, head):
    return slice(GROUP * which + HD * head, GROUP * which + HD * (head + 1))


def temporal_fwd_kernel(normed_ref, weight_ref, qkv_ref, mixed_ref, out):
    for f in range(FRAMES):
        qkv_ref[0, f] = low(dot(normed_ref[frame_rows(f), :], weight_ref[0, :, :QKV])).T
    for head in range(GROUP // HD):
        query, keys, values = (
            [qkv_ref[0, f, head_features(i, head), :].astype(SINGLE) for f in range(FRAMES)]
            for i in range(3)
        )
        for f in range(FRAMES):
            probs = frame_probs(query[f], keys)
            mixed = sum(rounded(prob) * value for prob, value in zip(probs, values))
            out[f, head_features(0, head), :] = low(mixed)
    for f in range(FRAMES):
        mixed_ref[0, frame_rows(f), :] = out[f].T


def temporal_bwd_kernel(
    normed_ref,
    grad_ref,
    weight_ref,
    qkv_ref,
    mixed_ref,
    dweight_ref,
    dnormed_ref,
    dqkv,
    dmix,
    dcol,
):
    scale = HD ** (-0.5)
    for f in range(FRAMES):
        dmix[f] = low(dot(grad_ref[frame_rows(f), :], weight_ref[0, :, QKV:])).T
    for head in range(GROUP // HD):
        query, keys, values = (
            [qkv_ref[0, f, head_features(i, head), :].astype(SINGLE) for f in range(FRAMES)]
            for i in range(3)
        )
        d_keys = [jnp.zeros((HD, SLOTS), SINGLE) for _ in range(FRAMES)]
        d_values = [jnp.zeros((HD, SLOTS), SINGLE) for _ in range(FRAMES)]
        for f in range(FRAMES):
            d_mixed = dmix[f, head_features(0, head), :].astype(SINGLE)
            probs = frame_probs(query[f], keys)
            d_probs = [jnp.sum(d_mixed * value, axis=0, keepdims=True) for value in values]
            row = sum(prob * d_prob for prob, d_prob in zip(probs, d_probs))
            d_query = jnp.zeros((HD, SLOTS), SINGLE)
            for g in range(FRAMES):
                d_score = rounded(probs[g] * (d_probs[g] - row))
                d_query = d_query + d_score * keys[g]
                d_keys[g] = d_keys[g] + d_score * query[f]
                d_values[g] = d_values[g] + rounded(probs[g]) * d_mixed
            dcol[f, head_features(0, head), :] = low(d_query * scale)
        for g in range(FRAMES):
            dcol[g, head_features(1, head), :] = low(d_keys[g] * scale)
            dcol[g, head_features(2, head), :] = low(d_values[g])
    for f in range(FRAMES):
        dqkv[frame_rows(f), :] = dcol[f].T
    finish_backward(normed_ref, grad_ref, weight_ref, mixed_ref, dweight_ref, dnormed_ref, dqkv)


def finish_backward(
    normed_ref, grad_ref, weight_ref, mixed_ref, dweight_ref, dnormed_ref, dqkv
):
    dweight_ref[0, :, :QKV] = low(dot(normed_ref[...], dqkv[...], TN))
    dweight_ref[0, :, QKV:] = low(dot(grad_ref[...], mixed_ref[0], TN))
    d_normed = dot(dqkv[...], weight_ref[0, :, :QKV], NT)

    accumulate(dnormed_ref, d_normed)


def lane_pieces(pieces, rows):
    lane = lax.broadcasted_iota(jnp.int32, (rows, HD), 1)
    result = jnp.zeros((rows, HD), SINGLE)
    for number, piece in enumerate(pieces):
        result = jnp.where(lane == number, piece.astype(SINGLE), result)
    return low(result)


def spatial_fwd_kernel(
    normed_ref, weight_ref, key_extra_ref, qkv_ref, mixed_ref, extra_ref, branch_ref
):
    qkv_ref[0] = low(dot(normed_ref[...], weight_ref[0, :, :QKV]))
    one = jnp.ones((ROWS, 1), SINGLE)
    for head in range(GROUP // HD):
        at = HD * head
        query = qkv_ref[0, :, at : at + HD] * jnp.asarray(HD ** (-0.5), LOWER)
        query = jnp.concatenate([query, lane_pieces([one], ROWS)], axis=1)
        keys = jnp.concatenate(
            [qkv_ref[0, :, GROUP + at : GROUP + at + HD], key_extra_ref[...]], axis=1
        )
        values = jnp.concatenate(
            [qkv_ref[0, :, 2 * GROUP + at : 2 * GROUP + at + HD], lane_pieces([one], ROWS)], axis=1
        )
        score = dot(query, keys, NT)
        top = jnp.max(score, axis=1, keepdims=True)
        mixed = dot(low(jnp.exp(score - top)), values)
        total = mixed[:, HD : HD + 1]
        mixed_ref[0, :, at : at + HD] = low(mixed[:, :HD] / total)
        logsum = -(top + jnp.log(total))
        extra_ref[0, :, at : at + HD] = lane_pieces([one, *three_parts(logsum)], ROWS)
    branch = dot(mixed_ref[0], weight_ref[0, :, QKV:], NT)

    accumulate(branch_ref, branch)


def spatial_fwd_last_kernel(
    normed_ref,
    weight_ref,
    key_extra_ref,
    resid_ref,
    branch_ref,
    norms_ref,
    qkv_ref,
    mixed_ref,
    extra_ref,
    out_ref,
    out_normed_ref,
    branch,
):
    spatial_fwd_kernel(
        normed_ref, weight_ref, key_extra_ref, qkv_ref, mixed_ref, extra_ref, branch
    )

    @pl.when(pl.program_id(0) == 1)
    def _():
        for f in range(FRAMES):
            rows = frame_rows(f)
            value = resid_ref[rows, :] + (branch_ref[rows, :] + branch[rows, :])
            out_ref[rows, :] = value
            out_normed_ref[rows, :] = low(layer_norm(value, norms_ref[4:5, :], norms_ref[5:6, :]))


def spatial_bwd_kernel(
    normed_ref,
    grad_ref,
    weight_ref,
    qkv_ref,
    mixed_ref,
    extra_ref,
    key_extra_ref,
    dweight_ref,
    dnormed_ref,
    dqkv,
):
    scale = HD ** (-0.5)
    d_mixed_all = low(dot(grad_ref[...], weight_ref[0, :, QKV:]))
    one = jnp.ones((ROWS, 1), SINGLE)
    for head in range(GROUP // HD):
        at = HD * head
        query = qkv_ref[0, :, at : at + HD]
        query_long = jnp.concatenate(
            [query * jnp.asarray(scale, LOWER), extra_ref[0, :, at : at + HD]], axis=1
        )
        d_mixed = d_mixed_all[:, at : at + HD]
        delta = -jnp.sum(
            d_mixed.astype(SINGLE) * mixed_ref[0, :, at : at + HD].astype(SINGLE),
            axis=1,
            keepdims=True,
        )
        d_mixed_long = jnp.concatenate([d_mixed, lane_pieces(three_parts(delta), ROWS)], axis=1)
        d_query = jnp.zeros((ROWS, HD), SINGLE)
        for part in range(FRAMES):
            rows = slice(SLOTS * part, SLOTS * (part + 1))
            keys = qkv_ref[0, rows, GROUP + at : GROUP + at + HD]
            values = qkv_ref[0, rows, 2 * GROUP + at : 2 * GROUP + at + HD]
            keys_long = jnp.concatenate([keys, key_extra_ref[rows, :]], axis=1)
            values_long = jnp.concatenate(
                [values, lane_pieces([one[rows]] * 3, SLOTS)], axis=1
            )
            prob = jnp.exp(dot(keys_long, query_long, NT))
            d_score = low(prob * dot(values_long, d_mixed_long, NT))
            dqkv[rows, 2 * GROUP + at : 2 * GROUP + at + HD] = low(dot(low(prob), d_mixed))
            dqkv[rows, GROUP + at : GROUP + at + HD] = low(dot(d_score, query) * scale)
            d_query = d_query + dot(d_score, keys, TN)
        dqkv[:, at : at + HD] = low(d_query * scale)
    finish_backward(normed_ref, grad_ref, weight_ref, mixed_ref, dweight_ref, dnormed_ref, dqkv)


def spatial_bwd_last_kernel(
    normed_ref,
    grad_ref,
    weight_ref,
    qkv_ref,
    mixed_ref,
    extra_ref,
    key_extra_ref,
    resid_ref,
    dresid_ref,
    dother_ref,
    norms_ref,
    dweight_ref,
    drows_ref,
    dnorms_ref,
    dqkv,
    dnormed,
):
    spatial_bwd_kernel(
        normed_ref,
        grad_ref,
        weight_ref,
        qkv_ref,
        mixed_ref,
        extra_ref,
        key_extra_ref,
        dweight_ref,
        dnormed,
        dqkv,
    )

    @pl.when(pl.program_id(0) == 1)
    def _():
        norm_rows_back(
            resid_ref, norms_ref, 2, dother_ref, dnormed, dresid_ref, None, drows_ref, dnorms_ref
        )


def norm_back(value, gain, grad):
    center = value - jnp.mean(value, axis=-1, keepdims=True)
    inverse = lax.rsqrt(jnp.mean(center * center, axis=-1, keepdims=True) + 1e-06)
    hat = center * inverse
    scaled = grad * gain
    d_value = inverse * (
        scaled
        - jnp.mean(scaled, axis=-1, keepdims=True)
        - hat * jnp.mean(scaled * hat, axis=-1, keepdims=True)
    )
    return (
        d_value,
        jnp.sum(grad * hat, axis=0, keepdims=True),
        jnp.sum(grad, axis=0, keepdims=True),
    )


def norm_rows_back(
    resid_ref, norms_ref, at, dother_ref, dnormed_ref, dresid_ref, out_ref, rows_ref, dnorms_ref
):
    d_gain = jnp.zeros((1, resid_ref.shape[1]), SINGLE)
    d_bias = jnp.zeros((1, resid_ref.shape[1]), SINGLE)
    for f in range(FRAMES):
        rows = frame_rows(f)
        d_value, gain, bias = norm_back(
            resid_ref[rows, :],
            norms_ref[at : at + 1, :],
            dother_ref[rows, :] + dnormed_ref[rows, :],
        )
        d_value = d_value + dresid_ref[rows, :]
        if out_ref is not None:
            out_ref[rows, :] = d_value
        rows_ref[rows, :] = low(d_value)
        d_gain, d_bias = d_gain + gain, d_bias + bias
    dnorms_ref[0:1, :] = d_gain
    dnorms_ref[1:2, :] = d_bias


def accumulate(ref, value):
    first = pl.program_id(0) == 0
    ref[...] = jnp.where(first, value, ref[...] + value)


def feed_fwd_kernel(normed_ref, up_ref, down_ref, act_ref, slope_ref, branch_ref):
    hidden = dot(normed_ref[...], up_ref[0])
    root = 0.7978845608028654
    square = hidden * hidden
    bend = jnp.tanh(hidden * (root + root * 0.044715 * square))
    half = 0.5 + 0.5 * bend
    act_ref[0] = low(hidden * half)
    slope_ref[0] = low(
        half + hidden * (0.5 - 0.5 * bend * bend) * (root + 3.0 * root * 0.044715 * square)
    )
    accumulate(branch_ref, dot(act_ref[0], down_ref[0], NT))


def feed_fwd_last_kernel(
    normed_ref,
    up_ref,
    down_ref,
    resid_ref,
    branch_ref,
    norms_ref,
    valid_ref,
    act_ref,
    slope_ref,
    out_ref,
    sums_ref,
    branch,
):
    feed_fwd_kernel(normed_ref, up_ref, down_ref, act_ref, slope_ref, branch)

    @pl.when(pl.program_id(0) == 1)
    def _():
        sums = jnp.zeros(sums_ref.shape, SINGLE)
        for f in range(FRAMES):
            rows = frame_rows(f)
            value = resid_ref[rows, :] + (branch_ref[rows, :] + branch[rows, :])
            out_ref[rows, :] = value
            normed = layer_norm(value, norms_ref[6:7, :], norms_ref[7:8, :])
            sums = sums + jnp.sum(normed * valid_ref[rows, :], axis=0, keepdims=True)
        sums_ref[...] = sums


def feed_bwd_kernel(
    normed_ref, grad_ref, up_ref, down_ref, act_ref, slope_ref, dup_ref, ddown_ref, dnormed_ref, dhid
):
    dhid[...] = low(dot(grad_ref[...], down_ref[0]) * slope_ref[0].astype(SINGLE))
    ddown_ref[0] = low(dot(grad_ref[...], act_ref[0], TN))
    dup_ref[0] = low(dot(normed_ref[...], dhid[...], TN))
    accumulate(dnormed_ref, dot(dhid[...], up_ref[0], NT))


def feed_bwd_last_kernel(
    normed_ref,
    grad_ref,
    up_ref,
    down_ref,
    act_ref,
    slope_ref,
    resid_ref,
    dresid_ref,
    dother_ref,
    norms_ref,
    dup_ref,
    ddown_ref,
    out_ref,
    drows_ref,
    dnorms_ref,
    dhid,
    dnormed,
):
    feed_bwd_kernel(
        normed_ref, grad_ref, up_ref, down_ref, act_ref, slope_ref, dup_ref, ddown_ref, dnormed, dhid
    )

    @pl.when(pl.program_id(0) == 1)
    def _():
        norm_rows_back(
            resid_ref, norms_ref, 4, dother_ref, dnormed, dresid_ref, out_ref, drows_ref, dnorms_ref
        )


def embed_kernel(patches_ref, early_ref, valid_ref, start_ref, normed_ref, norms_ref):
    dim = start_ref.shape[1]
    norms = early_ref[:, dim : dim + 128].astype(SINGLE).T[:8]
    norms_ref[...] = norms
    for f in range(FRAMES):
        rows = frame_rows(f)
        start = dot(patches_ref[rows, :], early_ref[:, :dim]) * valid_ref[rows, :]
        start_ref[rows, :] = start
        normed_ref[rows, :] = low(layer_norm(start, norms[0:1], norms[1:2]))


def embed_bwd_kernel(
    patches_ref, start_ref, valid_ref, drows_ref, da_ref, db_ref, norms_ref, dnorms_ref, out_ref, dstart
):
    dim = start_ref.shape[1]
    d_gain, d_bias = jnp.zeros((1, dim), SINGLE), jnp.zeros((1, dim), SINGLE)
    for f in range(FRAMES):
        rows = frame_rows(f)
        d_value, gain, bias = norm_back(
            start_ref[rows, :], norms_ref[0:1, :], da_ref[rows, :] + db_ref[rows, :]
        )
        dstart[rows, :] = low((drows_ref[rows, :].astype(SINGLE) + d_value) * valid_ref[rows, :])
        d_gain, d_bias = d_gain + gain, d_bias + bias
    out_ref[:, :dim] = low(dot(patches_ref[...], dstart[...], TN))
    padded = jnp.concatenate(
        [d_gain, d_bias, dnorms_ref[...], jnp.zeros((120, dim), SINGLE)], axis=0
    )
    out_ref[:, dim : dim + 128] = low(padded.T)


def enter_frame_kernel(
    patches_ref, early_ref, valid_ref, mixed_ref, own_ref, other_ref, norms_ref, out_ref, normed_ref
):
    for f in range(FRAMES):
        rows = frame_rows(f)
        value = dot(patches_ref[rows, :], early_ref[:, : out_ref.shape[1]]) * valid_ref[rows, :]
        for place, (ref, at) in enumerate(
            ((own_ref, 0), (own_ref, 1), (other_ref, 0), (other_ref, 1))
        ):
            mixed = mixed_ref[rows, GROUP * place : GROUP * (place + 1)]
            value = value + dot(mixed, ref[at, :, QKV:], NT)
        out_ref[rows, :] = value
        normed_ref[rows, :] = low(layer_norm(value, norms_ref[2:3, :], norms_ref[3:4, :]))


def loss_kernel(
    dim,
    classes,
    proj,
    clip_ref,
    facts_ref,
    small_ref,
    resid_ref,
    valid_ref,
    norms_ref,
    loss_ref,
    dsmall_ref,
    pooled_ref,
    dresid_ref,
    drows_ref,
    dnorms_ref,
    dpool,
):
    facts = facts_ref[...]
    count = facts.shape[0]
    label, mate = (facts[:, dim + i : dim + i + 1].astype(jnp.int32) for i in range(2))
    pooled = low(facts[:, :dim] / facts[:, dim + 2 : dim + 3])
    pooled_ref[...] = pooled
    both = dot(pooled, small_ref[...])
    lane = lax.broadcasted_iota(jnp.int32, both.shape, 1)
    logits = jnp.where(lane < classes, both, -1e30)
    hot = (lane == label).astype(SINGLE)
    top = jnp.max(logits, axis=1, keepdims=True)
    raised = jnp.exp(logits - top)
    total = jnp.sum(raised, axis=1, keepdims=True)
    cross = top + jnp.log(total) - jnp.sum(both * hot, axis=1, keepdims=True)
    d_logits = raised / total - hot
    embedding = jnp.where((lane >= classes) & (lane < classes + proj), both, 0.0)
    inverse = lax.rsqrt(jnp.sum(embedding * embedding, axis=1, keepdims=True) + 1e-06)
    unit = embedding * inverse
    exact = functools.partial(
        lax.dot_general, precision=EXACT, preferred_element_type=SINGLE
    )
    similar = exact(unit, unit, NT) / TEMPER
    row = lax.broadcasted_iota(jnp.int32, (count, count), 0)
    col = lax.broadcasted_iota(jnp.int32, (count, count), 1)
    mate_hot = (col == mate).astype(SINGLE)
    masked = jnp.where(row == col, -1e30, similar)
    top = jnp.max(masked, axis=1, keepdims=True)
    raised = jnp.exp(masked - top)
    total = jnp.sum(raised, axis=1, keepdims=True)
    contrast = top + jnp.log(total) - jnp.sum(similar * mate_hot, axis=1, keepdims=True)
    loss_ref[...] = jnp.sum(cross + contrast, axis=0, keepdims=True)
    d_similar = (raised / total - mate_hot) / TEMPER
    d_unit = exact(d_similar, unit, NN) + exact(d_similar, unit, TN)
    d_embed = inverse * d_unit - embedding * (inverse * inverse * inverse) * jnp.sum(
        embedding * d_unit, axis=1, keepdims=True
    )
    dsmall_ref[...] = low(jnp.where(lane < classes, d_logits, d_embed))
    dpool[...] = dot(dsmall_ref[...], small_ref[...], NT) / facts[:, dim + 2 : dim + 3]
    d_pooled = dpool[pl.ds(clip_ref[0], 1), :]
    d_gain, d_bias = jnp.zeros((1, dim), SINGLE), jnp.zeros((1, dim), SINGLE)
    for f in range(FRAMES):
        rows = frame_rows(f)
        d_value, gain, bias = norm_back(
            resid_ref[rows, :], norms_ref[6:7, :], valid_ref[rows, :] * d_pooled
        )
        dresid_ref[rows, :] = d_value
        drows_ref[rows, :] = low(d_value)
        d_gain, d_bias = d_gain + gain, d_bias + bias
    dnorms_ref[0:1, :] = d_gain
    dnorms_ref[1:2, :] = d_bias


def adam_step(master, first, second, clipped, rate):
    first_new = BETA_ONE * first + (1.0 - BETA_ONE) * clipped
    second_new = BETA_TWO * second + (1.0 - BETA_TWO) * clipped * clipped
    first_hat = first_new / (1.0 - BETA_ONE**STEP)
    second_hat = second_new / (1.0 - BETA_TWO**STEP)
    master_new = master - rate * (first_hat / (jnp.sqrt(second_hat) + ADAM_EPS) + DECAY * master)
    return (master_new, first_new, second_new)


def adam_kernel(classes, proj, total_ref, *refs):
    masters, firsts, seconds, parts, outs = (
        refs[0:8], refs[8:16], refs[16:24], refs[24:30], refs[31:]
    )
    norm = jnp.sqrt(total_ref[...])
    refs[30][...] = norm
    factor = jnp.minimum(1.0, CLIP_AT / (norm + 1e-06))
    early, small, first, second, up, down = (ref[...] * factor for ref in parts)
    dim = masters[0].shape[1]
    columns = lambda k: slice(GROUP * k, GROUP * (k + 1))
    todo = [
        (0, ..., early[:, :dim]),
        (1, ..., early[:, dim : dim + 128].T[:8]),
        (2, ..., small[:, :classes]),
        (3, ..., small[:, classes : classes + proj]),
        (6, ..., up),
        (7, ..., down),
    ]
    for layer, grad in enumerate((first, second)):
        todo += [(4, (layer, k), grad[:, columns(k)]) for k in range(3)]
        todo.append((5, layer, grad[:, columns(3)].T))
    for i, at, grad in todo:
        results = adam_step(
            masters[i][at], firsts[i][at], seconds[i][at], grad, NORM_RATE if i == 1 else RATE
        )
        for j, result in enumerate(results):
            outs[3 * i + j][at] = result


def whole(shape):
    return pl.BlockSpec(shape, lambda g: (0,) * len(shape))


def per_group(rows, width):
    return pl.BlockSpec((1, rows, width), lambda g: (g, 0, 0))


def columns_of(width):
    return pl.BlockSpec((1, FRAMES, width, SLOTS), lambda g: (g, 0, 0, 0))


def shaped(*shape, dtype=SINGLE):
    return jax.ShapeDtypeStruct(shape, dtype)


def spec_of(value):
    shape = value.shape
    if len(shape) == 4:
        return columns_of(shape[2])
    return per_group(*shape[1:]) if len(shape) == 3 else whole(shape)


def call(kernel, name, inputs, outputs, scratch=(), gflops=1, steps=2, in_specs=None):
    return pl.pallas_call(
        kernel,
        grid=(steps,),
        in_specs=in_specs or [spec_of(value) for value in inputs],
        out_specs=[spec_of(value) for value in outputs],
        out_shape=list(outputs),
        scratch_shapes=[pltpu.VMEM(shape, dtype) for shape, dtype in scratch],
        compiler_params=pltpu.CompilerParams(vmem_limit_bytes=GRANT),
        cost_estimate=pl.CostEstimate(
            flops=gflops * 10**9, bytes_accessed=8 << 20, transcendentals=0
        ),
        name=name,
    )(*inputs)


def by_group(width, rows=ROWS):
    return shaped(2, rows, width, dtype=LOWER)


def temporal_forward(normed, weight):
    return call(
        temporal_fwd_kernel,
        "temporal_forward",
        (normed, weight),
        (shaped(2, FRAMES, QKV, SLOTS, dtype=LOWER), by_group(GROUP)),
        [((FRAMES, GROUP, SLOTS), LOWER)],
        5,
    )


def temporal_backward(normed, grad, weight, qkv, mixed):
    dim = normed.shape[1]
    return call(
        temporal_bwd_kernel,
        "temporal_backward",
        (normed, grad, weight, qkv, mixed),
        (by_group(dim, dim), shaped(ROWS, dim)),
        [((ROWS, QKV), LOWER), ((FRAMES, GROUP, SLOTS), LOWER), ((FRAMES, QKV, SLOTS), LOWER)],
        14,
    )


def spatial_forward(normed, weight, key_extra, last=None):
    dim = normed.shape[1]
    saved = (by_group(QKV), by_group(GROUP), by_group(GROUP))
    inputs = (normed, weight, key_extra)
    if last is None:
        return call(
            spatial_fwd_kernel, "spatial_forward", inputs, (*saved, shaped(ROWS, dim)), [], 15
        )
    return call(
        spatial_fwd_last_kernel,
        "spatial_forward",
        (*inputs, *last),
        (*saved, shaped(ROWS, dim), shaped(ROWS, dim, dtype=LOWER)),
        [((ROWS, dim), SINGLE)],
        15,
    )


def spatial_backward(normed, grad, weight, qkv, mixed, extra, key_extra, last=None):
    dim = normed.shape[1]
    inputs = (normed, grad, weight, qkv, mixed, extra, key_extra)
    scratch = [((ROWS, QKV), LOWER)]
    if last is None:
        outputs = (by_group(dim, dim), shaped(ROWS, dim))
        return call(spatial_bwd_kernel, "spatial_backward", inputs, outputs, scratch, 30)
    return call(
        spatial_bwd_last_kernel,
        "spatial_backward",
        (*inputs, *last),
        (by_group(dim, dim), shaped(ROWS, dim, dtype=LOWER), shaped(2, dim)),
        scratch + [((ROWS, dim), SINGLE)],
        30,
    )


def feed_forward(normed, up, down, last=None):
    dim, width = normed.shape[1], up.shape[2]
    inputs, saved = (normed, up, down), (by_group(width), by_group(width))
    if last is None:
        return call(feed_fwd_kernel, "feed_forward", inputs, (*saved, shaped(ROWS, dim)), [], 10)
    return call(
        feed_fwd_last_kernel,
        "feed_forward",
        (*inputs, *last),
        (*saved, shaped(ROWS, dim), shaped(1, dim)),
        [((ROWS, dim), SINGLE)],
        10,
    )


def feed_backward(normed, grad, up, down, act, slope, last=None):
    dim, width = normed.shape[1], up.shape[2]
    inputs = (normed, grad, up, down, act, slope)
    weights = (by_group(width, dim), by_group(width, dim))
    scratch = [((ROWS, width), LOWER)]
    if last is None:
        outputs = (*weights, shaped(ROWS, dim))
        return call(feed_bwd_kernel, "feed_backward", inputs, outputs, scratch, 15)
    return call(
        feed_bwd_last_kernel,
        "feed_backward",
        (*inputs, *last),
        (*weights, shaped(ROWS, dim), shaped(ROWS, dim, dtype=LOWER), shaped(2, dim)),
        scratch + [((ROWS, dim), SINGLE)],
        15,
    )


def embed(patches, early, valid):
    dim = patches.shape[1]
    outputs = (shaped(ROWS, dim), shaped(ROWS, dim, dtype=LOWER), shaped(8, dim))
    return call(embed_kernel, "embed", (patches, early, valid), outputs, steps=1)


def embed_backward(patches, start, valid, d_rows, d_a, d_b, norms, d_norms):
    dim = patches.shape[1]
    return call(
        embed_bwd_kernel,
        "embed_backward",
        (patches, start, valid, d_rows, d_a, d_b, norms, d_norms),
        (shaped(dim, dim + 128, dtype=LOWER),),
        [((ROWS, dim), LOWER)],
        2,
        1,
    )[0]


def enter_frame(patches, early, valid, mixed, own, other, norms):
    dim = patches.shape[1]
    inputs = (patches, early, valid, mixed, own, other, norms)
    return call(
        enter_frame_kernel,
        "enter_frame",
        inputs,
        (shaped(ROWS, dim), shaped(ROWS, dim, dtype=LOWER)),
        [],
        2,
        1,
        [whole(value.shape) for value in inputs],
    )


def all_losses(clip, facts, small, resid, valid, norms, classes, proj):
    count, dim = facts.shape[0], resid.shape[1]
    inputs = (facts, small, resid, valid, norms)
    return call(
        functools.partial(loss_kernel, dim, classes, proj),
        "losses",
        (clip, *inputs),
        (
            shaped(1, 1),
            shaped(count, dim, dtype=LOWER),
            shaped(count, dim, dtype=LOWER),
            shaped(ROWS, dim),
            shaped(ROWS, dim, dtype=LOWER),
            shaped(2, dim),
        ),
        [((count, dim), SINGLE)],
        1,
        1,
        [pl.BlockSpec(memory_space=pltpu.SMEM)] + [whole(value.shape) for value in inputs],
    )


def optimizer(total, masters, firsts, seconds, parts, classes, proj):
    inputs = (total, *masters, *firsts, *seconds, *parts)
    outputs = [shaped(1, 1)] + [shaped(*value.shape) for value in masters for _ in range(3)]
    return pl.pallas_call(
        functools.partial(adam_kernel, classes, proj),
        grid=(1,),
        in_specs=[whole(value.shape) for value in inputs],
        out_specs=[whole(value.shape) for value in outputs],
        out_shape=outputs,
        compiler_params=pltpu.CompilerParams(vmem_limit_bytes=GRANT),
        name="optimizer",
    )(*inputs)


def tick(*values):
    return lax.optimization_barrier(values)


def summed(terms):
    return functools.reduce(jnp.add, (term.astype(SINGLE) for term in terms))


class Cube:
    def __init__(self, sizes):
        self.count = sizes["batch"] * sizes["head"]
        self.mine = lax.axis_index(ALL)
        batch_bits = sizes["batch"].bit_length() - 1
        self.batch_masks = [4 << k for k in reversed(range(batch_bits))]

    def swap(self, value, mask):
        return lax.ppermute(value, ALL, [(i, i ^ mask) for i in range(self.count)])

    def has(self, mask):
        return (self.mine & mask) != 0

    def join(self, value, *masks):
        for mask in masks:
            other = self.swap(value, mask)
            has = self.has(mask)
            both = jnp.stack([jnp.where(has, other, value), jnp.where(has, value, other)], axis=-3)
            shape = value.shape
            value = both.reshape(*shape[:-3], 2 * shape[-3], *shape[-2:])
        return value

    def fork(self, value):
        return jnp.stack([value, self.swap(value, 2)])


    def shed(self, terms, *masks):
        for mask in masks:
            shape = terms[0].shape
            has = self.has(mask)
            send, keep = [], []
            for term in terms:
                pair = term.reshape(*shape[:-3], shape[-3] // 2, 2, *shape[-2:])
                send.append(jnp.where(has, pair[..., 0, :, :], pair[..., 1, :, :]))
                keep.append(jnp.where(has, pair[..., 1, :, :], pair[..., 0, :, :]))
            terms = keep + [self.swap(low(summed(send)), mask)]
        return terms

    def meet(self, terms):
        send = low(summed([term[1] for term in terms]))
        return [term[0] for term in terms] + [self.swap(send, 2)]

    def total(self, value):
        for mask in [1, 2] + self.batch_masks[::-1]:
            value = value + self.swap(value, mask)
        return value

    def swap_frames(self, parts):
        return [parts[0]] + [self.swap(parts[r], r) for r in range(1, FRAMES)]


def body(sizes, *args):
    patches, bucket, labels, partner = args[:4]
    views = [lambda v: v] * 4 + [
        lambda v: v.transpose(0, 2, 1, 3), lambda v: v, lambda v: v, lambda v: v.T
    ]
    masters, firsts, seconds = (
        [view(value) for view, value in zip(views, args[4 + 8 * i : 12 + 8 * i])] for i in range(3)
    )
    patch_weight, norm_params, head_weight, proj_weight, attn_in, attn_out, up, down = masters
    cube = Cube(sizes)
    dim = norm_params.shape[1] * cube.count
    classes, proj = head_weight.shape[1], proj_weight.shape[1]
    rows_wide, rows_small = attn_in.shape[2], patch_weight.shape[0]
    place = lax.axis_index("head")

    *first, near, last = cube.batch_masks
    middle = dim // 2
    flat = lambda value: value.reshape(2, dim, -1)
    blocked = lambda value: value.reshape(*value.shape[:-2], -1, rows_wide, value.shape[-1])
    pack = lambda w_in, w_out: jnp.concatenate(
        [low(w_in[0]), low(w_in[1]), low(w_in[2]), low(w_out).T], axis=1
    )[None]
    patch_count = jnp.where(bucket == 1, PMAX, PSMALL)
    offset = jnp.arange(SLOTS)[None, :]
    number = (place ^ jnp.arange(FRAMES))[:, None]
    frame_valid = ((number * SLOTS + offset) < patch_count).reshape(ROWS, 1).astype(SINGLE)
    slot_valid = (jnp.broadcast_to(place * SLOTS + offset, (FRAMES, SLOTS)) < patch_count).reshape(
        ROWS, 1
    ).astype(SINGLE)
    lane = jnp.arange(HD)[None, :]
    key_extra = low(
        jnp.where(lane == 0, jnp.where(frame_valid > 0, 0.0, -1e30), (lane < 4).astype(SINGLE))
    )

    first_w = pack(attn_in[0], attn_out[0])
    first_w, clip, w_patch, w_norms = tick(first_w, patches[0], patch_weight, norm_params)
    first_w = cube.join(first_w, *first)
    early = jnp.concatenate([low(w_patch), low(w_norms).T], axis=1)
    early = jnp.pad(early, ((0, 0), (0, 120)))[None]
    early = cube.join(early, *first)
    blocks = jnp.pad(clip, ((0, ROWS - PMAX), (0, 0))).reshape(FRAMES, SLOTS, -1)
    blocks = jnp.where((place & 1) != 0, blocks[jnp.array([1, 0, 3, 2])], blocks)
    blocks = jnp.where((place & 2) != 0, blocks[jnp.array([2, 3, 0, 1])], blocks)
    second_w = pack(attn_in[1], attn_out[1])
    first_w, early, blocks, second_w = tick(first_w, early, blocks, second_w)

    first_w = cube.join(first_w, near)
    early = cube.join(early, near)
    by_frame = blocks.reshape(ROWS, -1)
    by_slot = jnp.concatenate(cube.swap_frames(list(blocks)))
    up_w, down_w = low(up)[None], low(down)[None]
    first_w, early, by_slot, up_w, down_w = tick(first_w, early, by_slot, up_w, down_w)

    left = cube.join(first_w[..., :middle], last)
    right = cube.fork(first_w[..., middle:])
    early = cube.join(early, last)
    second_w, up_w = cube.join(second_w, *first), cube.join(up_w, *first)
    left, right, early, second_w, up_w = tick(left, right, early, second_w, up_w)

    left, right = cube.fork(left), cube.join(right, last)
    own_first = jnp.concatenate([flat(left), flat(right)], axis=-1)
    early = cube.join(early, 2)
    second_w, up_w = cube.join(second_w, near), cube.join(up_w, near)
    own_first, early, second_w, up_w = tick(own_first, early, second_w, up_w)

    early = cube.join(early, 1).reshape(dim, -1)
    other_first = cube.swap(own_first, 1)
    second_w, up_w, down_w = cube.fork(second_w), cube.join(up_w, last), cube.join(down_w, *first)
    start_slot, normed_t, norms = embed(by_slot, early, slot_valid)
    qkv_t, mixed_t = [None, None], [None, None]
    qkv_t[0], mixed_t[0] = temporal_forward(normed_t, own_first)
    mixed_t[0], normed_t, second_w, other_first, up_w, down_w = tick(
        mixed_t[0], normed_t, second_w, other_first, up_w, down_w
    )
    qkv_t[1], mixed_t[1] = temporal_forward(normed_t, other_first)
    own_second, down_w = flat(cube.join(second_w, last)), cube.join(down_w, near)
    small = jnp.concatenate([low(head_weight), low(proj_weight)], axis=1)
    small = cube.join(jnp.pad(small, ((0, 0), (0, dim - small.shape[1])))[None], *first)
    order = (0, 2, 1, 3)
    pieces = {m: mixed_t[m % 2][m // 2] for m in range(4)}
    parts = [
        jnp.concatenate([pieces[m ^ r][frame_rows(r)] for m in order], axis=1)
        for r in range(FRAMES)
    ]
    parts[0], parts[1], parts[2], parts[3], down_w, small = tick(*parts, down_w, small)

    mixed_frame = jnp.concatenate(cube.swap_frames(parts))
    small = cube.join(small, near)
    mixed_frame, own_second, small = tick(mixed_frame, own_second, small)

    resid_one, normed_s = enter_frame(
        by_frame, early, frame_valid, mixed_frame, own_first, other_first, norms
    )
    down_w, own_up = cube.fork(down_w), flat(cube.fork(up_w))
    other_second = cube.swap(own_second, 1)
    small = cube.join(small, last)
    qkv_s, mixed_s, extra_s = ([None, None] for _ in range(3))
    qkv_s[0], mixed_s[0], extra_s[0], branch = spatial_forward(normed_s, own_second, key_extra)
    branch, normed_s, other_second, down_w, small = tick(
        branch, normed_s, other_second, down_w, small
    )
    own_down = flat(cube.join(down_w, last))
    qkv_s[1], mixed_s[1], extra_s[1], resid_two, normed_m = spatial_forward(
        normed_s, other_second, key_extra, (resid_one, branch, norms)
    )
    normed_m, own_up, own_down = tick(normed_m, own_up, own_down)

    other_up, other_down = cube.swap(own_up, 1), cube.swap(own_down, 1)
    small = cube.join(small, 2)
    act, slope = ([None, None] for _ in range(2))
    act[0], slope[0], branch = feed_forward(normed_m, own_up, own_down)
    branch, normed_m, other_up, other_down, small = tick(
        branch, normed_m, other_up, other_down, small
    )
    act[1], slope[1], resid_three, sums = feed_forward(
        normed_m, other_up, other_down, (resid_two, branch, norms, frame_valid)
    )
    small = cube.join(small, 1).reshape(dim, -1)

    for mask in (1, 2):
        sums = sums + cube.swap(sums, mask)
    facts = jnp.stack([labels[0], partner[0], FRAMES * patch_count[0]]).astype(SINGLE)
    gathered = jnp.concatenate([sums, jnp.pad(facts, (0, 125))[None]], axis=1)[None]
    gathered = cube.join(gathered, *cube.batch_masks)[:, 0]
    clip = lax.axis_index("batch").reshape(1)
    loss_sum, d_small, pooled_low, d_resid, d_rows, d_norms_f = all_losses(
        clip, gathered, small, resid_three, frame_valid, norms, classes, proj
    )

    d_up, d_down = [None, None], [None, None]
    d_up[1], d_down[1], d_normed = feed_backward(
        normed_m, d_rows, other_up, other_down, act[1], slope[1]
    )
    up_other, down_other, d_normed, d_rows, normed_m = tick(
        d_up[1], d_down[1], d_normed, d_rows, normed_m
    )
    core_up, core_down = cube.swap(up_other, 1), cube.swap(down_other, 1)
    d_up[0], d_down[0], d_resid, d_rows, d_norms_m = feed_backward(
        normed_m,
        d_rows,
        own_up,
        own_down,
        act[0],
        slope[0],
        (resid_two, d_resid, d_normed, norms),
    )
    d_resid, d_rows, up_own, down_own, core_up, core_down = tick(
        d_resid, d_rows, d_up[0], d_down[0], core_up, core_down
    )

    sum_up = cube.meet([blocked(up_own), blocked(core_up)])
    sum_down = cube.shed([blocked(down_own), blocked(core_down)], last)
    d_second = [None, None]
    d_second[1], d_normed = spatial_backward(
        normed_s, d_rows, other_second, qkv_s[1], mixed_s[1], extra_s[1], key_extra
    )
    d_small = lax.dynamic_slice_in_dim(
        dot(pooled_low, d_small, TN), cube.mine * rows_small, rows_small, 0
    )
    second_other, d_normed, d_rows, normed_s, sum_up[-1], sum_down[-1], d_small = tick(
        d_second[1], d_normed, d_rows, normed_s, sum_up[-1], sum_down[-1], d_small
    )
    core_second = cube.swap(second_other, 1)
    sum_up, sum_down = cube.shed(sum_up, last), cube.meet(sum_down)
    d_second[0], d_rows, d_norms_s = spatial_backward(
        normed_s,
        d_rows,
        own_second,
        qkv_s[0],
        mixed_s[0],
        extra_s[0],
        key_extra,
        (resid_one, d_resid, d_normed, norms),
    )
    d_rows, second_own, sum_up[-1], sum_down[-1], core_second = tick(
        d_rows, d_second[0], sum_up[-1], sum_down[-1], core_second
    )

    d_rows = jnp.concatenate(cube.swap_frames(split_frames(d_rows)))
    sum_second = cube.shed([blocked(second_own), blocked(core_second)], last)
    d_rows, up_last, down_last = tick(d_rows, sum_up[-1], sum_down[-1])
    sum_up[-1], sum_down[-1] = up_last, down_last

    sum_up, sum_down = cube.shed(sum_up, near), cube.shed(sum_down, near)
    d_first, d_normed = [None, None], [None, None]
    d_first[1], d_normed[1] = temporal_backward(
        normed_t, d_rows, other_first, qkv_t[1], mixed_t[1]
    )
    first_other, d_normed[1], d_rows, normed_t, sum_up[-1], sum_down[-1], sum_second[-1] = tick(
        d_first[1], d_normed[1], d_rows, normed_t, sum_up[-1], sum_down[-1], sum_second[-1]
    )
    core_first = cube.swap(first_other, 1)
    sum_second = cube.meet(sum_second)
    sum_up, sum_down = cube.shed(sum_up, *first[::-1]), cube.shed(sum_down, *first[::-1])
    d_first[0], d_normed[0] = temporal_backward(
        normed_t, d_rows, own_first, qkv_t[0], mixed_t[0]
    )
    d_rows, first_own, d_normed[0], core_first, sum_second[-1], sum_up[-1], sum_down[-1] = tick(
        d_rows, d_first[0], d_normed[0], core_first, sum_second[-1], sum_up[-1], sum_down[-1]
    )

    sum_first = [blocked(first_own), blocked(core_first)]
    left = cube.meet([term[..., :middle] for term in sum_first])
    right = cube.shed([term[..., middle:] for term in sum_first], last)
    sum_second = cube.shed(sum_second, near)
    d_norms = jnp.concatenate([d_norms_s, d_norms_m, d_norms_f])
    d_early = embed_backward(
        by_slot, start_slot, slot_valid, d_rows, d_normed[0], d_normed[1], norms, d_norms
    )
    sum_early = cube.shed([d_early.reshape(-1, rows_small, dim + 128)], 1)
    d_up, d_down = summed(sum_up)[0], summed(sum_down)[0]
    square = lambda value: jnp.sum(value * value)
    squares = square(d_small) + square(d_up) + square(d_down)
    left[-1], right[-1], sum_early[-1], sum_second[-1], squares = tick(
        left[-1], right[-1], sum_early[-1], sum_second[-1], squares
    )
    left, right = cube.shed(left, last), cube.meet(right)
    sum_early = cube.shed(sum_early, 2)
    sum_second = cube.shed(sum_second, *first[::-1])
    left[-1], right[-1], sum_early[-1], sum_second[-1] = tick(
        left[-1], right[-1], sum_early[-1], sum_second[-1]
    )
    sum_first = [jnp.concatenate([summed(left), summed(right)], axis=-1)]
    sum_first = cube.shed(sum_first, near)
    sum_early = cube.shed(sum_early, last)
    d_second = summed(sum_second)[0]
    squares = squares + square(d_second)
    sum_first[-1], sum_early[-1], squares = tick(sum_first[-1], sum_early[-1], squares)
    sum_first = cube.shed(sum_first, *first[::-1])
    sum_early = cube.shed(sum_early, near)
    sum_first[-1], sum_early[-1] = tick(sum_first[-1], sum_early[-1])
    sum_early = cube.shed(sum_early, *first[::-1])
    d_first, d_early = summed(sum_first)[0], summed(sum_early)[0]

    total = cube.total((squares + square(d_first) + square(d_early)).reshape(1, 1))
    parts = (d_early, d_small, d_first, d_second, d_up, d_down)
    grad_norm, *updates = optimizer(total, masters, firsts, seconds, parts, classes, proj)
    updates = [views[i // 3](update) for i, update in enumerate(updates)]
    return (loss_sum[0, 0], grad_norm[0, 0], *updates)


def solution(mesh):
    placed = (
        P("batch", "head", None),
        P("batch"),
        P("batch"),
        P("batch"),
        P(("batch", "head"), None),
        P(None, ("batch", "head")),
        P(("batch", "head"), None),
        P(("batch", "head"), None),
        P(None, "batch", None, "head"),
        P(None, "head", "batch"),
        P("batch", "head"),
        P("head", "batch"),
        P(("batch", "head"), None),
        P(None, ("batch", "head")),
        P(("batch", "head"), None),
        P(("batch", "head"), None),
        P(None, "batch", None, "head"),
        P(None, "head", "batch"),
        P("batch", "head"),
        P("head", "batch"),
        P(("batch", "head"), None),
        P(None, ("batch", "head")),
        P(("batch", "head"), None),
        P(("batch", "head"), None),
        P(None, "batch", None, "head"),
        P(None, "head", "batch"),
        P("batch", "head"),
        P("head", "batch"),
    )
    return jax.shard_map(
        functools.partial(body, dict(mesh.shape)),
        mesh=mesh,
        in_specs=placed,
        out_specs=(
            P(),
            P(),
            P(("batch", "head"), None),
            P(("batch", "head"), None),
            P(("batch", "head"), None),
            P(None, ("batch", "head")),
            P(None, ("batch", "head")),
            P(None, ("batch", "head")),
            P(("batch", "head"), None),
            P(("batch", "head"), None),
            P(("batch", "head"), None),
            P(("batch", "head"), None),
            P(("batch", "head"), None),
            P(("batch", "head"), None),
            P(None, "batch", None, "head"),
            P(None, "batch", None, "head"),
            P(None, "batch", None, "head"),
            P(None, "head", "batch"),
            P(None, "head", "batch"),
            P(None, "head", "batch"),
            P("batch", "head"),
            P("batch", "head"),
            P("batch", "head"),
            P("head", "batch"),
            P("head", "batch"),
            P("head", "batch"),
        ),
        check_vma=False,
    )
```

```python
import functools

import jax
import jax.numpy as jnp
from jax import lax
from jax.experimental import pallas as pl
from jax.experimental.pallas import tpu as pltpu
from jax.sharding import Mesh
from jax.sharding import PartitionSpec as P

HD = 64
FRAMES = 4
PMAX = 784
PSMALL = 196
STEP = 5
SLOTS = 208
ROWS = FRAMES * SLOTS
GROUP = 192
QKV = 3 * GROUP


EXACT = lax.Precision.HIGHEST
TEMPER = 0.05
BETA_ONE = 0.5
BETA_TWO = 0.5
RATE = 0.04
NORM_RATE = 0.3
DECAY = 0.05
ADAM_EPS = 1e-08
CLIP_AT = 1.0
LOWER = jnp.bfloat16
SINGLE = jnp.float32
ALL = ("batch", "row", "core")
HEAD = ("row", "core")
GRANT = 56 << 20

NN = (((1,), (0,)), ((), ()))
NT = (((1,), (1,)), ((), ()))
TN = (((0,), (0,)), ((), ()))


def dot(left, right, dims=NN):
    return lax.dot_general(left, right, dims, preferred_element_type=SINGLE)


def low(value):
    return value.astype(LOWER)


def layer_norm(value, gain, bias):
    center = value - jnp.mean(value, axis=-1, keepdims=True)
    spread = jnp.mean(center * center, axis=-1, keepdims=True)
    return center * lax.rsqrt(spread + 1e-06) * gain + bias


def three_parts(value):
    high = low(value)
    rest = value - high.astype(SINGLE)
    middle = low(rest)
    return high, middle, low(rest - middle.astype(SINGLE))


def frame_probs(query, keys):
    scores = [jnp.sum(query * key, axis=0, keepdims=True) * HD ** (-0.5) for key in keys]
    top = functools.reduce(jnp.maximum, scores)
    raised = [jnp.exp(score - top) for score in scores]
    total = functools.reduce(jnp.add, raised)
    return [value / total for value in raised]


def rounded(value):
    return low(value).astype(SINGLE)


def frame_rows(f):
    return slice(SLOTS * f, SLOTS * (f + 1))


def split_frames(rows):
    return [rows[frame_rows(f)] for f in range(FRAMES)]


def head_features(which, head):
    return slice(GROUP * which + HD * head, GROUP * which + HD * (head + 1))


def temporal_fwd_kernel(normed_ref, weight_ref, qkv_ref, mixed_ref, out):
    for f in range(FRAMES):
        qkv_ref[0, f] = low(dot(normed_ref[frame_rows(f), :], weight_ref[0, :, :QKV])).T
    for head in range(GROUP // HD):
        query, keys, values = (
            [qkv_ref[0, f, head_features(i, head), :].astype(SINGLE) for f in range(FRAMES)]
            for i in range(3)
        )
        for f in range(FRAMES):
            probs = frame_probs(query[f], keys)
            mixed = sum(rounded(prob) * value for prob, value in zip(probs, values))
            out[f, head_features(0, head), :] = low(mixed)
    for f in range(FRAMES):
        mixed_ref[0, frame_rows(f), :] = out[f].T


def temporal_bwd_kernel(
    normed_ref,
    grad_ref,
    weight_ref,
    qkv_ref,
    mixed_ref,
    dweight_ref,
    dnormed_ref,
    dqkv,
    dmix,
    dcol,
):
    scale = HD ** (-0.5)
    for f in range(FRAMES):
        dmix[f] = low(dot(grad_ref[frame_rows(f), :], weight_ref[0, :, QKV:])).T
    for head in range(GROUP // HD):
        query, keys, values = (
            [qkv_ref[0, f, head_features(i, head), :].astype(SINGLE) for f in range(FRAMES)]
            for i in range(3)
        )
        d_keys = [jnp.zeros((HD, SLOTS), SINGLE) for _ in range(FRAMES)]
        d_values = [jnp.zeros((HD, SLOTS), SINGLE) for _ in range(FRAMES)]
        for f in range(FRAMES):
            d_mixed = dmix[f, head_features(0, head), :].astype(SINGLE)
            probs = frame_probs(query[f], keys)
            d_probs = [jnp.sum(d_mixed * value, axis=0, keepdims=True) for value in values]
            row = sum(prob * d_prob for prob, d_prob in zip(probs, d_probs))
            d_query = jnp.zeros((HD, SLOTS), SINGLE)
            for g in range(FRAMES):
                d_score = rounded(probs[g] * (d_probs[g] - row))
                d_query = d_query + d_score * keys[g]
                d_keys[g] = d_keys[g] + d_score * query[f]
                d_values[g] = d_values[g] + rounded(probs[g]) * d_mixed
            dcol[f, head_features(0, head), :] = low(d_query * scale)
        for g in range(FRAMES):
            dcol[g, head_features(1, head), :] = low(d_keys[g] * scale)
            dcol[g, head_features(2, head), :] = low(d_values[g])
    for f in range(FRAMES):
        dqkv[frame_rows(f), :] = dcol[f].T
    finish_backward(normed_ref, grad_ref, weight_ref, mixed_ref, dweight_ref, dnormed_ref, dqkv)


def finish_backward(
    normed_ref, grad_ref, weight_ref, mixed_ref, dweight_ref, dnormed_ref, dqkv
):
    dweight_ref[0, :, :QKV] = low(dot(normed_ref[...], dqkv[...], TN))
    dweight_ref[0, :, QKV:] = low(dot(grad_ref[...], mixed_ref[0], TN))
    d_normed = dot(dqkv[...], weight_ref[0, :, :QKV], NT)

    accumulate(dnormed_ref, d_normed)


def lane_pieces(pieces, rows):
    lane = lax.broadcasted_iota(jnp.int32, (rows, HD), 1)
    result = jnp.zeros((rows, HD), SINGLE)
    for number, piece in enumerate(pieces):
        result = jnp.where(lane == number, piece.astype(SINGLE), result)
    return low(result)


def spatial_fwd_kernel(
    normed_ref, weight_ref, key_extra_ref, qkv_ref, mixed_ref, extra_ref, branch_ref
):
    qkv_ref[0] = low(dot(normed_ref[...], weight_ref[0, :, :QKV]))
    one = jnp.ones((ROWS, 1), SINGLE)
    for head in range(GROUP // HD):
        at = HD * head
        query = qkv_ref[0, :, at : at + HD] * jnp.asarray(HD ** (-0.5), LOWER)
        query = jnp.concatenate([query, lane_pieces([one], ROWS)], axis=1)
        keys = jnp.concatenate(
            [qkv_ref[0, :, GROUP + at : GROUP + at + HD], key_extra_ref[...]], axis=1
        )
        values = jnp.concatenate(
            [qkv_ref[0, :, 2 * GROUP + at : 2 * GROUP + at + HD], lane_pieces([one], ROWS)], axis=1
        )
        score = dot(query, keys, NT)
        top = jnp.max(score, axis=1, keepdims=True)
        mixed = dot(low(jnp.exp(score - top)), values)
        total = mixed[:, HD : HD + 1]
        mixed_ref[0, :, at : at + HD] = low(mixed[:, :HD] / total)
        logsum = -(top + jnp.log(total))
        extra_ref[0, :, at : at + HD] = lane_pieces([one, *three_parts(logsum)], ROWS)
    branch = dot(mixed_ref[0], weight_ref[0, :, QKV:], NT)

    accumulate(branch_ref, branch)


def spatial_fwd_last_kernel(
    normed_ref,
    weight_ref,
    key_extra_ref,
    resid_ref,
    branch_ref,
    norms_ref,
    qkv_ref,
    mixed_ref,
    extra_ref,
    out_ref,
    out_normed_ref,
    branch,
):
    spatial_fwd_kernel(
        normed_ref, weight_ref, key_extra_ref, qkv_ref, mixed_ref, extra_ref, branch
    )

    @pl.when(pl.program_id(0) == 1)
    def _():
        for f in range(FRAMES):
            rows = frame_rows(f)
            value = resid_ref[rows, :] + (branch_ref[rows, :] + branch[rows, :])
            out_ref[rows, :] = value
            out_normed_ref[rows, :] = low(layer_norm(value, norms_ref[4:5, :], norms_ref[5:6, :]))


def spatial_bwd_kernel(
    normed_ref,
    grad_ref,
    weight_ref,
    qkv_ref,
    mixed_ref,
    extra_ref,
    key_extra_ref,
    dweight_ref,
    dnormed_ref,
    dqkv,
):
    scale = HD ** (-0.5)
    d_mixed_all = low(dot(grad_ref[...], weight_ref[0, :, QKV:]))
    one = jnp.ones((ROWS, 1), SINGLE)
    for head in range(GROUP // HD):
        at = HD * head
        query = qkv_ref[0, :, at : at + HD]
        query_long = jnp.concatenate(
            [query * jnp.asarray(scale, LOWER), extra_ref[0, :, at : at + HD]], axis=1
        )
        d_mixed = d_mixed_all[:, at : at + HD]
        delta = -jnp.sum(
            d_mixed.astype(SINGLE) * mixed_ref[0, :, at : at + HD].astype(SINGLE),
            axis=1,
            keepdims=True,
        )
        d_mixed_long = jnp.concatenate([d_mixed, lane_pieces(three_parts(delta), ROWS)], axis=1)
        d_query = jnp.zeros((ROWS, HD), SINGLE)
        for part in range(FRAMES):
            rows = slice(SLOTS * part, SLOTS * (part + 1))
            keys = qkv_ref[0, rows, GROUP + at : GROUP + at + HD]
            values = qkv_ref[0, rows, 2 * GROUP + at : 2 * GROUP + at + HD]
            keys_long = jnp.concatenate([keys, key_extra_ref[rows, :]], axis=1)
            values_long = jnp.concatenate(
                [values, lane_pieces([one[rows]] * 3, SLOTS)], axis=1
            )
            prob = jnp.exp(dot(keys_long, query_long, NT))
            d_score = low(prob * dot(values_long, d_mixed_long, NT))
            dqkv[rows, 2 * GROUP + at : 2 * GROUP + at + HD] = low(dot(low(prob), d_mixed))
            dqkv[rows, GROUP + at : GROUP + at + HD] = low(dot(d_score, query) * scale)
            d_query = d_query + dot(d_score, keys, TN)
        dqkv[:, at : at + HD] = low(d_query * scale)
    finish_backward(normed_ref, grad_ref, weight_ref, mixed_ref, dweight_ref, dnormed_ref, dqkv)


def spatial_bwd_last_kernel(
    normed_ref,
    grad_ref,
    weight_ref,
    qkv_ref,
    mixed_ref,
    extra_ref,
    key_extra_ref,
    resid_ref,
    dresid_ref,
    dother_ref,
    norms_ref,
    dweight_ref,
    drows_ref,
    dnorms_ref,
    dqkv,
    dnormed,
):
    spatial_bwd_kernel(
        normed_ref,
        grad_ref,
        weight_ref,
        qkv_ref,
        mixed_ref,
        extra_ref,
        key_extra_ref,
        dweight_ref,
        dnormed,
        dqkv,
    )

    @pl.when(pl.program_id(0) == 1)
    def _():
        norm_rows_back(
            resid_ref, norms_ref, 2, dother_ref, dnormed, dresid_ref, None, drows_ref, dnorms_ref
        )


def norm_back(value, gain, grad):
    center = value - jnp.mean(value, axis=-1, keepdims=True)
    inverse = lax.rsqrt(jnp.mean(center * center, axis=-1, keepdims=True) + 1e-06)
    hat = center * inverse
    scaled = grad * gain
    d_value = inverse * (
        scaled
        - jnp.mean(scaled, axis=-1, keepdims=True)
        - hat * jnp.mean(scaled * hat, axis=-1, keepdims=True)
    )
    return (
        d_value,
        jnp.sum(grad * hat, axis=0, keepdims=True),
        jnp.sum(grad, axis=0, keepdims=True),
    )


def norm_rows_back(
    resid_ref, norms_ref, at, dother_ref, dnormed_ref, dresid_ref, out_ref, rows_ref, dnorms_ref
):
    d_gain = jnp.zeros((1, resid_ref.shape[1]), SINGLE)
    d_bias = jnp.zeros((1, resid_ref.shape[1]), SINGLE)
    for f in range(FRAMES):
        rows = frame_rows(f)
        d_value, gain, bias = norm_back(
            resid_ref[rows, :],
            norms_ref[at : at + 1, :],
            dother_ref[rows, :] + dnormed_ref[rows, :],
        )
        d_value = d_value + dresid_ref[rows, :]
        if out_ref is not None:
            out_ref[rows, :] = d_value
        rows_ref[rows, :] = low(d_value)
        d_gain, d_bias = d_gain + gain, d_bias + bias
    dnorms_ref[0:1, :] = d_gain
    dnorms_ref[1:2, :] = d_bias


def accumulate(ref, value):
    first = pl.program_id(0) == 0
    ref[...] = jnp.where(first, value, ref[...] + value)


def wide(ref):
    return ref[0].reshape(-1, ref.shape[-1])


def feed_fwd_kernel(normed_ref, up_ref, down_ref, act_ref, slope_ref, branch_ref):
    hidden = dot(normed_ref[...], wide(up_ref))
    root = 0.7978845608028654
    square = hidden * hidden
    bend = jnp.tanh(hidden * (root + root * 0.044715 * square))
    half = 0.5 + 0.5 * bend
    act_ref[0] = low(hidden * half)
    slope_ref[0] = low(
        half + hidden * (0.5 - 0.5 * bend * bend) * (root + 3.0 * root * 0.044715 * square)
    )
    accumulate(branch_ref, dot(act_ref[0], wide(down_ref), NT))


def feed_fwd_last_kernel(
    normed_ref,
    up_ref,
    down_ref,
    resid_ref,
    branch_ref,
    norms_ref,
    valid_ref,
    act_ref,
    slope_ref,
    out_ref,
    sums_ref,
    branch,
):
    feed_fwd_kernel(normed_ref, up_ref, down_ref, act_ref, slope_ref, branch)

    @pl.when(pl.program_id(0) == 1)
    def _():
        sums = jnp.zeros(sums_ref.shape, SINGLE)
        for f in range(FRAMES):
            rows = frame_rows(f)
            value = resid_ref[rows, :] + (branch_ref[rows, :] + branch[rows, :])
            out_ref[rows, :] = value
            normed = layer_norm(value, norms_ref[6:7, :], norms_ref[7:8, :])
            sums = sums + jnp.sum(normed * valid_ref[rows, :], axis=0, keepdims=True)
        sums_ref[...] = sums


def feed_bwd_kernel(
    normed_ref, grad_ref, up_ref, down_ref, act_ref, slope_ref, dup_ref, ddown_ref, dnormed_ref, dhid
):
    dhid[...] = low(dot(grad_ref[...], wide(down_ref)) * slope_ref[0].astype(SINGLE))
    ddown_ref[0] = low(dot(grad_ref[...], act_ref[0], TN))
    dup_ref[0] = low(dot(normed_ref[...], dhid[...], TN))
    accumulate(dnormed_ref, dot(dhid[...], wide(up_ref), NT))


def feed_bwd_last_kernel(
    normed_ref,
    grad_ref,
    up_ref,
    down_ref,
    act_ref,
    slope_ref,
    resid_ref,
    dresid_ref,
    dother_ref,
    norms_ref,
    dup_ref,
    ddown_ref,
    out_ref,
    drows_ref,
    dnorms_ref,
    dhid,
    dnormed,
):
    feed_bwd_kernel(
        normed_ref, grad_ref, up_ref, down_ref, act_ref, slope_ref, dup_ref, ddown_ref, dnormed, dhid
    )

    @pl.when(pl.program_id(0) == 1)
    def _():
        norm_rows_back(
            resid_ref, norms_ref, 4, dother_ref, dnormed, dresid_ref, out_ref, drows_ref, dnorms_ref
        )


def embed_kernel(patches_ref, weight_ref, valid_ref, norms_ref, start_ref, normed_ref):
    start_ref[...] = dot(patches_ref[...], weight_ref[...]) * valid_ref[...]
    for f in range(FRAMES):
        rows = frame_rows(f)
        normed_ref[rows, :] = low(
            layer_norm(start_ref[rows, :], norms_ref[0:1, :], norms_ref[1:2, :])
        )


def embed_bwd_kernel(
    patches_ref, start_ref, valid_ref, drows_ref, da_ref, db_ref, norms_ref, dnorms_ref, out_ref, dstart
):
    dim = start_ref.shape[1]
    d_gain, d_bias = jnp.zeros((1, dim), SINGLE), jnp.zeros((1, dim), SINGLE)
    for f in range(FRAMES):
        rows = frame_rows(f)
        d_value, gain, bias = norm_back(
            start_ref[rows, :], norms_ref[0:1, :], da_ref[rows, :] + db_ref[rows, :]
        )
        dstart[rows, :] = low((drows_ref[rows, :].astype(SINGLE) + d_value) * valid_ref[rows, :])
        d_gain, d_bias = d_gain + gain, d_bias + bias
    out_ref[:, :dim] = low(dot(patches_ref[...], dstart[...], TN))
    padded = jnp.concatenate(
        [d_gain, d_bias, dnorms_ref[...], jnp.zeros((120, dim), SINGLE)], axis=0
    )
    out_ref[:, dim : dim + 128] = low(padded.T)


def enter_frame_kernel(start_ref, mixed_ref, weight_ref, norms_ref, out_ref, normed_ref):
    out_ref[...] = start_ref[...] + dot(mixed_ref[...], weight_ref[...], NT)
    for f in range(FRAMES):
        rows = frame_rows(f)
        normed_ref[rows, :] = low(
            layer_norm(out_ref[rows, :], norms_ref[2:3, :], norms_ref[3:4, :])
        )


def loss_kernel(
    dim,
    classes,
    proj,
    clip_ref,
    facts_ref,
    small_ref,
    resid_ref,
    valid_ref,
    norms_ref,
    loss_ref,
    dsmall_ref,
    pooled_ref,
    dresid_ref,
    drows_ref,
    dnorms_ref,
    dpool,
):
    facts = facts_ref[...]
    count = facts.shape[0]
    label, mate = (facts[:, dim + i : dim + i + 1].astype(jnp.int32) for i in range(2))
    pooled = low(facts[:, :dim] / facts[:, dim + 2 : dim + 3])
    pooled_ref[...] = pooled
    both = dot(pooled, small_ref[...])
    lane = lax.broadcasted_iota(jnp.int32, both.shape, 1)
    logits = jnp.where(lane < classes, both, -1e30)
    hot = (lane == label).astype(SINGLE)
    top = jnp.max(logits, axis=1, keepdims=True)
    raised = jnp.exp(logits - top)
    total = jnp.sum(raised, axis=1, keepdims=True)
    cross = top + jnp.log(total) - jnp.sum(both * hot, axis=1, keepdims=True)
    d_logits = raised / total - hot
    embedding = jnp.where((lane >= classes) & (lane < classes + proj), both, 0.0)
    inverse = lax.rsqrt(jnp.sum(embedding * embedding, axis=1, keepdims=True) + 1e-06)
    unit = embedding * inverse
    exact = functools.partial(
        lax.dot_general, precision=EXACT, preferred_element_type=SINGLE
    )
    similar = exact(unit, unit, NT) / TEMPER
    row = lax.broadcasted_iota(jnp.int32, (count, count), 0)
    col = lax.broadcasted_iota(jnp.int32, (count, count), 1)
    mate_hot = (col == mate).astype(SINGLE)
    masked = jnp.where(row == col, -1e30, similar)
    top = jnp.max(masked, axis=1, keepdims=True)
    raised = jnp.exp(masked - top)
    total = jnp.sum(raised, axis=1, keepdims=True)
    contrast = top + jnp.log(total) - jnp.sum(similar * mate_hot, axis=1, keepdims=True)
    loss_ref[...] = jnp.sum(cross + contrast, axis=0, keepdims=True)
    d_similar = (raised / total - mate_hot) / TEMPER
    d_unit = exact(d_similar, unit, NN) + exact(d_similar, unit, TN)
    d_embed = inverse * d_unit - embedding * (inverse * inverse * inverse) * jnp.sum(
        embedding * d_unit, axis=1, keepdims=True
    )
    dsmall_ref[...] = low(jnp.where(lane < classes, d_logits, d_embed))
    dpool[...] = dot(dsmall_ref[...], small_ref[...], NT) / facts[:, dim + 2 : dim + 3]
    d_pooled = dpool[pl.ds(clip_ref[0], 1), :]
    d_gain, d_bias = jnp.zeros((1, dim), SINGLE), jnp.zeros((1, dim), SINGLE)
    for f in range(FRAMES):
        rows = frame_rows(f)
        d_value, gain, bias = norm_back(
            resid_ref[rows, :], norms_ref[6:7, :], valid_ref[rows, :] * d_pooled
        )
        dresid_ref[rows, :] = d_value
        drows_ref[rows, :] = low(d_value)
        d_gain, d_bias = d_gain + gain, d_bias + bias
    dnorms_ref[0:1, :] = d_gain
    dnorms_ref[1:2, :] = d_bias


def adam_step(master, first, second, clipped, rate):
    first_new = BETA_ONE * first + (1.0 - BETA_ONE) * clipped
    second_new = BETA_TWO * second + (1.0 - BETA_TWO) * clipped * clipped
    first_hat = first_new / (1.0 - BETA_ONE**STEP)
    second_hat = second_new / (1.0 - BETA_TWO**STEP)
    master_new = master - rate * (first_hat / (jnp.sqrt(second_hat) + ADAM_EPS) + DECAY * master)
    return (master_new, first_new, second_new)


def adam_kernel(classes, proj, total_ref, *refs):
    masters, firsts, seconds, parts, outs = (
        refs[0:8], refs[8:16], refs[16:24], refs[24:30], refs[31:]
    )
    norm = jnp.sqrt(total_ref[...])
    refs[30][...] = norm
    factor = jnp.minimum(1.0, CLIP_AT / (norm + 1e-06))
    early, small, first, second, up, down = (ref[...] * factor for ref in parts)
    dim = masters[0].shape[1]
    columns = lambda k: slice(GROUP * k, GROUP * (k + 1))
    todo = [
        (0, ..., early[:, :dim]),
        (1, ..., early[:, dim : dim + 128].T[:8]),
        (2, ..., small[:, :classes]),
        (3, ..., small[:, classes : classes + proj]),
        (6, ..., up),
        (7, ..., down),
    ]
    for layer, grad in enumerate((first, second)):
        todo += [(4, (layer, k), grad[:, columns(k)]) for k in range(3)]
        todo.append((5, layer, grad[:, columns(3)].T))
    for i, at, grad in todo:
        results = adam_step(
            masters[i][at], firsts[i][at], seconds[i][at], grad, NORM_RATE if i == 1 else RATE
        )
        for j, result in enumerate(results):
            outs[3 * i + j][at] = result


def whole(shape):
    return pl.BlockSpec(shape, lambda g: (0,) * len(shape))


def per_group(rows, width):
    return pl.BlockSpec((1, rows, width), lambda g: (g, 0, 0))


def columns_of(width):
    return pl.BlockSpec((1, FRAMES, width, SLOTS), lambda g: (g, 0, 0, 0))


def shaped(*shape, dtype=SINGLE):
    return jax.ShapeDtypeStruct(shape, dtype)


def spec_of(value):
    shape = value.shape
    if len(shape) == 4:
        return columns_of(shape[2])
    return per_group(*shape[1:]) if len(shape) == 3 else whole(shape)


def call(kernel, name, inputs, outputs, scratch=(), gflops=1, steps=2, in_specs=None):
    return pl.pallas_call(
        kernel,
        grid=(steps,),
        in_specs=in_specs or [spec_of(value) for value in inputs],
        out_specs=[spec_of(value) for value in outputs],
        out_shape=list(outputs),
        scratch_shapes=[pltpu.VMEM(shape, dtype) for shape, dtype in scratch],
        compiler_params=pltpu.CompilerParams(vmem_limit_bytes=GRANT),
        cost_estimate=pl.CostEstimate(
            flops=gflops * 10**9, bytes_accessed=8 << 20, transcendentals=0
        ),
        name=name,
    )(*inputs)


def by_group(width, rows=ROWS):
    return shaped(2, rows, width, dtype=LOWER)


def temporal_forward(normed, weight):
    return call(
        temporal_fwd_kernel,
        "temporal_forward",
        (normed, weight),
        (shaped(2, FRAMES, QKV, SLOTS, dtype=LOWER), by_group(GROUP)),
        [((FRAMES, GROUP, SLOTS), LOWER)],
        15,
    )


def temporal_backward(normed, grad, weight, qkv, mixed):
    dim = normed.shape[1]
    return call(
        temporal_bwd_kernel,
        "temporal_backward",
        (normed, grad, weight, qkv, mixed),
        (by_group(dim, dim), shaped(ROWS, dim)),
        [((ROWS, QKV), LOWER), ((FRAMES, GROUP, SLOTS), LOWER), ((FRAMES, QKV, SLOTS), LOWER)],
        14,
    )


def spatial_forward(normed, weight, key_extra, last=None):
    dim = normed.shape[1]
    saved = (by_group(QKV), by_group(GROUP), by_group(GROUP))
    inputs = (normed, weight, key_extra)
    if last is None:
        return call(
            spatial_fwd_kernel, "spatial_forward", inputs, (*saved, shaped(ROWS, dim)), [], 15
        )
    return call(
        spatial_fwd_last_kernel,
        "spatial_forward",
        (*inputs, *last),
        (*saved, shaped(ROWS, dim), shaped(ROWS, dim, dtype=LOWER)),
        [((ROWS, dim), SINGLE)],
        15,
    )


def spatial_backward(normed, grad, weight, qkv, mixed, extra, key_extra, last=None):
    dim = normed.shape[1]
    inputs = (normed, grad, weight, qkv, mixed, extra, key_extra)
    scratch = [((ROWS, QKV), LOWER)]
    if last is None:
        outputs = (by_group(dim, dim), shaped(ROWS, dim))
        return call(spatial_bwd_kernel, "spatial_backward", inputs, outputs, scratch, 30)
    return call(
        spatial_bwd_last_kernel,
        "spatial_backward",
        (*inputs, *last),
        (by_group(dim, dim), shaped(ROWS, dim, dtype=LOWER), shaped(2, dim)),
        scratch + [((ROWS, dim), SINGLE)],
        30,
    )


def feed_specs(pair, rows):
    if rows % 16 != 0:
        pair = [value[:, :, :rows].reshape(2, 1, -1, value.shape[-1]) for value in pair]
        rows = pair[0].shape[2]
    block = (1, pair[0].shape[1], rows, pair[0].shape[3])
    return pair, [pl.BlockSpec(block, lambda g: (g, 0, 0, 0)) for _ in pair]


def feed_forward(normed, pair, rows, last=None):
    dim, width = normed.shape[1], pair[0].shape[3]
    pair, specs = feed_specs(pair, rows)
    inputs, saved = (normed, *pair), (by_group(width), by_group(width))
    specs = [spec_of(normed), *specs] + [spec_of(value) for value in last or ()]
    if last is None:
        return call(
            feed_fwd_kernel,
            "feed_forward",
            inputs,
            (*saved, shaped(ROWS, dim)),
            [],
            10,
            in_specs=specs,
        )
    return call(
        feed_fwd_last_kernel,
        "feed_forward",
        (*inputs, *last),
        (*saved, shaped(ROWS, dim), shaped(1, dim)),
        [((ROWS, dim), SINGLE)],
        10,
        in_specs=specs,
    )


def feed_backward(normed, grad, pair, rows, act, slope, last=None):
    dim, width = normed.shape[1], pair[0].shape[3]
    pair, specs = feed_specs(pair, rows)
    inputs = (normed, grad, *pair, act, slope)
    specs = [spec_of(normed), spec_of(grad), *specs, spec_of(act), spec_of(slope)]
    specs += [spec_of(value) for value in last or ()]
    weights = (by_group(width, dim), by_group(width, dim))
    scratch = [((ROWS, width), LOWER)]
    if last is None:
        outputs = (*weights, shaped(ROWS, dim))
        return call(
            feed_bwd_kernel, "feed_backward", inputs, outputs, scratch, 15, in_specs=specs
        )
    return call(
        feed_bwd_last_kernel,
        "feed_backward",
        (*inputs, *last),
        (*weights, shaped(ROWS, dim), shaped(ROWS, dim, dtype=LOWER), shaped(2, dim)),
        scratch + [((ROWS, dim), SINGLE)],
        15,
        in_specs=specs,
    )


def embed(patches, weight, valid, norms):
    dim = patches.shape[1]
    outputs = (shaped(ROWS, dim), shaped(ROWS, dim, dtype=LOWER))
    return call(embed_kernel, "embed", (patches, weight, valid, norms), outputs, (), 15, 1)


def embed_backward(patches, start, valid, d_rows, d_a, d_b, norms, d_norms):
    dim = patches.shape[1]
    return call(
        embed_bwd_kernel,
        "embed_backward",
        (patches, start, valid, d_rows, d_a, d_b, norms, d_norms),
        (shaped(dim, dim + 128, dtype=LOWER),),
        [((ROWS, dim), LOWER)],
        30,
        1,
    )[0]


def enter_frame(start, mixed, weight, norms):
    dim = start.shape[1]
    return call(
        enter_frame_kernel,
        "enter_frame",
        (start, mixed, weight, norms),
        (shaped(ROWS, dim), shaped(ROWS, dim, dtype=LOWER)),
        [],
        2,
        1,
    )


def all_losses(clip, facts, small, resid, valid, norms, classes, proj):
    count, dim = facts.shape[0], resid.shape[1]
    inputs = (facts, small, resid, valid, norms)
    return call(
        functools.partial(loss_kernel, dim, classes, proj),
        "losses",
        (clip, *inputs),
        (
            shaped(1, 1),
            shaped(count, dim, dtype=LOWER),
            shaped(count, dim, dtype=LOWER),
            shaped(ROWS, dim),
            shaped(ROWS, dim, dtype=LOWER),
            shaped(2, dim),
        ),
        [((count, dim), SINGLE)],
        1,
        1,
        [pl.BlockSpec(memory_space=pltpu.SMEM)] + [whole(value.shape) for value in inputs],
    )


def optimizer(total, masters, firsts, seconds, parts, classes, proj):
    inputs = (total, *masters, *firsts, *seconds, *parts)
    outputs = [shaped(1, 1)] + [shaped(*value.shape) for value in masters for _ in range(3)]
    return pl.pallas_call(
        functools.partial(adam_kernel, classes, proj),
        grid=(1,),
        in_specs=[whole(value.shape) for value in inputs],
        out_specs=[whole(value.shape) for value in outputs],
        out_shape=outputs,
        compiler_params=pltpu.CompilerParams(vmem_limit_bytes=GRANT),
        name="optimizer",
    )(*inputs)


def pace_kernel(token_ref, out_ref):
    out_ref[...] = token_ref[...]


def pace(token):
    return call(pace_kernel, "pace", (token,), (shaped(*token.shape),), (), 30, 1)[0]


def tick(*values):
    return lax.optimization_barrier(values)


def summed(terms):
    return functools.reduce(jnp.add, (term.astype(SINGLE) for term in terms))


class Cube:
    def __init__(self, sizes):
        self.count = sizes["batch"] * sizes["head"]
        self.mine = lax.axis_index(ALL)
        batch_bits = sizes["batch"].bit_length() - 1
        self.batch_masks = [4 << k for k in reversed(range(batch_bits))]

    def swap(self, value, mask):
        return lax.ppermute(value, ALL, [(i, i ^ mask) for i in range(self.count)])

    def has(self, mask):
        return (self.mine & mask) != 0

    def join(self, value, *masks):
        for mask in masks:
            value = self.merge(value, self.swap(value, mask), mask)
        return value

    def fork(self, value):
        return self.stack(value, self.swap(value, 2), 2)

    def step(self, token, sends, late=()):
        values = [value for value, _ in (*sends, *late)]
        *values, token = tick(*values, token)
        masks = [mask for _, mask in (*sends, *late)]
        received = [self.swap(value, mask) for value, mask in zip(values, masks)]
        count = len(sends)
        *ended, token = tick(*received[:count], pace(token))
        return token, *ended, *received[count:]

    def merge(self, value, other, mask):
        has = self.has(mask)
        both = jnp.stack([jnp.where(has, other, value), jnp.where(has, value, other)], axis=-3)
        shape = value.shape
        return both.reshape(*shape[:-3], 2 * shape[-3], *shape[-2:])

    def stack(self, value, other, mask):
        has = self.has(mask)
        return jnp.stack([jnp.where(has, other, value), jnp.where(has, value, other)])


    def cut(self, terms, mask):
        shape = terms[0].shape
        mine = self.has(mask).astype(jnp.int32)
        pairs = [
            term.reshape(*shape[:-3], shape[-3] // 2, 2, *shape[-2:]) for term in terms
        ]
        half = lambda pair, which: lax.dynamic_index_in_dim(pair, which, pair.ndim - 3, False)
        return low(summed([half(pair, 1 - mine) for pair in pairs])), [
            half(pair, mine) for pair in pairs
        ]

    def shed(self, terms, *masks):
        for mask in masks:
            send, keep = self.cut(terms, mask)
            terms = keep + [self.swap(send, mask)]
        return terms

    def cut_row(self, terms):
        mine = self.has(2).astype(jnp.int32)
        half = lambda term, which: lax.dynamic_index_in_dim(term, which, 0, False)
        return low(summed([half(term, 1 - mine) for term in terms])), [
            half(term, mine) for term in terms
        ]

    def meet(self, terms):
        send, keep = self.cut_row(terms)
        return keep + [self.swap(send, 2)]

    def total(self, value):
        for mask in [1, 2] + self.batch_masks[::-1]:
            value = value + self.swap(value, mask)
        return value

    def swap_frames(self, parts):
        return [parts[0]] + [self.swap(parts[r], r) for r in range(1, FRAMES)]


def body(sizes, *args):
    patches, bucket, labels, partner = args[:4]
    views = [lambda v: v] * 4 + [
        lambda v: v.transpose(0, 2, 1, 3), lambda v: v, lambda v: v, lambda v: v.T
    ]
    masters, firsts, seconds = (
        [view(value) for view, value in zip(views, args[4 + 8 * i : 12 + 8 * i])] for i in range(3)
    )
    patch_weight, norm_params, head_weight, proj_weight, attn_in, attn_out, up, down = masters
    cube = Cube(sizes)
    dim = norm_params.shape[1] * cube.count
    classes, proj = head_weight.shape[1], proj_weight.shape[1]
    rows_wide, rows_small = attn_in.shape[2], patch_weight.shape[0]
    place = lax.axis_index(HEAD)

    *first, near, last = cube.batch_masks
    middle = dim // 2
    flat = lambda value: value.reshape(2, dim, -1)
    blocked = lambda value: value.reshape(*value.shape[:-2], -1, rows_wide, value.shape[-1])
    pack = lambda w_in, w_out: jnp.concatenate(
        [low(w_in[0]), low(w_in[1]), low(w_in[2]), low(w_out).T], axis=1
    )[None]
    patch_count = jnp.where(bucket == 1, PMAX, PSMALL)
    offset = jnp.arange(SLOTS)[None, :]
    number = (place ^ jnp.arange(FRAMES))[:, None]
    frame_valid = ((number * SLOTS + offset) < patch_count).reshape(ROWS, 1).astype(SINGLE)
    slot_valid = (jnp.broadcast_to(place * SLOTS + offset, (FRAMES, SLOTS)) < patch_count).reshape(
        ROWS, 1
    ).astype(SINGLE)
    lane = jnp.arange(HD)[None, :]
    key_extra = low(
        jnp.where(lane == 0, jnp.where(frame_valid > 0, 0.0, -1e30), (lane < 4).astype(SINGLE))
    )

    extra = -(-(rows_small + 1) // 16) * 16
    norm_row = low(norm_params).reshape(1, -1)
    first_w = jnp.concatenate(
        [
            pack(attn_in[0], attn_out[0])[0],
            low(patch_weight),
            jnp.pad(norm_row, ((0, extra - rows_small - 1), (0, dim - norm_row.shape[1]))),
        ]
    )[None]
    token = jnp.zeros((8, 128), SINGLE)
    clip, w_in, w_out, w_up, w_down = patches[0], attn_in[1], attn_out[1], up, down
    for mask in first:
        first_w, clip, w_in, w_out, w_up, w_down = tick(first_w, clip, w_in, w_out, w_up, w_down)
        token, other = cube.step(token, [(first_w, mask)])
        first_w = cube.merge(first_w, other, mask)
    blocks = jnp.pad(clip, ((0, ROWS - PMAX), (0, 0))).reshape(FRAMES, SLOTS, -1)
    blocks = jnp.where((place & 1) != 0, blocks[jnp.array([1, 0, 3, 2])], blocks)
    blocks = jnp.where((place & 2) != 0, blocks[jnp.array([2, 3, 0, 1])], blocks)
    second_w = jnp.concatenate([pack(w_in, w_out)[0], low(w_up)])[None]
    small = jnp.concatenate([low(head_weight), low(proj_weight)], axis=1)
    small = jnp.pad(small, ((0, -rows_small % 16), (0, dim - small.shape[1])))
    down_w = jnp.concatenate([low(w_down), small])[None]

    token, other, *slots = cube.step(
        token, [(first_w, near)] + [(blocks[r], r) for r in range(1, FRAMES)]
    )
    first_w = cube.merge(first_w, other, near)
    by_frame = blocks.reshape(ROWS, -1)

    left, right = first_w[..., :middle], first_w[..., middle:]
    token, other_left, other_right, other = cube.step(
        token, [(left, last), (right, 2), (second_w, first[0])]
    )
    left, right = cube.merge(left, other_left, last), cube.stack(right, other_right, 2)
    second_w = cube.join(cube.merge(second_w, other, first[0]), *first[1:])

    left, right, second_w, *slots = tick(left, right, second_w, *slots)
    by_slot = jnp.concatenate([blocks[0], *slots])
    token, other_left, other_right, other = cube.step(
        token, [(left, 2), (right, last), (second_w, near)]
    )
    by_slot, slot_valid, token = tick(by_slot, slot_valid, token)
    left, right = cube.stack(left, other_left, 2), cube.merge(right, other_right, last)
    joined = lambda at: jnp.concatenate([left[:, :, at], right[:, :, at]], axis=-1)
    own_first, early = flat(joined(slice(0, rows_wide))), joined(slice(rows_wide, None))

    early, own_first, other = tick(early, own_first, other)
    second_w = cube.merge(second_w, other, near)
    second_w, up_w = second_w[..., :rows_wide, :], second_w[..., rows_wide:, :]
    token, other, other_first, other_left, other_right, other_up = cube.step(
        token,
        [(early, 1)],
        [
            (own_first, 1),
            (second_w[..., :middle], last),
            (second_w[..., middle:], 2),
            (up_w, 2),
        ],
    )
    early = cube.stack(early, other, 1).transpose(2, 1, 0, 3, 4)
    patch_copy = early[..., :rows_small, :].reshape(dim, dim)
    norms = early[..., rows_small, : norm_row.shape[1]].reshape(-1, 8, rows_small)
    norms = norms.transpose(1, 0, 2).reshape(8, dim).astype(SINGLE)
    start_slot, normed_t = embed(by_slot, patch_copy, slot_valid, norms)
    start_slot, normed_t, other_left, other_right, down_w = tick(
        start_slot, normed_t, other_left, other_right, down_w
    )
    left = cube.fork(cube.merge(second_w[..., :middle], other_left, last))
    right = cube.join(cube.stack(second_w[..., middle:], other_right, 2), last)
    down_w = cube.join(down_w, *first)
    qkv_t, mixed_t = [None, None], [None, None]
    qkv_t[0], mixed_t[0] = temporal_forward(normed_t, own_first)
    mixed_t[0], normed_t, other_first, patch_copy, other_up, down_w = tick(
        mixed_t[0], normed_t, other_first, patch_copy, other_up, down_w
    )
    own_up = cube.join(cube.stack(up_w, other_up, 2), last)
    down_w = cube.join(down_w, near)
    pair = (own_first, other_first)
    out_first = jnp.concatenate([pair[c][y][:, QKV:] for c in range(2) for y in range(2)], axis=1)
    start_frame = dot(by_frame, patch_copy) * frame_valid
    qkv_t[1], mixed_t[1] = temporal_forward(normed_t, other_first)
    parts = [
        jnp.concatenate(
            [mixed_t[c ^ (r & 1)][y][frame_rows(r)] for c in range(2) for y in range(2)], axis=1
        )
        for r in range(FRAMES)
    ]
    own_second = jnp.concatenate([flat(left), flat(right)], axis=-1)

    parts[0], out_first, start_frame, token = tick(parts[0], out_first, start_frame, token)
    token, *received = cube.step(token, [(parts[r], r) for r in range(1, FRAMES)])
    mixed_frame = jnp.concatenate([parts[0], *received])
    mixed_frame, own_second, key_extra, down_w = tick(mixed_frame, own_second, key_extra, down_w)

    resid_one, normed_s = enter_frame(start_frame, mixed_frame, out_first, norms)
    other_second = cube.swap(own_second, 1)
    left, right = cube.join(down_w[..., :middle], last), cube.fork(down_w[..., middle:])
    qkv_s, mixed_s, extra_s = ([None, None] for _ in range(3))
    qkv_s[0], mixed_s[0], extra_s[0], branch = spatial_forward(normed_s, own_second, key_extra)
    branch, normed_s, other_second, own_up, left, right = tick(
        branch, normed_s, other_second, own_up, left, right
    )
    other_up = cube.swap(own_up, 1)
    left, right = cube.fork(left), cube.join(right, last)
    qkv_s[1], mixed_s[1], extra_s[1], resid_two, normed_m = spatial_forward(
        normed_s, other_second, key_extra, (resid_one, branch, norms)
    )
    own_down = jnp.concatenate([left, right], axis=-1)
    normed_m, own_down, other_up = tick(normed_m, own_down, other_up)

    other_down = cube.swap(own_down, 1)
    own_pair, other_pair = (own_up, own_down), (other_up, other_down)
    act, slope = ([None, None] for _ in range(2))
    act[0], slope[0], branch = feed_forward(normed_m, own_pair, rows_wide)
    act[1], slope[1], resid_three, sums = feed_forward(
        normed_m, other_pair, rows_wide, (resid_two, branch, norms, frame_valid)
    )
    small = slice(rows_wide, rows_wide + rows_small)
    small = cube.stack(own_down[:, :, small], other_down[:, :, small], 1)
    small = small.transpose(2, 1, 0, 3, 4).reshape(dim, dim)

    for mask in (1, 2):
        sums = sums + cube.swap(sums, mask)
    facts = jnp.stack([labels[0], partner[0], FRAMES * patch_count[0]]).astype(SINGLE)
    gathered = jnp.concatenate([sums, jnp.pad(facts, (0, 125))[None]], axis=1)[None]
    gathered = cube.join(gathered, *cube.batch_masks)[:, 0]
    clip = lax.axis_index("batch").reshape(1)
    loss_sum, d_small, pooled_low, d_resid, d_rows, d_norms_f = all_losses(
        clip, gathered, small, resid_three, frame_valid, norms, classes, proj
    )

    d_up, d_down = [None, None], [None, None]
    d_up[1], d_down[1], d_normed = feed_backward(
        normed_m, d_rows, other_pair, rows_wide, act[1], slope[1]
    )
    up_other, down_other, d_normed, d_rows, normed_m = tick(
        d_up[1], d_down[1], d_normed, d_rows, normed_m
    )
    core_up, core_down = cube.swap(up_other, 1), cube.swap(down_other, 1)
    d_up[0], d_down[0], d_resid, d_rows, d_norms_m = feed_backward(
        normed_m,
        d_rows,
        own_pair,
        rows_wide,
        act[0],
        slope[0],
        (resid_two, d_resid, d_normed, norms),
    )
    d_resid, d_rows, up_own, down_own, core_up, core_down = tick(
        d_resid, d_rows, d_up[0], d_down[0], core_up, core_down
    )

    sum_up = cube.meet([blocked(up_own), blocked(core_up)])
    sum_down = cube.shed([blocked(down_own), blocked(core_down)], last)
    d_second = [None, None]
    d_second[1], d_normed = spatial_backward(
        normed_s, d_rows, other_second, qkv_s[1], mixed_s[1], extra_s[1], key_extra
    )
    d_small = lax.dynamic_slice_in_dim(
        dot(pooled_low, d_small, TN), cube.mine * rows_small, rows_small, 0
    )
    second_other, d_normed, d_rows, normed_s, sum_up[-1], sum_down[-1], d_small = tick(
        d_second[1], d_normed, d_rows, normed_s, sum_up[-1], sum_down[-1], d_small
    )
    core_second = cube.swap(second_other, 1)
    sum_up, sum_down = cube.shed(sum_up, last), cube.meet(sum_down)
    d_second[0], d_rows, d_norms_s = spatial_backward(
        normed_s,
        d_rows,
        own_second,
        qkv_s[0],
        mixed_s[0],
        extra_s[0],
        key_extra,
        (resid_one, d_resid, d_normed, norms),
    )
    d_rows, second_own, sum_up[-1], sum_down[-1], core_second = tick(
        d_rows, d_second[0], sum_up[-1], sum_down[-1], core_second
    )

    parts = split_frames(d_rows)
    send, sum_second = cube.cut([blocked(second_own), blocked(core_second)], last)
    token, *received, other = cube.step(
        token, [(parts[r], r) for r in range(1, FRAMES)], [(send, last)]
    )
    d_rows = jnp.concatenate([parts[0], *received])
    sum_second.append(other)

    sum_up, sum_down = cube.shed(sum_up, near), cube.shed(sum_down, near)
    d_first, d_normed = [None, None], [None, None]
    d_first[1], d_normed[1] = temporal_backward(
        normed_t, d_rows, other_first, qkv_t[1], mixed_t[1]
    )
    first_other, d_normed[1], d_rows, normed_t, sum_up[-1], sum_down[-1], sum_second[-1] = tick(
        d_first[1], d_normed[1], d_rows, normed_t, sum_up[-1], sum_down[-1], sum_second[-1]
    )
    core_first = cube.swap(first_other, 1)
    sum_second = cube.meet(sum_second)
    sum_up, sum_down = cube.shed(sum_up, *first[::-1]), cube.shed(sum_down, *first[::-1])
    d_first[0], d_normed[0] = temporal_backward(
        normed_t, d_rows, own_first, qkv_t[0], mixed_t[0]
    )
    d_rows, first_own, d_normed[0], core_first, sum_second[-1], sum_up[-1], sum_down[-1] = tick(
        d_rows, d_first[0], d_normed[0], core_first, sum_second[-1], sum_up[-1], sum_down[-1]
    )

    sum_first = [blocked(first_own), blocked(core_first)]
    send_left, left = cube.cut_row([term[..., :middle] for term in sum_first])
    send_right, right = cube.cut([term[..., middle:] for term in sum_first], last)
    send_second, sum_second = cube.cut(sum_second, near)
    send_left, send_right, send_second, d_normed[0] = tick(
        send_left, send_right, send_second, d_normed[0]
    )
    other_left, other_right, other_second = (
        cube.swap(send_left, 2), cube.swap(send_right, last), cube.swap(send_second, near)
    )
    d_norms = jnp.concatenate([d_norms_s, d_norms_m, d_norms_f])
    d_early = embed_backward(
        by_slot, start_slot, slot_valid, d_rows, d_normed[0], d_normed[1], norms, d_norms
    )
    send, sum_early = cube.cut([d_early.reshape(-1, rows_small, dim + 128)], 1)
    other_left, other_right, other_second, send, token = tick(
        other_left, other_right, other_second, send, token
    )
    other = cube.swap(send, 1)
    left.append(other_left)
    right.append(other_right)
    sum_second.append(other_second)
    sum_early.append(other)

    send_left, left = cube.cut(left, last)
    send_right, right = cube.cut_row(right)
    send_second, sum_second = cube.cut(sum_second, first[-1])
    send, sum_early = cube.cut(sum_early, 2)
    token, other_left, other_right, other_second, other = cube.step(
        token, [(send_left, last), (send_right, 2), (send_second, first[-1]), (send, 2)]
    )
    sum_first = [jnp.concatenate([summed(left + [other_left]), summed(right + [other_right])], -1)]
    sum_second.append(other_second)
    sum_early.append(other)

    send_first, sum_first = cube.cut(sum_first, near)
    send, sum_early = cube.cut(sum_early, last)
    token, other_first, other = cube.step(token, [(send_first, near), (send, last)])
    sum_first.append(other_first)
    sum_early.append(other)

    send_first, sum_first = cube.cut(sum_first, first[-1])
    send, sum_early = cube.cut(sum_early, near)
    ready, up_last, down_last = tick(send_first, sum_up[-1], sum_down[-1])
    sum_up[-1], sum_down[-1] = up_last, down_last
    square = lambda value: jnp.sum(value * value)
    d_up, d_down = summed(sum_up)[0], summed(sum_down)[0]
    d_second = summed(cube.shed(sum_second, *first[-2::-1]))[0]
    squares = square(d_small) + square(d_up) + square(d_down) + square(d_second)
    token, other_first, other = cube.step(token, [(ready, first[-1]), (send, near)])
    sum_first.append(other_first)
    sum_early.append(other)
    sum_first = cube.shed(sum_first, *first[-2::-1])
    sum_early = cube.shed(sum_early, *first[::-1])
    d_first, d_early = summed(sum_first)[0], summed(sum_early)[0]

    total = cube.total((squares + square(d_first) + square(d_early)).reshape(1, 1))
    parts = (d_early, d_small, d_first, d_second, d_up, d_down)
    grad_norm, *updates = optimizer(total, masters, firsts, seconds, parts, classes, proj)
    updates = [views[i // 3](update) for i, update in enumerate(updates)]
    return (loss_sum[0, 0], grad_norm[0, 0], *updates)


def solution(mesh):
    sizes = dict(mesh.shape)
    split = Mesh(mesh.devices.reshape(sizes["batch"], 2, sizes["head"] // 2), ALL)
    placed = (
        P("batch", HEAD, None),
        P("batch"),
        P("batch"),
        P("batch"),
        P(ALL, None),
        P(None, ALL),
        P(ALL, None),
        P(ALL, None),
        P(None, "batch", None, HEAD),
        P(None, HEAD, "batch"),
        P("batch", HEAD),
        P(HEAD, "batch"),
        P(ALL, None),
        P(None, ALL),
        P(ALL, None),
        P(ALL, None),
        P(None, "batch", None, HEAD),
        P(None, HEAD, "batch"),
        P("batch", HEAD),
        P(HEAD, "batch"),
        P(ALL, None),
        P(None, ALL),
        P(ALL, None),
        P(ALL, None),
        P(None, "batch", None, HEAD),
        P(None, HEAD, "batch"),
        P("batch", HEAD),
        P(HEAD, "batch"),
    )
    return jax.shard_map(
        functools.partial(body, sizes),
        mesh=split,
        in_specs=placed,
        out_specs=(
            P(),
            P(),
            P(ALL, None),
            P(ALL, None),
            P(ALL, None),
            P(None, ALL),
            P(None, ALL),
            P(None, ALL),
            P(ALL, None),
            P(ALL, None),
            P(ALL, None),
            P(ALL, None),
            P(ALL, None),
            P(ALL, None),
            P(None, "batch", None, HEAD),
            P(None, "batch", None, HEAD),
            P(None, "batch", None, HEAD),
            P(None, HEAD, "batch"),
            P(None, HEAD, "batch"),
            P(None, HEAD, "batch"),
            P("batch", HEAD),
            P("batch", HEAD),
            P("batch", HEAD),
            P(HEAD, "batch"),
            P(HEAD, "batch"),
            P(HEAD, "batch"),
        ),
        check_vma=False,
    )
```

```python
import functools

import jax
import jax.numpy as jnp
from jax import lax
from jax.experimental import pallas as pl
from jax.experimental.pallas import tpu as pltpu
from jax.sharding import Mesh
from jax.sharding import PartitionSpec as P

HD = 64
FRAMES = 4
PMAX = 784
PSMALL = 196
STEP = 5
SLOTS = 208
ROWS = FRAMES * SLOTS
GROUP = 192
QKV = 3 * GROUP


EXACT = lax.Precision.HIGHEST
TEMPER = 0.05
BETA_ONE = 0.5
BETA_TWO = 0.5
RATE = 0.04
NORM_RATE = 0.3
DECAY = 0.05
ADAM_EPS = 1e-08
CLIP_AT = 1.0
LOWER = jnp.bfloat16
SINGLE = jnp.float32
ALL = ("batch", "row", "core")
HEAD = ("row", "core")
GRANT = 56 << 20

NN = (((1,), (0,)), ((), ()))
NT = (((1,), (1,)), ((), ()))
TN = (((0,), (0,)), ((), ()))


def dot(left, right, dims=NN):
    return lax.dot_general(left, right, dims, preferred_element_type=SINGLE)


def low(value):
    return value.astype(LOWER)


def layer_norm(value, gain, bias):
    center = value - jnp.mean(value, axis=-1, keepdims=True)
    spread = jnp.mean(center * center, axis=-1, keepdims=True)
    return center * lax.rsqrt(spread + 1e-06) * gain + bias


def wide(*refs):
    return jnp.concatenate([ref[0].reshape(-1, ref.shape[-1]) for ref in refs], axis=1)


def three_parts(value):
    high = low(value)
    rest = value - high.astype(SINGLE)
    middle = low(rest)
    return high, middle, low(rest - middle.astype(SINGLE))


def frame_probs(query, keys):
    scores = [jnp.sum(query * key, axis=0, keepdims=True) * HD ** (-0.5) for key in keys]
    top = functools.reduce(jnp.maximum, scores)
    raised = [jnp.exp(score - top) for score in scores]
    total = functools.reduce(jnp.add, raised)
    return [value / total for value in raised]


def rounded(value):
    return low(value).astype(SINGLE)


def frame_rows(f):
    return slice(SLOTS * f, SLOTS * (f + 1))


def split_frames(rows):
    return [rows[frame_rows(f)] for f in range(FRAMES)]


def head_features(which, head):
    return slice(GROUP * which + HD * head, GROUP * which + HD * (head + 1))


def temporal_fwd_kernel(
    normed_ref, own_left, own_right, other_left, other_right, qkv_ref, mixed_ref, out, left, right
):
    for chosen, parts in (
        (pl.program_id(0) < 2, (own_left, own_right)),
        (pl.program_id(0) >= 2, (other_left, other_right)),
    ):

        @pl.when(chosen)
        def _(parts=parts):
            left[...], right[...] = wide(parts[0]), wide(parts[1])

    for f in range(FRAMES):
        rows = normed_ref[frame_rows(f), :]
        qkv_ref[0, f, : 2 * GROUP, :] = low(dot(rows, left[...])).T
        qkv_ref[0, f, 2 * GROUP :, :] = low(dot(rows, right[:, :GROUP])).T
    for head in range(GROUP // HD):
        query, keys, values = (
            [qkv_ref[0, f, head_features(i, head), :].astype(SINGLE) for f in range(FRAMES)]
            for i in range(3)
        )
        for f in range(FRAMES):
            probs = frame_probs(query[f], keys)
            mixed = sum(rounded(prob) * value for prob, value in zip(probs, values))
            out[f, head_features(0, head), :] = low(mixed)
    for f in range(FRAMES):
        mixed_ref[0, frame_rows(f), :] = out[f].T


def temporal_bwd_kernel(
    normed_ref,
    grad_ref,
    left_ref,
    right_ref,
    qkv_ref,
    mixed_ref,
    dweight_ref,
    dnormed_ref,
    dqkv,
    dmix,
    dcol,
):
    scale = HD ** (-0.5)
    for f in range(FRAMES):
        dmix[f] = low(dot(grad_ref[frame_rows(f), :], wide(right_ref)[:, GROUP:])).T
    for head in range(GROUP // HD):
        query, keys, values = (
            [qkv_ref[0, f, head_features(i, head), :].astype(SINGLE) for f in range(FRAMES)]
            for i in range(3)
        )
        d_keys = [jnp.zeros((HD, SLOTS), SINGLE) for _ in range(FRAMES)]
        d_values = [jnp.zeros((HD, SLOTS), SINGLE) for _ in range(FRAMES)]
        for f in range(FRAMES):
            d_mixed = dmix[f, head_features(0, head), :].astype(SINGLE)
            probs = frame_probs(query[f], keys)
            d_probs = [jnp.sum(d_mixed * value, axis=0, keepdims=True) for value in values]
            row = sum(prob * d_prob for prob, d_prob in zip(probs, d_probs))
            d_query = jnp.zeros((HD, SLOTS), SINGLE)
            for g in range(FRAMES):
                d_score = rounded(probs[g] * (d_probs[g] - row))
                d_query = d_query + d_score * keys[g]
                d_keys[g] = d_keys[g] + d_score * query[f]
                d_values[g] = d_values[g] + rounded(probs[g]) * d_mixed
            dcol[f, head_features(0, head), :] = low(d_query * scale)
        for g in range(FRAMES):
            dcol[g, head_features(1, head), :] = low(d_keys[g] * scale)
            dcol[g, head_features(2, head), :] = low(d_values[g])
    for f in range(FRAMES):
        dqkv[frame_rows(f), :] = dcol[f].T
    finish_backward(normed_ref, grad_ref, left_ref, right_ref, mixed_ref, dweight_ref, dnormed_ref, dqkv)


def finish_backward(
    normed_ref, grad_ref, left_ref, right_ref, mixed_ref, dweight_ref, dnormed_ref, dqkv
):
    dweight_ref[0, :, :QKV] = low(dot(normed_ref[...], dqkv[...], TN))
    dweight_ref[0, :, QKV:] = low(dot(grad_ref[...], mixed_ref[0], TN))
    d_normed = dot(dqkv[:, : 2 * GROUP], wide(left_ref), NT) + dot(
        dqkv[:, 2 * GROUP :], wide(right_ref)[:, :GROUP], NT
    )

    accumulate(dnormed_ref, d_normed)


def lane_pieces(pieces, rows):
    lane = lax.broadcasted_iota(jnp.int32, (rows, HD), 1)
    result = jnp.zeros((rows, HD), SINGLE)
    for number, piece in enumerate(pieces):
        result = jnp.where(lane == number, piece.astype(SINGLE), result)
    return low(result)


def spatial_fwd_kernel(
    normed_ref, left_ref, right_ref, key_extra_ref, qkv_ref, mixed_ref, extra_ref, branch_ref
):
    qkv_ref[0, :, : 2 * GROUP] = low(dot(normed_ref[...], wide(left_ref)))
    qkv_ref[0, :, 2 * GROUP :] = low(dot(normed_ref[...], wide(right_ref)[:, :GROUP]))
    one = jnp.ones((ROWS, 1), SINGLE)
    for head in range(GROUP // HD):
        at = HD * head
        query = qkv_ref[0, :, at : at + HD] * jnp.asarray(HD ** (-0.5), LOWER)
        query = jnp.concatenate([query, lane_pieces([one], ROWS)], axis=1)
        keys = jnp.concatenate(
            [qkv_ref[0, :, GROUP + at : GROUP + at + HD], key_extra_ref[...]], axis=1
        )
        values = jnp.concatenate(
            [qkv_ref[0, :, 2 * GROUP + at : 2 * GROUP + at + HD], lane_pieces([one], ROWS)], axis=1
        )
        score = dot(query, keys, NT)
        top = jnp.max(score, axis=1, keepdims=True)
        mixed = dot(low(jnp.exp(score - top)), values)
        total = mixed[:, HD : HD + 1]
        mixed_ref[0, :, at : at + HD] = low(mixed[:, :HD] / total)
        logsum = -(top + jnp.log(total))
        extra_ref[0, :, at : at + HD] = lane_pieces([one, *three_parts(logsum)], ROWS)
    branch = dot(mixed_ref[0], wide(right_ref)[:, GROUP:], NT)

    accumulate(branch_ref, branch)


def spatial_fwd_last_kernel(
    normed_ref,
    left_ref,
    right_ref,
    key_extra_ref,
    resid_ref,
    branch_ref,
    norms_ref,
    qkv_ref,
    mixed_ref,
    extra_ref,
    out_ref,
    out_normed_ref,
    branch,
):
    spatial_fwd_kernel(
        normed_ref, left_ref, right_ref, key_extra_ref, qkv_ref, mixed_ref, extra_ref, branch
    )

    @pl.when(pl.program_id(0) == 1)
    def _():
        for f in range(FRAMES):
            rows = frame_rows(f)
            value = resid_ref[rows, :] + (branch_ref[rows, :] + branch[rows, :])
            out_ref[rows, :] = value
            out_normed_ref[rows, :] = low(layer_norm(value, norms_ref[4:5, :], norms_ref[5:6, :]))


def spatial_bwd_kernel(
    normed_ref,
    grad_ref,
    left_ref,
    right_ref,
    qkv_ref,
    mixed_ref,
    extra_ref,
    key_extra_ref,
    dweight_ref,
    dnormed_ref,
    dqkv,
):
    scale = HD ** (-0.5)
    d_mixed_all = low(dot(grad_ref[...], wide(right_ref)[:, GROUP:]))
    one = jnp.ones((ROWS, 1), SINGLE)
    for head in range(GROUP // HD):
        at = HD * head
        query = qkv_ref[0, :, at : at + HD]
        query_long = jnp.concatenate(
            [query * jnp.asarray(scale, LOWER), extra_ref[0, :, at : at + HD]], axis=1
        )
        d_mixed = d_mixed_all[:, at : at + HD]
        delta = -jnp.sum(
            d_mixed.astype(SINGLE) * mixed_ref[0, :, at : at + HD].astype(SINGLE),
            axis=1,
            keepdims=True,
        )
        d_mixed_long = jnp.concatenate([d_mixed, lane_pieces(three_parts(delta), ROWS)], axis=1)
        d_query = jnp.zeros((ROWS, HD), SINGLE)
        for part in range(FRAMES):
            rows = slice(SLOTS * part, SLOTS * (part + 1))
            keys = qkv_ref[0, rows, GROUP + at : GROUP + at + HD]
            values = qkv_ref[0, rows, 2 * GROUP + at : 2 * GROUP + at + HD]
            keys_long = jnp.concatenate([keys, key_extra_ref[rows, :]], axis=1)
            values_long = jnp.concatenate(
                [values, lane_pieces([one[rows]] * 3, SLOTS)], axis=1
            )
            prob = jnp.exp(dot(keys_long, query_long, NT))
            d_score = low(prob * dot(values_long, d_mixed_long, NT))
            dqkv[rows, 2 * GROUP + at : 2 * GROUP + at + HD] = low(dot(low(prob), d_mixed))
            dqkv[rows, GROUP + at : GROUP + at + HD] = low(dot(d_score, query) * scale)
            d_query = d_query + dot(d_score, keys, TN)
        dqkv[:, at : at + HD] = low(d_query * scale)
    finish_backward(normed_ref, grad_ref, left_ref, right_ref, mixed_ref, dweight_ref, dnormed_ref, dqkv)


def spatial_bwd_last_kernel(
    normed_ref,
    grad_ref,
    left_ref,
    right_ref,
    qkv_ref,
    mixed_ref,
    extra_ref,
    key_extra_ref,
    resid_ref,
    dresid_ref,
    dother_ref,
    norms_ref,
    dweight_ref,
    drows_ref,
    dnorms_ref,
    dqkv,
    dnormed,
):
    spatial_bwd_kernel(
        normed_ref,
        grad_ref,
        left_ref,
    right_ref,
        qkv_ref,
        mixed_ref,
        extra_ref,
        key_extra_ref,
        dweight_ref,
        dnormed,
        dqkv,
    )

    @pl.when(pl.program_id(0) == 1)
    def _():
        norm_rows_back(
            resid_ref, norms_ref, 2, dother_ref, dnormed, dresid_ref, None, drows_ref, dnorms_ref
        )


def norm_back(value, gain, grad):
    center = value - jnp.mean(value, axis=-1, keepdims=True)
    inverse = lax.rsqrt(jnp.mean(center * center, axis=-1, keepdims=True) + 1e-06)
    hat = center * inverse
    scaled = grad * gain
    d_value = inverse * (
        scaled
        - jnp.mean(scaled, axis=-1, keepdims=True)
        - hat * jnp.mean(scaled * hat, axis=-1, keepdims=True)
    )
    return (
        d_value,
        jnp.sum(grad * hat, axis=0, keepdims=True),
        jnp.sum(grad, axis=0, keepdims=True),
    )


def norm_rows_back(
    resid_ref, norms_ref, at, dother_ref, dnormed_ref, dresid_ref, out_ref, rows_ref, dnorms_ref
):
    d_gain = jnp.zeros((1, resid_ref.shape[1]), SINGLE)
    d_bias = jnp.zeros((1, resid_ref.shape[1]), SINGLE)
    for f in range(FRAMES):
        rows = frame_rows(f)
        d_value, gain, bias = norm_back(
            resid_ref[rows, :],
            norms_ref[at : at + 1, :],
            dother_ref[rows, :] + dnormed_ref[rows, :],
        )
        d_value = d_value + dresid_ref[rows, :]
        if out_ref is not None:
            out_ref[rows, :] = d_value
        rows_ref[rows, :] = low(d_value)
        d_gain, d_bias = d_gain + gain, d_bias + bias
    dnorms_ref[0:1, :] = d_gain
    dnorms_ref[1:2, :] = d_bias


def accumulate(ref, value):
    first = pl.program_id(0) == 0
    ref[...] = jnp.where(first, value, ref[...] + value)


def feed_fwd_kernel(normed_ref, *refs):
    up_refs, down_refs = refs[:2], refs[2:4]
    act_ref, slope_ref, branch_ref = refs[4:]
    hidden = dot(normed_ref[...], wide(*up_refs))
    root = 0.7978845608028654
    square = hidden * hidden
    bend = jnp.tanh(hidden * (root + root * 0.044715 * square))
    half = 0.5 + 0.5 * bend
    act_ref[0] = low(hidden * half)
    slope_ref[0] = low(
        half + hidden * (0.5 - 0.5 * bend * bend) * (root + 3.0 * root * 0.044715 * square)
    )
    accumulate(branch_ref, dot(act_ref[0], wide(*down_refs), NT))


def feed_fwd_last_kernel(normed_ref, *refs):
    resid_ref, branch_ref, norms_ref, valid_ref = refs[4:8]
    act_ref, slope_ref, out_ref, sums_ref, branch = refs[8:]
    feed_fwd_kernel(normed_ref, *refs[:4], act_ref, slope_ref, branch)

    @pl.when(pl.program_id(0) == 1)
    def _():
        sums = jnp.zeros(sums_ref.shape, SINGLE)
        for f in range(FRAMES):
            rows = frame_rows(f)
            value = resid_ref[rows, :] + (branch_ref[rows, :] + branch[rows, :])
            out_ref[rows, :] = value
            normed = layer_norm(value, norms_ref[6:7, :], norms_ref[7:8, :])
            sums = sums + jnp.sum(normed * valid_ref[rows, :], axis=0, keepdims=True)
        sums_ref[...] = sums


def feed_bwd_kernel(normed_ref, grad_ref, *refs):
    up_refs, down_refs = refs[:2], refs[2:4]
    act_ref, slope_ref, dup_ref, ddown_ref, dnormed_ref, dhid = refs[4:]
    dhid[...] = low(dot(grad_ref[...], wide(*down_refs)) * slope_ref[0].astype(SINGLE))
    ddown_ref[0] = low(dot(grad_ref[...], act_ref[0], TN))
    dup_ref[0] = low(dot(normed_ref[...], dhid[...], TN))
    accumulate(dnormed_ref, dot(dhid[...], wide(*up_refs), NT))


def feed_bwd_last_kernel(normed_ref, grad_ref, *refs):
    act_ref, slope_ref, resid_ref, dresid_ref, dother_ref, norms_ref = refs[4:10]
    dup_ref, ddown_ref, out_ref, drows_ref, dnorms_ref, dhid, dnormed = refs[10:]
    feed_bwd_kernel(
        normed_ref, grad_ref, *refs[:4], act_ref, slope_ref, dup_ref, ddown_ref, dnormed, dhid
    )

    @pl.when(pl.program_id(0) == 1)
    def _():
        norm_rows_back(
            resid_ref, norms_ref, 4, dother_ref, dnormed, dresid_ref, out_ref, drows_ref, dnorms_ref
        )


def embed_kernel(patches_ref, weight_ref, valid_ref, norms_ref, start_ref, normed_ref):
    start_ref[...] = dot(patches_ref[...], weight_ref[...]) * valid_ref[...]
    for f in range(FRAMES):
        rows = frame_rows(f)
        normed_ref[rows, :] = low(
            layer_norm(start_ref[rows, :], norms_ref[0:1, :], norms_ref[1:2, :])
        )


def embed_bwd_kernel(
    patches_ref, start_ref, valid_ref, drows_ref, da_ref, db_ref, norms_ref, dnorms_ref, out_ref, dstart
):
    dim = start_ref.shape[1]
    d_gain, d_bias = jnp.zeros((1, dim), SINGLE), jnp.zeros((1, dim), SINGLE)
    for f in range(FRAMES):
        rows = frame_rows(f)
        d_value, gain, bias = norm_back(
            start_ref[rows, :], norms_ref[0:1, :], da_ref[rows, :] + db_ref[rows, :]
        )
        dstart[rows, :] = low((drows_ref[rows, :].astype(SINGLE) + d_value) * valid_ref[rows, :])
        d_gain, d_bias = d_gain + gain, d_bias + bias
    out_ref[:, :dim] = low(dot(patches_ref[...], dstart[...], TN))
    padded = jnp.concatenate(
        [d_gain, d_bias, dnorms_ref[...], jnp.zeros((120, dim), SINGLE)], axis=0
    )
    out_ref[:, dim : dim + 128] = low(padded.T)


def enter_frame_kernel(start_ref, mixed_ref, weight_ref, norms_ref, out_ref, normed_ref):
    out_ref[...] = start_ref[...] + dot(mixed_ref[...], weight_ref[...], NT)
    for f in range(FRAMES):
        rows = frame_rows(f)
        normed_ref[rows, :] = low(
            layer_norm(out_ref[rows, :], norms_ref[2:3, :], norms_ref[3:4, :])
        )


def loss_kernel(
    dim,
    classes,
    proj,
    clip_ref,
    facts_ref,
    small_ref,
    resid_ref,
    valid_ref,
    norms_ref,
    loss_ref,
    dsmall_ref,
    pooled_ref,
    dresid_ref,
    drows_ref,
    dnorms_ref,
    dpool,
):
    facts = facts_ref[...]
    count = facts.shape[0]
    label, mate = (facts[:, dim + i : dim + i + 1].astype(jnp.int32) for i in range(2))
    pooled = low(facts[:, :dim] / facts[:, dim + 2 : dim + 3])
    pooled_ref[...] = pooled
    both = dot(pooled, small_ref[...])
    lane = lax.broadcasted_iota(jnp.int32, both.shape, 1)
    logits = jnp.where(lane < classes, both, -1e30)
    hot = (lane == label).astype(SINGLE)
    top = jnp.max(logits, axis=1, keepdims=True)
    raised = jnp.exp(logits - top)
    total = jnp.sum(raised, axis=1, keepdims=True)
    cross = top + jnp.log(total) - jnp.sum(both * hot, axis=1, keepdims=True)
    d_logits = raised / total - hot
    embedding = jnp.where((lane >= classes) & (lane < classes + proj), both, 0.0)
    inverse = lax.rsqrt(jnp.sum(embedding * embedding, axis=1, keepdims=True) + 1e-06)
    unit = embedding * inverse
    exact = functools.partial(
        lax.dot_general, precision=EXACT, preferred_element_type=SINGLE
    )
    similar = exact(unit, unit, NT) / TEMPER
    row = lax.broadcasted_iota(jnp.int32, (count, count), 0)
    col = lax.broadcasted_iota(jnp.int32, (count, count), 1)
    mate_hot = (col == mate).astype(SINGLE)
    masked = jnp.where(row == col, -1e30, similar)
    top = jnp.max(masked, axis=1, keepdims=True)
    raised = jnp.exp(masked - top)
    total = jnp.sum(raised, axis=1, keepdims=True)
    contrast = top + jnp.log(total) - jnp.sum(similar * mate_hot, axis=1, keepdims=True)
    loss_ref[...] = jnp.sum(cross + contrast, axis=0, keepdims=True)
    d_similar = (raised / total - mate_hot) / TEMPER
    d_unit = exact(d_similar, unit, NN) + exact(d_similar, unit, TN)
    d_embed = inverse * d_unit - embedding * (inverse * inverse * inverse) * jnp.sum(
        embedding * d_unit, axis=1, keepdims=True
    )
    dsmall_ref[...] = low(jnp.where(lane < classes, d_logits, d_embed))
    dpool[...] = dot(dsmall_ref[...], small_ref[...], NT) / facts[:, dim + 2 : dim + 3]
    d_pooled = dpool[pl.ds(clip_ref[0], 1), :]
    d_gain, d_bias = jnp.zeros((1, dim), SINGLE), jnp.zeros((1, dim), SINGLE)
    for f in range(FRAMES):
        rows = frame_rows(f)
        d_value, gain, bias = norm_back(
            resid_ref[rows, :], norms_ref[6:7, :], valid_ref[rows, :] * d_pooled
        )
        dresid_ref[rows, :] = d_value
        drows_ref[rows, :] = low(d_value)
        d_gain, d_bias = d_gain + gain, d_bias + bias
    dnorms_ref[0:1, :] = d_gain
    dnorms_ref[1:2, :] = d_bias


def adam_step(master, first, second, clipped, rate):
    first_new = BETA_ONE * first + (1.0 - BETA_ONE) * clipped
    second_new = BETA_TWO * second + (1.0 - BETA_TWO) * clipped * clipped
    first_hat = first_new / (1.0 - BETA_ONE**STEP)
    second_hat = second_new / (1.0 - BETA_TWO**STEP)
    master_new = master - rate * (first_hat / (jnp.sqrt(second_hat) + ADAM_EPS) + DECAY * master)
    return (master_new, first_new, second_new)


def adam_kernel(classes, proj, total_ref, *refs):
    masters, firsts, seconds, parts, outs = (
        refs[0:8], refs[8:16], refs[16:24], refs[24:30], refs[31:]
    )
    norm = jnp.sqrt(total_ref[...])
    refs[30][...] = norm
    factor = jnp.minimum(1.0, CLIP_AT / (norm + 1e-06))
    early, small, first, second, up, down = (ref[...] * factor for ref in parts)
    dim = masters[0].shape[1]
    columns = lambda k: slice(GROUP * k, GROUP * (k + 1))
    todo = [
        (0, ..., early[:, :dim]),
        (1, ..., early[:, dim : dim + 128].T[:8]),
        (2, ..., small[:, :classes]),
        (3, ..., small[:, classes : classes + proj]),
        (6, ..., up),
        (7, ..., down),
    ]
    for layer, grad in enumerate((first, second)):
        todo += [(4, (layer, k), grad[:, columns(k)]) for k in range(3)]
        todo.append((5, layer, grad[:, columns(3)].T))
    for i, at, grad in todo:
        results = adam_step(
            masters[i][at], firsts[i][at], seconds[i][at], grad, NORM_RATE if i == 1 else RATE
        )
        for j, result in enumerate(results):
            outs[3 * i + j][at] = result


def whole(shape):
    return pl.BlockSpec(shape, lambda g: (0,) * len(shape))


def per_group(rows, width):
    return pl.BlockSpec((1, rows, width), lambda g: (g, 0, 0))


def columns_of(width):
    return pl.BlockSpec((1, FRAMES, width, SLOTS), lambda g: (g, 0, 0, 0))


def shaped(*shape, dtype=SINGLE):
    return jax.ShapeDtypeStruct(shape, dtype)


def spec_of(value):
    shape = value.shape
    if len(shape) == 4:
        return columns_of(shape[2])
    return per_group(*shape[1:]) if len(shape) == 3 else whole(shape)


def call(kernel, name, inputs, outputs, scratch=(), gflops=1, steps=2, in_specs=None):
    return pl.pallas_call(
        kernel,
        grid=(steps,),
        in_specs=in_specs or [spec_of(value) for value in inputs],
        out_specs=[spec_of(value) for value in outputs],
        out_shape=list(outputs),
        scratch_shapes=[pltpu.VMEM(shape, dtype) for shape, dtype in scratch],
        compiler_params=pltpu.CompilerParams(vmem_limit_bytes=GRANT),
        cost_estimate=pl.CostEstimate(
            flops=gflops * 10**9, bytes_accessed=8 << 20, transcendentals=0
        ),
        name=name,
    )(*inputs)


def by_group(width, rows=ROWS):
    return shaped(2, rows, width, dtype=LOWER)


def weight_specs(parts, rows):
    inputs, specs = [], []
    for value, half in parts:
        taken = rows
        if rows % 16 != 0:
            value = value[:, :, :rows].reshape(2, 1, -1, value.shape[-1])
            taken = value.shape[2]
        width = value.shape[3] if half is None else value.shape[3] // 2
        inputs.append(value)
        specs.append(
            pl.BlockSpec((1, value.shape[1], taken, width), lambda g, h=half or 0: (g, 0, 0, h))
        )
    return inputs, specs


def block_call(kernel, name, before, parts, rows, rest, outputs, scratch, gflops):
    parts, specs = weight_specs(parts, rows)
    specs = [spec_of(v) for v in before] + specs + [spec_of(v) for v in rest]
    return call(
        kernel, name, (*before, *parts, *rest), outputs, scratch, gflops, in_specs=specs
    )


def temporal_forward(normed, own, other, rows):
    dim = normed.shape[1]
    parts, specs = weight_specs([*own, *other], rows)
    place = [lambda g: jnp.minimum(g, 1)] * 2 + [lambda g: jnp.maximum(g - 2, 0)] * 2
    specs = [
        pl.BlockSpec(spec.block_shape, lambda g, at=at: (at(g), 0, 0, 0))
        for spec, at in zip(specs, place)
    ]
    width = parts[0].shape[3]
    return call(
        temporal_fwd_kernel,
        "temporal_forward",
        (normed, *parts),
        (shaped(4, FRAMES, QKV, SLOTS, dtype=LOWER), shaped(4, ROWS, GROUP, dtype=LOWER)),
        [((FRAMES, GROUP, SLOTS), LOWER), ((dim, width), LOWER), ((dim, width), LOWER)],
        40,
        4,
        [spec_of(normed), *specs],
    )


def temporal_backward(normed, grad, parts, rows, qkv, mixed, skip):
    dim = normed.shape[1]
    parts, specs = weight_specs(parts, rows)
    specs = [spec_of(normed), spec_of(grad), *specs]
    specs += [
        pl.BlockSpec((1, FRAMES, QKV, SLOTS), lambda g: (g + skip, 0, 0, 0)),
        pl.BlockSpec((1, ROWS, GROUP), lambda g: (g + skip, 0, 0)),
    ]
    return call(
        temporal_bwd_kernel,
        "temporal_backward",
        (normed, grad, *parts, qkv, mixed),
        (by_group(dim, dim), shaped(ROWS, dim)),
        [((ROWS, QKV), LOWER), ((FRAMES, GROUP, SLOTS), LOWER), ((FRAMES, QKV, SLOTS), LOWER)],
        14,
        2,
        specs,
    )


def spatial_forward(normed, parts, rows, key_extra, last=None):
    dim = normed.shape[1]
    outputs = (by_group(QKV), by_group(GROUP), by_group(GROUP), shaped(ROWS, dim))
    kernel, scratch = spatial_fwd_kernel, []
    if last is not None:
        kernel, scratch = spatial_fwd_last_kernel, [((ROWS, dim), SINGLE)]
        outputs += (shaped(ROWS, dim, dtype=LOWER),)
    rest = (key_extra, *(last or ()))
    return block_call(
        kernel, "spatial_forward", (normed,), parts, rows, rest, outputs, scratch, 15
    )


def spatial_backward(normed, grad, parts, rows, qkv, mixed, extra, key_extra, last=None):
    dim = normed.shape[1]
    kernel, scratch = spatial_bwd_kernel, [((ROWS, QKV), LOWER)]
    outputs = (by_group(dim, dim), shaped(ROWS, dim))
    if last is not None:
        kernel, scratch = spatial_bwd_last_kernel, scratch + [((ROWS, dim), SINGLE)]
        outputs = (by_group(dim, dim), shaped(ROWS, dim, dtype=LOWER), shaped(2, dim))
    rest = (qkv, mixed, extra, key_extra, *(last or ()))
    return block_call(
        kernel, "spatial_backward", (normed, grad), parts, rows, rest, outputs, scratch, 30
    )


def feed_forward(normed, parts, rows, last=None):
    dim, width = normed.shape[1], 2 * parts[0][0].shape[3]
    outputs = (by_group(width), by_group(width), shaped(ROWS, dim))
    kernel, scratch = feed_fwd_kernel, []
    if last is not None:
        kernel, scratch = feed_fwd_last_kernel, [((ROWS, dim), SINGLE)]
        outputs += (shaped(1, dim),)
    return block_call(
        kernel, "feed_forward", (normed,), parts, rows, last or (), outputs, scratch, 10
    )


def feed_backward(normed, grad, parts, rows, act, slope, last=None):
    dim, width = normed.shape[1], 2 * parts[0][0].shape[3]
    kernel, scratch = feed_bwd_kernel, [((ROWS, width), LOWER)]
    outputs = (by_group(width, dim), by_group(width, dim), shaped(ROWS, dim))
    if last is not None:
        kernel, scratch = feed_bwd_last_kernel, scratch + [((ROWS, dim), SINGLE)]
        outputs += (shaped(ROWS, dim, dtype=LOWER), shaped(2, dim))
    rest = (act, slope, *(last or ()))
    return block_call(
        kernel, "feed_backward", (normed, grad), parts, rows, rest, outputs, scratch, 15
    )


def embed(patches, weight, valid, norms):
    dim = patches.shape[1]
    outputs = (shaped(ROWS, dim), shaped(ROWS, dim, dtype=LOWER))
    return call(embed_kernel, "embed", (patches, weight, valid, norms), outputs, (), 15, 1)


def embed_backward(patches, start, valid, d_rows, d_a, d_b, norms, d_norms):
    dim = patches.shape[1]
    return call(
        embed_bwd_kernel,
        "embed_backward",
        (patches, start, valid, d_rows, d_a, d_b, norms, d_norms),
        (shaped(dim, dim + 128, dtype=LOWER),),
        [((ROWS, dim), LOWER)],
        30,
        1,
    )[0]


def enter_frame(start, mixed, weight, norms):
    dim = start.shape[1]
    return call(
        enter_frame_kernel,
        "enter_frame",
        (start, mixed, weight, norms),
        (shaped(ROWS, dim), shaped(ROWS, dim, dtype=LOWER)),
        [],
        2,
        1,
    )


def all_losses(clip, facts, small, resid, valid, norms, classes, proj):
    count, dim = facts.shape[0], resid.shape[1]
    inputs = (facts, small, resid, valid, norms)
    return call(
        functools.partial(loss_kernel, dim, classes, proj),
        "losses",
        (clip, *inputs),
        (
            shaped(1, 1),
            shaped(count, dim, dtype=LOWER),
            shaped(count, dim, dtype=LOWER),
            shaped(ROWS, dim),
            shaped(ROWS, dim, dtype=LOWER),
            shaped(2, dim),
        ),
        [((count, dim), SINGLE)],
        1,
        1,
        [pl.BlockSpec(memory_space=pltpu.SMEM)] + [whole(value.shape) for value in inputs],
    )


def optimizer(total, masters, firsts, seconds, parts, classes, proj):
    inputs = (total, *masters, *firsts, *seconds, *parts)
    outputs = [shaped(1, 1)] + [shaped(*value.shape) for value in masters for _ in range(3)]
    return pl.pallas_call(
        functools.partial(adam_kernel, classes, proj),
        grid=(1,),
        in_specs=[whole(value.shape) for value in inputs],
        out_specs=[whole(value.shape) for value in outputs],
        out_shape=outputs,
        compiler_params=pltpu.CompilerParams(vmem_limit_bytes=GRANT),
        name="optimizer",
    )(*inputs)


def finish_kernel(count, token_ref, *refs):
    squares = jnp.zeros((1, 1), SINGLE)
    ins, outs = list(refs[: -count - 2]), refs[-count - 2 :]
    per = len(ins) // count
    for i in range(count):
        value = functools.reduce(
            jnp.add, (ref[...].astype(SINGLE) for ref in ins[per * i : per * (i + 1)])
        )
        outs[i][...] = value
        squares = squares + jnp.sum(
            jnp.sum(value * value, axis=1, keepdims=True), axis=0, keepdims=True
        )
    outs[count][...] = squares
    outs[count + 1][...] = token_ref[...]


def finish(token, lists):
    inputs = (token, *(term for terms in lists for term in terms))
    outputs = [shaped(*terms[0].shape) for terms in lists]
    outputs += [shaped(1, 1), shaped(*token.shape)]
    return call(
        functools.partial(finish_kernel, len(lists)),
        "finish",
        inputs,
        outputs,
        (),
        30,
        1,
        [whole(value.shape) for value in inputs],
    )


def pace_kernel(token_ref, out_ref):
    out_ref[...] = token_ref[...]


def pace(token):
    return call(pace_kernel, "pace", (token,), (shaped(*token.shape),), (), 30, 1)[0]


def tick(*values):
    return lax.optimization_barrier(values)


def summed(terms):
    return functools.reduce(jnp.add, (term.astype(SINGLE) for term in terms))


class Cube:
    def __init__(self, sizes):
        self.count = sizes["batch"] * sizes["head"]
        self.mine = lax.axis_index(ALL)
        batch_bits = sizes["batch"].bit_length() - 1
        self.batch_masks = [4 << k for k in reversed(range(batch_bits))]

    def swap(self, value, mask):
        return lax.ppermute(value, ALL, [(i, i ^ mask) for i in range(self.count)])

    def has(self, mask):
        return (self.mine & mask) != 0

    def join(self, value, *masks):
        for mask in masks:
            value = self.merge(value, self.swap(value, mask), mask)
        return value

    def fork(self, value):
        return self.stack(value, self.swap(value, 2), 2)

    def step(self, token, sends, late=(), work=None):
        values = [value for value, _ in (*sends, *late)]
        *values, token = tick(*values, token)
        masks = [mask for _, mask in (*sends, *late)]
        received = [self.swap(value, mask) for value, mask in zip(values, masks)]
        count = len(sends)
        if work is not None:
            *done, paced = finish(token, work)
            *ended, token = tick(*received[:count], paced)
            return token, done, *ended, *received[count:]
        *ended, token = tick(*received[:count], pace(token))
        return token, *ended, *received[count:]


    def quads(self):
        *_, high, near, _ = self.batch_masks
        return [near, high, near | high]

    def gathered(self, value, others):
        near, high, _ = (self.has(mask) for mask in self.quads())
        p = [value, *others]
        p = [jnp.where(near, p[i ^ 1], p[i]) for i in range(4)]
        p = [jnp.where(high, p[i ^ 2], p[i]) for i in range(4)]
        shape = value.shape
        return jnp.stack(p, axis=-3).reshape(*shape[:-3], 4 * shape[-3], *shape[-2:])

    def quarter(self, terms):
        near, high, _ = (self.has(mask).astype(jnp.int32) for mask in self.quads())
        place = near + 2 * high
        views = [term.reshape(-1, 4, *term.shape[-2:]) for term in terms]
        part = lambda view, r: lax.dynamic_index_in_dim(view, place ^ r, 1, False)
        sends = [low(summed([part(view, r) for view in views])) for r in range(1, 4)]
        return sends, [part(view, 0) for view in views]

    def fourfold(self, sends):
        return list(zip(sends, self.quads()))

    def merge(self, value, other, mask):
        has = self.has(mask)
        both = jnp.stack([jnp.where(has, other, value), jnp.where(has, value, other)], axis=-3)
        shape = value.shape
        return both.reshape(*shape[:-3], 2 * shape[-3], *shape[-2:])

    def stack(self, value, other, mask):
        has = self.has(mask)
        return jnp.stack([jnp.where(has, other, value), jnp.where(has, value, other)])


    def cut(self, terms, mask):
        shape = terms[0].shape
        mine = self.has(mask).astype(jnp.int32)
        pairs = [
            term.reshape(*shape[:-3], shape[-3] // 2, 2, *shape[-2:]) for term in terms
        ]
        half = lambda pair, which: lax.dynamic_index_in_dim(pair, which, pair.ndim - 3, False)
        return low(summed([half(pair, 1 - mine) for pair in pairs])), [
            half(pair, mine) for pair in pairs
        ]

    def shed(self, terms, *masks):
        for mask in masks:
            send, keep = self.cut(terms, mask)
            terms = keep + [self.swap(send, mask)]
        return terms

    def cut_row(self, terms):
        mine = self.has(2).astype(jnp.int32)
        half = lambda term, which: lax.dynamic_index_in_dim(term, which, 0, False)
        return low(summed([half(term, 1 - mine) for term in terms])), [
            half(term, mine) for term in terms
        ]

    def meet(self, terms):
        send, keep = self.cut_row(terms)
        return keep + [self.swap(send, 2)]

    def total(self, value):
        for mask in [1, 2, *self.batch_masks[::-1]]:
            value = value + self.swap(value, mask)
        return value

    def swap_frames(self, parts):
        return [parts[0]] + [self.swap(parts[r], r) for r in range(1, FRAMES)]


def body(sizes, *args):
    patches, bucket, labels, partner = args[:4]
    views = [lambda v: v] * 4 + [
        lambda v: v.transpose(0, 2, 1, 3), lambda v: v, lambda v: v, lambda v: v.T
    ]
    masters, firsts, seconds = (
        [view(value) for view, value in zip(views, args[4 + 8 * i : 12 + 8 * i])] for i in range(3)
    )
    patch_weight, norm_params, head_weight, proj_weight, attn_in, attn_out, up, down = masters
    cube = Cube(sizes)
    dim = norm_params.shape[1] * cube.count
    classes, proj = head_weight.shape[1], proj_weight.shape[1]
    rows_wide, rows_small = attn_in.shape[2], patch_weight.shape[0]
    place = lax.axis_index(HEAD)

    *first, near, last = cube.batch_masks
    middle = dim // 2
    blocked = lambda value: value.reshape(*value.shape[:-2], -1, rows_wide, value.shape[-1])
    pack = lambda w_in, w_out: jnp.concatenate(
        [low(w_in[0]), low(w_in[1]), low(w_in[2]), low(w_out).T], axis=1
    )[None]
    patch_count = jnp.where(bucket == 1, PMAX, PSMALL)
    offset = jnp.arange(SLOTS)[None, :]
    number = (place ^ jnp.arange(FRAMES))[:, None]
    frame_valid = ((number * SLOTS + offset) < patch_count).reshape(ROWS, 1).astype(SINGLE)
    slot_valid = (jnp.broadcast_to(place * SLOTS + offset, (FRAMES, SLOTS)) < patch_count).reshape(
        ROWS, 1
    ).astype(SINGLE)
    lane = jnp.arange(HD)[None, :]
    key_extra = low(
        jnp.where(lane == 0, jnp.where(frame_valid > 0, 0.0, -1e30), (lane < 4).astype(SINGLE))
    )

    extra = -(-(rows_small + 1) // 16) * 16
    norm_row = low(norm_params).reshape(1, -1)
    first_w = jnp.concatenate(
        [
            pack(attn_in[0], attn_out[0])[0],
            low(patch_weight),
            jnp.pad(norm_row, ((0, extra - rows_small - 1), (0, dim - norm_row.shape[1]))),
        ]
    )[None]
    token = jnp.zeros((8, 128), SINGLE)
    clip, w_in, w_out, w_up, w_down = patches[0], attn_in[1], attn_out[1], up, down
    for mask in first:
        first_w, clip, w_in, w_out, w_up, w_down = tick(first_w, clip, w_in, w_out, w_up, w_down)
        token, other = cube.step(token, [(first_w, mask)])
        first_w = cube.merge(first_w, other, mask)
    blocks = jnp.pad(clip, ((0, ROWS - PMAX), (0, 0))).reshape(FRAMES, SLOTS, -1)
    blocks = jnp.where((place & 1) != 0, blocks[jnp.array([1, 0, 3, 2])], blocks)
    blocks = jnp.where((place & 2) != 0, blocks[jnp.array([2, 3, 0, 1])], blocks)
    blocks, token = tick(blocks, token)
    second_w = jnp.concatenate([pack(w_in, w_out)[0], low(w_up)])[None]
    small = jnp.concatenate([low(head_weight), low(proj_weight)], axis=1)
    small = jnp.pad(small, ((0, -rows_small % 16), (0, dim - small.shape[1])))
    down_w = jnp.concatenate([low(w_down), small])[None]

    token, other, *slots = cube.step(
        token, [(first_w, near)] + [(blocks[r], r) for r in range(1, FRAMES)]
    )
    first_w = cube.merge(first_w, other, near)
    by_frame = blocks.reshape(ROWS, -1)

    left, right = first_w[..., :middle], first_w[..., middle:]
    second_w = cube.join(second_w, *first[:-1])
    token, other_left, other_right, *others = cube.step(
        token, [(left, last), (right, 2)], cube.fourfold([second_w] * 3)
    )
    left, right = cube.merge(left, other_left, last), cube.stack(right, other_right, 2)

    left, right, *slots = tick(left, right, *slots)
    by_slot = jnp.concatenate([blocks[0], *slots])
    token, other_left, other_right = cube.step(token, [(left, 2), (right, last)])
    by_slot, slot_valid, token, *others = tick(by_slot, slot_valid, token, *others)
    own_first = (cube.stack(left, other_left, 2), cube.merge(right, other_right, last))

    second_w = cube.gathered(second_w, others)
    token, *other_first, other_left, other_right, other = cube.step(
        token,
        [(own_first[0], 1), (own_first[1], 1)],
        [(second_w[..., :middle], last), (second_w[..., middle:], 2)]
        + [(down_w, mask) for mask in first[:1]],
    )
    other_down = other
    joined = lambda parts, at: jnp.concatenate([part[:, :, at] for part in parts], axis=-1)
    early = [joined(parts, slice(rows_wide, None)) for parts in (own_first, other_first)]
    early = cube.stack(*early, 1).transpose(2, 1, 0, 3, 4)
    patch_copy = early[..., :rows_small, :].reshape(dim, dim)
    norms = early[..., rows_small, : norm_row.shape[1]].reshape(-1, 8, rows_small)
    norms = norms.transpose(1, 0, 2).reshape(8, dim).astype(SINGLE)
    start_slot, normed_t = embed(by_slot, patch_copy, slot_valid, norms)
    normed_t, other_left, other_right = tick(normed_t, other_left, other_right)
    left = cube.merge(second_w[..., :middle], other_left, last)
    right = cube.stack(second_w[..., middle:], other_right, 2)
    ours, theirs = slice(0, rows_wide), slice(rows_wide, None)
    other_left, other_right = (
        cube.swap(left[..., ours, :], 2), cube.swap(right[..., ours, :], last)
    )
    first_w = tuple([(part, None) for part in parts] for parts in (own_first, other_first))
    qkv_t, mixed_t = temporal_forward(normed_t, *first_w, rows_wide)
    mixed_t, other_left, other_right = tick(mixed_t, other_left, other_right)
    parts = [
        jnp.concatenate(
            [mixed_t[2 * (c ^ (r & 1)) + y][frame_rows(r)] for c in range(2) for y in range(2)],
            axis=1,
        )
        for r in range(FRAMES)
    ]
    parts[0], other_down, patch_copy, token = tick(parts[0], other_down, patch_copy, token)
    outs = [
        part[y, :, :rows_wide, GROUP:].reshape(dim, GROUP)
        for part in (own_first[1], other_first[1])
        for y in range(2)
    ]
    out_first = jnp.concatenate(outs, axis=1)
    start_frame = dot(by_frame, patch_copy) * frame_valid
    own_second = jnp.concatenate(
        [
            cube.stack(left[..., ours, :], other_left, 2),
            cube.merge(right[..., ours, :], other_right, last),
        ],
        axis=-1,
    )
    down_w = cube.join(cube.merge(down_w, other_down, first[0]), *first[1:])

    token, *received, other = cube.step(
        token, [(parts[r], r) for r in range(1, FRAMES)] + [(down_w, near)]
    )
    down_w = cube.merge(down_w, other, near)
    mixed_frame = jnp.concatenate([parts[0], *received])
    mixed_frame, key_extra, own_second, down_w, out_first, start_frame = tick(
        mixed_frame, key_extra, own_second, down_w, out_first, start_frame
    )

    resid_one, normed_s = enter_frame(start_frame, mixed_frame, out_first, norms)
    other_second = cube.swap(own_second, 1)
    other_left = cube.swap(left[..., theirs, :], 2)
    other_right = cube.swap(right[..., theirs, :], last)
    left_down, right_down = cube.join(down_w[..., :middle], last), cube.fork(down_w[..., middle:])
    qkv_s, mixed_s, extra_s = ([None, None] for _ in range(3))
    halves = lambda value: [(value, 0), (value, 1)]
    qkv_s[0], mixed_s[0], extra_s[0], branch = spatial_forward(
        normed_s, halves(own_second), rows_wide, key_extra
    )
    branch, normed_s, other_second, other_left, other_right, left_down, right_down = tick(
        branch, normed_s, other_second, other_left, other_right, left_down, right_down
    )
    own_up = (
        cube.stack(left[..., theirs, :], other_left, 2),
        cube.merge(right[..., theirs, :], other_right, last),
    )
    other_up = [cube.swap(part, 1) for part in own_up]
    left, right = cube.fork(left_down), cube.join(right_down, last)
    qkv_s[1], mixed_s[1], extra_s[1], resid_two, normed_m = spatial_forward(
        normed_s, halves(other_second), rows_wide, key_extra, (resid_one, branch, norms)
    )
    normed_m, left, right, *other_up = tick(normed_m, left, right, *other_up)

    own_down, other_down = (left, right), (cube.swap(left, 1), cube.swap(right, 1))
    own_feed = [(part, None) for part in (*own_up, *own_down)]
    other_feed = [(part, None) for part in (*other_up, *other_down)]
    act, slope = ([None, None] for _ in range(2))
    act[0], slope[0], branch = feed_forward(normed_m, own_feed, rows_wide)
    act[1], slope[1], resid_three, sums = feed_forward(
        normed_m, other_feed, rows_wide, (resid_two, branch, norms, frame_valid)
    )
    small = [
        joined(parts, slice(rows_wide, rows_wide + rows_small)) for parts in (own_down, other_down)
    ]
    small = cube.stack(*small, 1).transpose(2, 1, 0, 3, 4).reshape(dim, dim)

    for mask in (1, 2):
        sums = sums + cube.swap(sums, mask)
    facts = jnp.stack([labels[0], partner[0], FRAMES * patch_count[0]]).astype(SINGLE)
    gathered = jnp.concatenate([sums, jnp.pad(facts, (0, 125))[None]], axis=1)[None]
    gathered = cube.join(gathered, *first[:-1])
    others = [cube.swap(gathered, mask) for mask in cube.quads()]
    gathered = cube.join(cube.gathered(gathered, others), last)[:, 0]
    clip = lax.axis_index("batch").reshape(1)
    loss_sum, d_small, pooled_low, d_resid, d_rows, d_norms_f = all_losses(
        clip, gathered, small, resid_three, frame_valid, norms, classes, proj
    )

    d_up, d_down = [None, None], [None, None]
    d_up[1], d_down[1], d_normed = feed_backward(
        normed_m, d_rows, other_feed, rows_wide, act[1], slope[1]
    )
    up_other, down_other, d_normed, d_rows, normed_m = tick(
        d_up[1], d_down[1], d_normed, d_rows, normed_m
    )
    core_up, core_down = cube.swap(up_other, 1), cube.swap(down_other, 1)
    d_up[0], d_down[0], d_resid, d_rows, d_norms_m = feed_backward(
        normed_m,
        d_rows,
        own_feed,
        rows_wide,
        act[0],
        slope[0],
        (resid_two, d_resid, d_normed, norms),
    )
    d_resid, d_rows, up_own, down_own, core_up, core_down = tick(
        d_resid, d_rows, d_up[0], d_down[0], core_up, core_down
    )

    sum_up = cube.meet([blocked(up_own), blocked(core_up)])
    sum_down = cube.shed([blocked(down_own), blocked(core_down)], last)
    d_second = [None, None]
    d_second[1], d_normed = spatial_backward(
        normed_s, d_rows, halves(other_second), rows_wide, qkv_s[1], mixed_s[1], extra_s[1], key_extra
    )
    d_small = lax.dynamic_slice_in_dim(
        dot(pooled_low, d_small, TN), cube.mine * rows_small, rows_small, 0
    )
    second_other, d_normed, d_rows, normed_s, sum_up[-1], sum_down[-1], d_small = tick(
        d_second[1], d_normed, d_rows, normed_s, sum_up[-1], sum_down[-1], d_small
    )
    core_second = cube.swap(second_other, 1)
    sum_up, sum_down = cube.shed(sum_up, last), cube.meet(sum_down)
    d_second[0], d_rows, d_norms_s = spatial_backward(
        normed_s,
        d_rows,
        halves(own_second),
        rows_wide,
        qkv_s[0],
        mixed_s[0],
        extra_s[0],
        key_extra,
        (resid_one, d_resid, d_normed, norms),
    )
    d_rows, second_own, sum_up[-1], sum_down[-1], core_second = tick(
        d_rows, d_second[0], sum_up[-1], sum_down[-1], core_second
    )

    parts = split_frames(d_rows)
    send, sum_second = cube.cut([blocked(second_own), blocked(core_second)], last)
    token, *received, other = cube.step(
        token, [(parts[r], r) for r in range(1, FRAMES)], [(send, last)]
    )
    d_rows = jnp.concatenate([parts[0], *received])
    sum_second.append(other)

    sum_up, sum_down = cube.shed(sum_up, *first[-2::-1]), cube.shed(sum_down, *first[-2::-1])
    (sends_up, sum_up), (sends_down, sum_down) = cube.quarter(sum_up), cube.quarter(sum_down)
    sends = [jnp.concatenate(pair, axis=-2) for pair in zip(sends_up, sends_down)]
    others = [cube.swap(send, mask) for send, mask in cube.fourfold(sends)]
    d_first, d_normed = [None, None], [None, None]
    d_first[1], d_normed[1] = temporal_backward(
        normed_t, d_rows, first_w[1], rows_wide, qkv_t, mixed_t, 2
    )
    first_other, d_normed[1], d_rows, normed_t, sum_second[-1] = tick(
        d_first[1], d_normed[1], d_rows, normed_t, sum_second[-1]
    )
    core_first = cube.swap(first_other, 1)
    sum_second = cube.meet(sum_second)
    d_first[0], d_normed[0] = temporal_backward(
        normed_t, d_rows, first_w[0], rows_wide, qkv_t, mixed_t, 0
    )
    d_rows, first_own, d_normed[0], core_first, sum_second[-1], *others = tick(
        d_rows, d_first[0], d_normed[0], core_first, sum_second[-1], *others
    )
    sum_up += [other[..., :rows_wide, :] for other in others]
    sum_down += [other[..., rows_wide:, :] for other in others]

    sum_first = [blocked(first_own), blocked(core_first)]
    send_left, left = cube.cut_row([term[..., :middle] for term in sum_first])
    send_right, right = cube.cut([term[..., middle:] for term in sum_first], last)
    sum_second = cube.shed(sum_second, *first[-2::-1])
    send_left, send_right, d_normed[0], d_norms_f, d_small, sum_second[-1] = tick(
        send_left, send_right, d_normed[0], d_norms_f, d_small, sum_second[-1]
    )
    other_left, other_right = cube.swap(send_left, 2), cube.swap(send_right, last)
    sends, sum_second = cube.quarter(sum_second)
    others = [cube.swap(send, mask) for send, mask in cube.fourfold(sends)]
    d_norms = jnp.concatenate([d_norms_s, d_norms_m, d_norms_f])
    d_early = embed_backward(
        by_slot, start_slot, slot_valid, d_rows, d_normed[0], d_normed[1], norms, d_norms
    )
    send, sum_early = cube.cut([d_early.reshape(-1, rows_small, dim + 128)], 1)
    other_left, other_right, send, token = tick(other_left, other_right, send, token)
    other = cube.swap(send, 1)
    left.append(other_left)
    right.append(other_right)
    sum_early.append(other)

    send_left, left = cube.cut(left, last)
    send_right, right = cube.cut_row(right)
    send, sum_early = cube.cut(sum_early, 2)
    flat = lambda terms: [summed(terms)[0]]
    token, other_left, other_right, other = cube.step(
        token, [(send_left, last), (send_right, 2), (send, 2)]
    )
    *others, token = tick(*others, token)
    sum_second += others
    sum_first = [jnp.concatenate([summed(left + [other_left]), summed(right + [other_right])], -1)]
    sum_early.append(other)

    sum_first = cube.shed(sum_first, *first[-2::-1])
    sends, sum_first = cube.quarter(sum_first)
    send, sum_early = cube.cut(sum_early, last)
    token, (d_second, d_up, d_down, squares), *others, other = cube.step(
        token,
        [*cube.fourfold(sends), (send, last)],
        work=[flat(terms) for terms in (sum_second, sum_up, sum_down)],
    )
    sum_first += others
    sum_early.append(other)

    sum_early = cube.shed(sum_early, *first[-2::-1])
    sends, sum_early = cube.quarter(sum_early)
    square = lambda value: jnp.sum(value * value)
    d_first = summed(sum_first)[0]
    token, *others = cube.step(token, cube.fourfold(sends))
    d_early = summed(sum_early + others)[0]
    squares = squares[0, 0] + square(d_small) + square(d_first)

    total = cube.total((squares + square(d_early)).reshape(1, 1))
    parts = (d_early, d_small, d_first, d_second, d_up, d_down)
    grad_norm, *updates = optimizer(total, masters, firsts, seconds, parts, classes, proj)
    updates = [views[i // 3](update) for i, update in enumerate(updates)]
    return (loss_sum[0, 0], grad_norm[0, 0], *updates)


def solution(mesh):
    sizes = dict(mesh.shape)
    split = Mesh(mesh.devices.reshape(sizes["batch"], 2, sizes["head"] // 2), ALL)
    placed = (
        P("batch", HEAD, None),
        P("batch"),
        P("batch"),
        P("batch"),
        P(ALL, None),
        P(None, ALL),
        P(ALL, None),
        P(ALL, None),
        P(None, "batch", None, HEAD),
        P(None, HEAD, "batch"),
        P("batch", HEAD),
        P(HEAD, "batch"),
        P(ALL, None),
        P(None, ALL),
        P(ALL, None),
        P(ALL, None),
        P(None, "batch", None, HEAD),
        P(None, HEAD, "batch"),
        P("batch", HEAD),
        P(HEAD, "batch"),
        P(ALL, None),
        P(None, ALL),
        P(ALL, None),
        P(ALL, None),
        P(None, "batch", None, HEAD),
        P(None, HEAD, "batch"),
        P("batch", HEAD),
        P(HEAD, "batch"),
    )
    return jax.shard_map(
        functools.partial(body, sizes),
        mesh=split,
        in_specs=placed,
        out_specs=(
            P(),
            P(),
            P(ALL, None),
            P(ALL, None),
            P(ALL, None),
            P(None, ALL),
            P(None, ALL),
            P(None, ALL),
            P(ALL, None),
            P(ALL, None),
            P(ALL, None),
            P(ALL, None),
            P(ALL, None),
            P(ALL, None),
            P(None, "batch", None, HEAD),
            P(None, "batch", None, HEAD),
            P(None, "batch", None, HEAD),
            P(None, HEAD, "batch"),
            P(None, HEAD, "batch"),
            P(None, HEAD, "batch"),
            P("batch", HEAD),
            P("batch", HEAD),
            P("batch", HEAD),
            P(HEAD, "batch"),
            P(HEAD, "batch"),
            P(HEAD, "batch"),
        ),
        check_vma=False,
    )
```

```python
import functools

import jax
import jax.numpy as jnp
from jax import lax
from jax.experimental import pallas as pl
from jax.experimental.pallas import tpu as pltpu
from jax.sharding import Mesh
from jax.sharding import PartitionSpec as P

HD = 64
FRAMES = 4
PMAX = 784
PSMALL = 196
STEP = 5
SLOTS = 208
ROWS = FRAMES * SLOTS
GROUP = 192
QKV = 3 * GROUP


EXACT = lax.Precision.HIGHEST
TEMPER = 0.05
BETA_ONE = 0.5
BETA_TWO = 0.5
RATE = 0.04
NORM_RATE = 0.3
DECAY = 0.05
ADAM_EPS = 1e-08
CLIP_AT = 1.0
LOWER = jnp.bfloat16
SINGLE = jnp.float32
ALL = ("batch", "row", "core")
HEAD = ("row", "core")
GRANT = 56 << 20

NN = (((1,), (0,)), ((), ()))
NT = (((1,), (1,)), ((), ()))
TN = (((0,), (0,)), ((), ()))


def dot(left, right, dims=NN):
    return lax.dot_general(left, right, dims, preferred_element_type=SINGLE)


def low(value):
    return value.astype(LOWER)


def layer_norm(value, gain, bias):
    center = value - jnp.mean(value, axis=-1, keepdims=True)
    spread = jnp.mean(center * center, axis=-1, keepdims=True)
    return center * lax.rsqrt(spread + 1e-06) * gain + bias


def wide(*refs):
    return jnp.concatenate([ref[0].reshape(-1, ref.shape[-1]) for ref in refs], axis=1)


def three_parts(value):
    high = low(value)
    rest = value - high.astype(SINGLE)
    middle = low(rest)
    return high, middle, low(rest - middle.astype(SINGLE))


def frame_probs(query, keys):
    scores = [jnp.sum(query * key, axis=0, keepdims=True) * HD ** (-0.5) for key in keys]
    top = functools.reduce(jnp.maximum, scores)
    raised = [jnp.exp(score - top) for score in scores]
    total = functools.reduce(jnp.add, raised)
    return [value / total for value in raised]


def rounded(value):
    return low(value).astype(SINGLE)


def frame_rows(f):
    return slice(SLOTS * f, SLOTS * (f + 1))


def split_frames(rows):
    return [rows[frame_rows(f)] for f in range(FRAMES)]


def head_features(which, head):
    return slice(GROUP * which + HD * head, GROUP * which + HD * (head + 1))


def temporal_fwd_kernel(
    normed_ref, own_left, own_right, other_left, other_right, qkv_ref, mixed_ref, out, left, right
):
    for chosen, parts in (
        (pl.program_id(0) < 2, (own_left, own_right)),
        (pl.program_id(0) >= 2, (other_left, other_right)),
    ):

        @pl.when(chosen)
        def _(parts=parts):
            left[...], right[...] = wide(parts[0]), wide(parts[1])

    for f in range(FRAMES):
        rows = normed_ref[frame_rows(f), :]
        qkv_ref[0, f, : 2 * GROUP, :] = low(dot(rows, left[...])).T
        qkv_ref[0, f, 2 * GROUP :, :] = low(dot(rows, right[:, :GROUP])).T
    for head in range(GROUP // HD):
        query, keys, values = (
            [qkv_ref[0, f, head_features(i, head), :].astype(SINGLE) for f in range(FRAMES)]
            for i in range(3)
        )
        for f in range(FRAMES):
            probs = frame_probs(query[f], keys)
            mixed = sum(rounded(prob) * value for prob, value in zip(probs, values))
            out[f, head_features(0, head), :] = low(mixed)
    for f in range(FRAMES):
        mixed_ref[0, frame_rows(f), :] = out[f].T


def temporal_bwd_kernel(
    normed_ref,
    grad_ref,
    left_ref,
    right_ref,
    qkv_ref,
    mixed_ref,
    dweight_ref,
    dnormed_ref,
    dqkv,
    dmix,
    dcol,
):
    scale = HD ** (-0.5)
    for f in range(FRAMES):
        dmix[f] = low(dot(grad_ref[frame_rows(f), :], wide(right_ref)[:, GROUP:])).T
    for head in range(GROUP // HD):
        query, keys, values = (
            [qkv_ref[0, f, head_features(i, head), :].astype(SINGLE) for f in range(FRAMES)]
            for i in range(3)
        )
        d_keys = [jnp.zeros((HD, SLOTS), SINGLE) for _ in range(FRAMES)]
        d_values = [jnp.zeros((HD, SLOTS), SINGLE) for _ in range(FRAMES)]
        for f in range(FRAMES):
            d_mixed = dmix[f, head_features(0, head), :].astype(SINGLE)
            probs = frame_probs(query[f], keys)
            d_probs = [jnp.sum(d_mixed * value, axis=0, keepdims=True) for value in values]
            row = sum(prob * d_prob for prob, d_prob in zip(probs, d_probs))
            d_query = jnp.zeros((HD, SLOTS), SINGLE)
            for g in range(FRAMES):
                d_score = rounded(probs[g] * (d_probs[g] - row))
                d_query = d_query + d_score * keys[g]
                d_keys[g] = d_keys[g] + d_score * query[f]
                d_values[g] = d_values[g] + rounded(probs[g]) * d_mixed
            dcol[f, head_features(0, head), :] = low(d_query * scale)
        for g in range(FRAMES):
            dcol[g, head_features(1, head), :] = low(d_keys[g] * scale)
            dcol[g, head_features(2, head), :] = low(d_values[g])
    for f in range(FRAMES):
        dqkv[frame_rows(f), :] = dcol[f].T
    finish_backward(normed_ref, grad_ref, left_ref, right_ref, mixed_ref, dweight_ref, dnormed_ref, dqkv)


def finish_backward(
    normed_ref, grad_ref, left_ref, right_ref, mixed_ref, dweight_ref, dnormed_ref, dqkv
):
    dweight_ref[0, :, :QKV] = low(dot(normed_ref[...], dqkv[...], TN))
    dweight_ref[0, :, QKV:] = low(dot(grad_ref[...], mixed_ref[0], TN))
    d_normed = dot(dqkv[:, : 2 * GROUP], wide(left_ref), NT) + dot(
        dqkv[:, 2 * GROUP :], wide(right_ref)[:, :GROUP], NT
    )

    accumulate(dnormed_ref, d_normed)


def lane_pieces(pieces, rows):
    lane = lax.broadcasted_iota(jnp.int32, (rows, HD), 1)
    result = jnp.zeros((rows, HD), SINGLE)
    for number, piece in enumerate(pieces):
        result = jnp.where(lane == number, piece.astype(SINGLE), result)
    return low(result)


def spatial_fwd_kernel(
    normed_ref, left_ref, right_ref, key_extra_ref, qkv_ref, mixed_ref, extra_ref, branch_ref
):
    qkv_ref[0, :, : 2 * GROUP] = low(dot(normed_ref[...], wide(left_ref)))
    qkv_ref[0, :, 2 * GROUP :] = low(dot(normed_ref[...], wide(right_ref)[:, :GROUP]))
    one = jnp.ones((ROWS, 1), SINGLE)
    for head in range(GROUP // HD):
        at = HD * head
        query = qkv_ref[0, :, at : at + HD] * jnp.asarray(HD ** (-0.5), LOWER)
        query = jnp.concatenate([query, lane_pieces([one], ROWS)], axis=1)
        keys = jnp.concatenate(
            [qkv_ref[0, :, GROUP + at : GROUP + at + HD], key_extra_ref[...]], axis=1
        )
        values = jnp.concatenate(
            [qkv_ref[0, :, 2 * GROUP + at : 2 * GROUP + at + HD], lane_pieces([one], ROWS)], axis=1
        )
        score = dot(query, keys, NT)
        top = jnp.max(score, axis=1, keepdims=True)
        mixed = dot(low(jnp.exp(score - top)), values)
        total = mixed[:, HD : HD + 1]
        mixed_ref[0, :, at : at + HD] = low(mixed[:, :HD] / total)
        logsum = -(top + jnp.log(total))
        extra_ref[0, :, at : at + HD] = lane_pieces([one, *three_parts(logsum)], ROWS)
    branch = dot(mixed_ref[0], wide(right_ref)[:, GROUP:], NT)

    accumulate(branch_ref, branch)


def spatial_fwd_last_kernel(
    normed_ref,
    left_ref,
    right_ref,
    key_extra_ref,
    resid_ref,
    branch_ref,
    norms_ref,
    qkv_ref,
    mixed_ref,
    extra_ref,
    out_ref,
    out_normed_ref,
    branch,
):
    spatial_fwd_kernel(
        normed_ref, left_ref, right_ref, key_extra_ref, qkv_ref, mixed_ref, extra_ref, branch
    )

    @pl.when(pl.program_id(0) == 1)
    def _():
        for f in range(FRAMES):
            rows = frame_rows(f)
            value = resid_ref[rows, :] + (branch_ref[rows, :] + branch[rows, :])
            out_ref[rows, :] = value
            out_normed_ref[rows, :] = low(layer_norm(value, norms_ref[4:5, :], norms_ref[5:6, :]))


def spatial_bwd_kernel(
    normed_ref,
    grad_ref,
    left_ref,
    right_ref,
    qkv_ref,
    mixed_ref,
    extra_ref,
    key_extra_ref,
    dweight_ref,
    dnormed_ref,
    dqkv,
):
    scale = HD ** (-0.5)
    d_mixed_all = low(dot(grad_ref[...], wide(right_ref)[:, GROUP:]))
    one = jnp.ones((ROWS, 1), SINGLE)
    for head in range(GROUP // HD):
        at = HD * head
        query = qkv_ref[0, :, at : at + HD]
        query_long = jnp.concatenate(
            [query * jnp.asarray(scale, LOWER), extra_ref[0, :, at : at + HD]], axis=1
        )
        d_mixed = d_mixed_all[:, at : at + HD]
        delta = -jnp.sum(
            d_mixed.astype(SINGLE) * mixed_ref[0, :, at : at + HD].astype(SINGLE),
            axis=1,
            keepdims=True,
        )
        d_mixed_long = jnp.concatenate([d_mixed, lane_pieces(three_parts(delta), ROWS)], axis=1)
        d_query = jnp.zeros((ROWS, HD), SINGLE)
        for part in range(FRAMES):
            rows = slice(SLOTS * part, SLOTS * (part + 1))
            keys = qkv_ref[0, rows, GROUP + at : GROUP + at + HD]
            values = qkv_ref[0, rows, 2 * GROUP + at : 2 * GROUP + at + HD]
            keys_long = jnp.concatenate([keys, key_extra_ref[rows, :]], axis=1)
            values_long = jnp.concatenate(
                [values, lane_pieces([one[rows]] * 3, SLOTS)], axis=1
            )
            prob = jnp.exp(dot(keys_long, query_long, NT))
            d_score = low(prob * dot(values_long, d_mixed_long, NT))
            dqkv[rows, 2 * GROUP + at : 2 * GROUP + at + HD] = low(dot(low(prob), d_mixed))
            dqkv[rows, GROUP + at : GROUP + at + HD] = low(dot(d_score, query) * scale)
            d_query = d_query + dot(d_score, keys, TN)
        dqkv[:, at : at + HD] = low(d_query * scale)
    finish_backward(normed_ref, grad_ref, left_ref, right_ref, mixed_ref, dweight_ref, dnormed_ref, dqkv)


def spatial_bwd_last_kernel(
    normed_ref,
    grad_ref,
    left_ref,
    right_ref,
    qkv_ref,
    mixed_ref,
    extra_ref,
    key_extra_ref,
    resid_ref,
    dresid_ref,
    dother_ref,
    norms_ref,
    dweight_ref,
    drows_ref,
    dnorms_ref,
    dqkv,
    dnormed,
):
    spatial_bwd_kernel(
        normed_ref,
        grad_ref,
        left_ref,
    right_ref,
        qkv_ref,
        mixed_ref,
        extra_ref,
        key_extra_ref,
        dweight_ref,
        dnormed,
        dqkv,
    )

    @pl.when(pl.program_id(0) == 1)
    def _():
        norm_rows_back(
            resid_ref, norms_ref, 2, dother_ref, dnormed, dresid_ref, None, drows_ref, dnorms_ref
        )


def norm_back(value, gain, grad):
    center = value - jnp.mean(value, axis=-1, keepdims=True)
    inverse = lax.rsqrt(jnp.mean(center * center, axis=-1, keepdims=True) + 1e-06)
    hat = center * inverse
    scaled = grad * gain
    d_value = inverse * (
        scaled
        - jnp.mean(scaled, axis=-1, keepdims=True)
        - hat * jnp.mean(scaled * hat, axis=-1, keepdims=True)
    )
    return (
        d_value,
        jnp.sum(grad * hat, axis=0, keepdims=True),
        jnp.sum(grad, axis=0, keepdims=True),
    )


def norm_rows_back(
    resid_ref, norms_ref, at, dother_ref, dnormed_ref, dresid_ref, out_ref, rows_ref, dnorms_ref
):
    d_gain = jnp.zeros((1, resid_ref.shape[1]), SINGLE)
    d_bias = jnp.zeros((1, resid_ref.shape[1]), SINGLE)
    for f in range(FRAMES):
        rows = frame_rows(f)
        d_value, gain, bias = norm_back(
            resid_ref[rows, :],
            norms_ref[at : at + 1, :],
            dother_ref[rows, :] + dnormed_ref[rows, :],
        )
        d_value = d_value + dresid_ref[rows, :]
        if out_ref is not None:
            out_ref[rows, :] = d_value
        rows_ref[rows, :] = low(d_value)
        d_gain, d_bias = d_gain + gain, d_bias + bias
    dnorms_ref[0:1, :] = d_gain
    dnorms_ref[1:2, :] = d_bias


def accumulate(ref, value):
    first = pl.program_id(0) == 0
    ref[...] = jnp.where(first, value, ref[...] + value)


def feed_fwd_kernel(normed_ref, *refs):
    up_refs, down_refs = refs[:2], refs[2:4]
    act_ref, slope_ref, branch_ref = refs[4:]
    hidden = dot(normed_ref[...], wide(*up_refs))
    root = 0.7978845608028654
    square = hidden * hidden
    bend = jnp.tanh(hidden * (root + root * 0.044715 * square))
    half = 0.5 + 0.5 * bend
    act_ref[0] = low(hidden * half)
    slope_ref[0] = low(
        half + hidden * (0.5 - 0.5 * bend * bend) * (root + 3.0 * root * 0.044715 * square)
    )
    accumulate(branch_ref, dot(act_ref[0], wide(*down_refs), NT))


def feed_fwd_last_kernel(normed_ref, *refs):
    resid_ref, branch_ref, norms_ref, valid_ref = refs[4:8]
    act_ref, slope_ref, out_ref, sums_ref, branch = refs[8:]
    feed_fwd_kernel(normed_ref, *refs[:4], act_ref, slope_ref, branch)

    @pl.when(pl.program_id(0) == 1)
    def _():
        sums = jnp.zeros(sums_ref.shape, SINGLE)
        for f in range(FRAMES):
            rows = frame_rows(f)
            value = resid_ref[rows, :] + (branch_ref[rows, :] + branch[rows, :])
            out_ref[rows, :] = value
            normed = layer_norm(value, norms_ref[6:7, :], norms_ref[7:8, :])
            sums = sums + jnp.sum(normed * valid_ref[rows, :], axis=0, keepdims=True)
        sums_ref[...] = sums


def feed_bwd_kernel(normed_ref, grad_ref, *refs):
    up_refs, down_refs = refs[:2], refs[2:4]
    act_ref, slope_ref, dup_ref, ddown_ref, dnormed_ref, dhid = refs[4:]
    dhid[...] = low(dot(grad_ref[...], wide(*down_refs)) * slope_ref[0].astype(SINGLE))
    ddown_ref[0] = low(dot(grad_ref[...], act_ref[0], TN))
    dup_ref[0] = low(dot(normed_ref[...], dhid[...], TN))
    accumulate(dnormed_ref, dot(dhid[...], wide(*up_refs), NT))


def feed_bwd_last_kernel(normed_ref, grad_ref, *refs):
    act_ref, slope_ref, resid_ref, dresid_ref, dother_ref, norms_ref = refs[4:10]
    dup_ref, ddown_ref, out_ref, drows_ref, dnorms_ref, dhid, dnormed = refs[10:]
    feed_bwd_kernel(
        normed_ref, grad_ref, *refs[:4], act_ref, slope_ref, dup_ref, ddown_ref, dnormed, dhid
    )

    @pl.when(pl.program_id(0) == 1)
    def _():
        norm_rows_back(
            resid_ref, norms_ref, 4, dother_ref, dnormed, dresid_ref, out_ref, drows_ref, dnorms_ref
        )


def embed_kernel(patches_ref, weight_ref, valid_ref, norms_ref, start_ref, normed_ref):
    start_ref[...] = dot(patches_ref[...], weight_ref[...]) * valid_ref[...]
    for f in range(FRAMES):
        rows = frame_rows(f)
        normed_ref[rows, :] = low(
            layer_norm(start_ref[rows, :], norms_ref[0:1, :], norms_ref[1:2, :])
        )


def embed_bwd_kernel(
    patches_ref, start_ref, valid_ref, drows_ref, da_ref, db_ref, norms_ref, dnorms_ref, out_ref, dstart
):
    dim = start_ref.shape[1]
    d_gain, d_bias = jnp.zeros((1, dim), SINGLE), jnp.zeros((1, dim), SINGLE)
    for f in range(FRAMES):
        rows = frame_rows(f)
        d_value, gain, bias = norm_back(
            start_ref[rows, :], norms_ref[0:1, :], da_ref[rows, :] + db_ref[rows, :]
        )
        dstart[rows, :] = low((drows_ref[rows, :].astype(SINGLE) + d_value) * valid_ref[rows, :])
        d_gain, d_bias = d_gain + gain, d_bias + bias
    out_ref[:, :dim] = low(dot(patches_ref[...], dstart[...], TN))
    padded = jnp.concatenate(
        [d_gain, d_bias, dnorms_ref[...], jnp.zeros((120, dim), SINGLE)], axis=0
    )
    out_ref[:, dim : dim + 128] = low(padded.T)


def enter_frame_kernel(start_ref, *refs):
    parts, (weight_ref, norms_ref, out_ref, normed_ref, mixed) = refs[:FRAMES], refs[FRAMES:]
    for f in range(FRAMES):
        mixed[frame_rows(f), :] = parts[f][...]
    out_ref[...] = start_ref[...] + dot(mixed[...], weight_ref[...], NT)
    for f in range(FRAMES):
        rows = frame_rows(f)
        normed_ref[rows, :] = low(
            layer_norm(out_ref[rows, :], norms_ref[2:3, :], norms_ref[3:4, :])
        )


def loss_kernel(
    dim,
    classes,
    proj,
    clip_ref,
    facts_ref,
    small_ref,
    resid_ref,
    valid_ref,
    norms_ref,
    loss_ref,
    dsmall_ref,
    pooled_ref,
    dresid_ref,
    drows_ref,
    dnorms_ref,
    dpool,
):
    facts = facts_ref[...]
    count = facts.shape[0]
    label, mate = (facts[:, dim + i : dim + i + 1].astype(jnp.int32) for i in range(2))
    pooled = low(facts[:, :dim] / facts[:, dim + 2 : dim + 3])
    pooled_ref[...] = pooled
    both = dot(pooled, small_ref[...])
    lane = lax.broadcasted_iota(jnp.int32, both.shape, 1)
    logits = jnp.where(lane < classes, both, -1e30)
    hot = (lane == label).astype(SINGLE)
    top = jnp.max(logits, axis=1, keepdims=True)
    raised = jnp.exp(logits - top)
    total = jnp.sum(raised, axis=1, keepdims=True)
    cross = top + jnp.log(total) - jnp.sum(both * hot, axis=1, keepdims=True)
    d_logits = raised / total - hot
    embedding = jnp.where((lane >= classes) & (lane < classes + proj), both, 0.0)
    inverse = lax.rsqrt(jnp.sum(embedding * embedding, axis=1, keepdims=True) + 1e-06)
    unit = embedding * inverse
    exact = functools.partial(
        lax.dot_general, precision=EXACT, preferred_element_type=SINGLE
    )
    similar = exact(unit, unit, NT) / TEMPER
    row = lax.broadcasted_iota(jnp.int32, (count, count), 0)
    col = lax.broadcasted_iota(jnp.int32, (count, count), 1)
    mate_hot = (col == mate).astype(SINGLE)
    masked = jnp.where(row == col, -1e30, similar)
    top = jnp.max(masked, axis=1, keepdims=True)
    raised = jnp.exp(masked - top)
    total = jnp.sum(raised, axis=1, keepdims=True)
    contrast = top + jnp.log(total) - jnp.sum(similar * mate_hot, axis=1, keepdims=True)
    loss_ref[...] = jnp.sum(cross + contrast, axis=0, keepdims=True)
    d_similar = (raised / total - mate_hot) / TEMPER
    d_unit = exact(d_similar, unit, NN) + exact(d_similar, unit, TN)
    d_embed = inverse * d_unit - embedding * (inverse * inverse * inverse) * jnp.sum(
        embedding * d_unit, axis=1, keepdims=True
    )
    dsmall_ref[...] = low(jnp.where(lane < classes, d_logits, d_embed))
    dpool[...] = dot(dsmall_ref[...], small_ref[...], NT) / facts[:, dim + 2 : dim + 3]
    d_pooled = dpool[pl.ds(clip_ref[0], 1), :]
    d_gain, d_bias = jnp.zeros((1, dim), SINGLE), jnp.zeros((1, dim), SINGLE)
    for f in range(FRAMES):
        rows = frame_rows(f)
        d_value, gain, bias = norm_back(
            resid_ref[rows, :], norms_ref[6:7, :], valid_ref[rows, :] * d_pooled
        )
        dresid_ref[rows, :] = d_value
        drows_ref[rows, :] = low(d_value)
        d_gain, d_bias = d_gain + gain, d_bias + bias
    dnorms_ref[0:1, :] = d_gain
    dnorms_ref[1:2, :] = d_bias


def adam_step(master, first, second, clipped, rate):
    first_new = BETA_ONE * first + (1.0 - BETA_ONE) * clipped
    second_new = BETA_TWO * second + (1.0 - BETA_TWO) * clipped * clipped
    first_hat = first_new / (1.0 - BETA_ONE**STEP)
    second_hat = second_new / (1.0 - BETA_TWO**STEP)
    master_new = master - rate * (first_hat / (jnp.sqrt(second_hat) + ADAM_EPS) + DECAY * master)
    return (master_new, first_new, second_new)


def adam_kernel(classes, proj, total_ref, *refs):
    masters, firsts, seconds, parts, outs = (
        refs[0:8], refs[8:16], refs[16:24], refs[24:30], refs[31:]
    )
    norm = jnp.sqrt(total_ref[...])
    refs[30][...] = norm
    factor = jnp.minimum(1.0, CLIP_AT / (norm + 1e-06))
    early, small, first, second, up, down = (ref[...] * factor for ref in parts)
    dim = masters[0].shape[1]
    columns = lambda k: slice(GROUP * k, GROUP * (k + 1))
    todo = [
        (0, ..., early[:, :dim]),
        (1, ..., early[:, dim : dim + 128].T[:8]),
        (2, ..., small[:, :classes]),
        (3, ..., small[:, classes : classes + proj]),
        (6, ..., up),
        (7, ..., down),
    ]
    for layer, grad in enumerate((first, second)):
        todo += [(4, (layer, k), grad[:, columns(k)]) for k in range(3)]
        todo.append((5, layer, grad[:, columns(3)].T))
    for i, at, grad in todo:
        results = adam_step(
            masters[i][at], firsts[i][at], seconds[i][at], grad, NORM_RATE if i == 1 else RATE
        )
        for j, result in enumerate(results):
            outs[3 * i + j][at] = result


def whole(shape):
    return pl.BlockSpec(shape, lambda g: (0,) * len(shape))


def per_group(rows, width):
    return pl.BlockSpec((1, rows, width), lambda g: (g, 0, 0))


def columns_of(width):
    return pl.BlockSpec((1, FRAMES, width, SLOTS), lambda g: (g, 0, 0, 0))


def shaped(*shape, dtype=SINGLE):
    return jax.ShapeDtypeStruct(shape, dtype)


def spec_of(value):
    shape = value.shape
    if len(shape) == 4:
        return columns_of(shape[2])
    return per_group(*shape[1:]) if len(shape) == 3 else whole(shape)


def call(kernel, name, inputs, outputs, scratch=(), gflops=1, steps=2, in_specs=None):
    return pl.pallas_call(
        kernel,
        grid=(steps,),
        in_specs=in_specs or [spec_of(value) for value in inputs],
        out_specs=[spec_of(value) for value in outputs],
        out_shape=list(outputs),
        scratch_shapes=[pltpu.VMEM(shape, dtype) for shape, dtype in scratch],
        compiler_params=pltpu.CompilerParams(vmem_limit_bytes=GRANT),
        cost_estimate=pl.CostEstimate(
            flops=gflops * 10**9, bytes_accessed=8 << 20, transcendentals=0
        ),
        name=name,
    )(*inputs)


def by_group(width, rows=ROWS):
    return shaped(2, rows, width, dtype=LOWER)


def weight_specs(parts, rows):
    inputs, specs = [], []
    for value, half in parts:
        taken = rows
        if rows % 16 != 0:
            value = value[:, :, :rows].reshape(2, 1, -1, value.shape[-1])
            taken = value.shape[2]
        width = value.shape[3] if half is None else value.shape[3] // 2
        inputs.append(value)
        specs.append(
            pl.BlockSpec((1, value.shape[1], taken, width), lambda g, h=half or 0: (g, 0, 0, h))
        )
    return inputs, specs


def with_fetches(kernel, places):
    def wrapped(*refs):
        *refs, sems = refs
        buffers = refs[len(refs) - len(places) :]
        refs = list(refs[: len(refs) - len(places)])
        copies = [
            pltpu.make_async_copy(refs[at], buffer, sems.at[i])
            for i, (at, buffer) in enumerate(zip(places, buffers))
        ]

        @pl.when(pl.program_id(0) == 0)
        def _():
            for copy in copies:
                copy.start()

        @pl.when(pl.program_id(0) == 1)
        def _():
            for copy in copies:
                copy.wait()

        for at, buffer in zip(places, buffers):
            refs[at] = buffer
        kernel(*refs)

    return wrapped


def block_call(kernel, name, before, parts, rows, rest, outputs, scratch, gflops, later=False):
    parts, specs = weight_specs(parts, rows)
    specs = [spec_of(v) for v in before] + specs + [spec_of(v) for v in rest]
    inputs = (*before, *parts, *rest)
    if not later:
        return call(kernel, name, inputs, outputs, scratch, gflops, in_specs=specs)
    places = [
        i
        for i, value in enumerate(inputs)
        if value.dtype == SINGLE and value.shape == (ROWS, inputs[0].shape[1])
    ]
    for at in places:
        specs[at] = pl.BlockSpec(memory_space=pl.ANY)
    scratch = [pltpu.VMEM(shape, dtype) for shape, dtype in scratch]
    scratch += [pltpu.VMEM(inputs[at].shape, SINGLE) for at in places]
    return pl.pallas_call(
        with_fetches(kernel, places),
        grid=(2,),
        in_specs=specs,
        out_specs=[spec_of(value) for value in outputs],
        out_shape=list(outputs),
        scratch_shapes=scratch + [pltpu.SemaphoreType.DMA((len(places),))],
        compiler_params=pltpu.CompilerParams(vmem_limit_bytes=GRANT),
        cost_estimate=pl.CostEstimate(
            flops=gflops * 10**9, bytes_accessed=8 << 20, transcendentals=0
        ),
        name=name,
    )(*inputs)


def temporal_forward(normed, own, other, rows):
    dim = normed.shape[1]
    parts, specs = weight_specs([*own, *other], rows)
    place = [lambda g: jnp.minimum(g, 1)] * 2 + [lambda g: jnp.maximum(g - 2, 0)] * 2
    specs = [
        pl.BlockSpec(spec.block_shape, lambda g, at=at: (at(g), 0, 0, 0))
        for spec, at in zip(specs, place)
    ]
    width = parts[0].shape[3]
    return call(
        temporal_fwd_kernel,
        "temporal_forward",
        (normed, *parts),
        (shaped(4, FRAMES, QKV, SLOTS, dtype=LOWER), shaped(4, ROWS, GROUP, dtype=LOWER)),
        [((FRAMES, GROUP, SLOTS), LOWER), ((dim, width), LOWER), ((dim, width), LOWER)],
        40,
        4,
        [spec_of(normed), *specs],
    )


def temporal_backward(normed, grad, parts, rows, qkv, mixed, skip):
    dim = normed.shape[1]
    parts, specs = weight_specs(parts, rows)
    specs = [spec_of(normed), spec_of(grad), *specs]
    specs += [
        pl.BlockSpec((1, FRAMES, QKV, SLOTS), lambda g: (g + skip, 0, 0, 0)),
        pl.BlockSpec((1, ROWS, GROUP), lambda g: (g + skip, 0, 0)),
    ]
    return call(
        temporal_bwd_kernel,
        "temporal_backward",
        (normed, grad, *parts, qkv, mixed),
        (by_group(dim, dim), shaped(ROWS, dim)),
        [((ROWS, QKV), LOWER), ((FRAMES, GROUP, SLOTS), LOWER), ((FRAMES, QKV, SLOTS), LOWER)],
        14,
        2,
        specs,
    )


def spatial_forward(normed, parts, rows, key_extra, last=None):
    dim = normed.shape[1]
    outputs = (by_group(QKV), by_group(GROUP), by_group(GROUP), shaped(ROWS, dim))
    kernel, scratch = spatial_fwd_kernel, []
    if last is not None:
        kernel, scratch = spatial_fwd_last_kernel, [((ROWS, dim), SINGLE)]
        outputs += (shaped(ROWS, dim, dtype=LOWER),)
    rest = (key_extra, *(last or ()))
    return block_call(
        kernel, "spatial_forward", (normed,), parts, rows, rest, outputs, scratch, 15, last is not None
    )


def spatial_backward(normed, grad, parts, rows, qkv, mixed, extra, key_extra, last=None):
    dim = normed.shape[1]
    kernel, scratch = spatial_bwd_kernel, [((ROWS, QKV), LOWER)]
    outputs = (by_group(dim, dim), shaped(ROWS, dim))
    if last is not None:
        kernel, scratch = spatial_bwd_last_kernel, scratch + [((ROWS, dim), SINGLE)]
        outputs = (by_group(dim, dim), shaped(ROWS, dim, dtype=LOWER), shaped(2, dim))
    rest = (qkv, mixed, extra, key_extra, *(last or ()))
    return block_call(
        kernel, "spatial_backward", (normed, grad), parts, rows, rest, outputs, scratch, 30, last is not None
    )


def feed_forward(normed, parts, rows, last=None):
    dim, width = normed.shape[1], 2 * parts[0][0].shape[3]
    outputs = (by_group(width), by_group(width), shaped(ROWS, dim))
    kernel, scratch = feed_fwd_kernel, []
    if last is not None:
        kernel, scratch = feed_fwd_last_kernel, [((ROWS, dim), SINGLE)]
        outputs += (shaped(1, dim),)
    return block_call(
        kernel, "feed_forward", (normed,), parts, rows, last or (), outputs, scratch, 10, last is not None
    )


def feed_backward(normed, grad, parts, rows, act, slope, last=None):
    dim, width = normed.shape[1], 2 * parts[0][0].shape[3]
    kernel, scratch = feed_bwd_kernel, [((ROWS, width), LOWER)]
    outputs = (by_group(width, dim), by_group(width, dim), shaped(ROWS, dim))
    if last is not None:
        kernel, scratch = feed_bwd_last_kernel, scratch + [((ROWS, dim), SINGLE)]
        outputs += (shaped(ROWS, dim, dtype=LOWER), shaped(2, dim))
    rest = (act, slope, *(last or ()))
    return block_call(
        kernel, "feed_backward", (normed, grad), parts, rows, rest, outputs, scratch, 15, last is not None
    )


def embed(patches, weight, valid, norms):
    dim = patches.shape[1]
    outputs = (shaped(ROWS, dim), shaped(ROWS, dim, dtype=LOWER))
    return call(embed_kernel, "embed", (patches, weight, valid, norms), outputs, (), 15, 1)


def embed_backward(patches, start, valid, d_rows, d_a, d_b, norms, d_norms):
    dim = patches.shape[1]
    return call(
        embed_bwd_kernel,
        "embed_backward",
        (patches, start, valid, d_rows, d_a, d_b, norms, d_norms),
        (shaped(dim, dim + 128, dtype=LOWER),),
        [((ROWS, dim), LOWER)],
        30,
        1,
    )[0]


def enter_frame(start, parts, weight, norms):
    dim = start.shape[1]
    return call(
        enter_frame_kernel,
        "enter_frame",
        (start, *parts, weight, norms),
        (shaped(ROWS, dim), shaped(ROWS, dim, dtype=LOWER)),
        [((ROWS, dim), LOWER)],
        2,
        1,
    )


def all_losses(clip, facts, small, resid, valid, norms, classes, proj):
    count, dim = facts.shape[0], resid.shape[1]
    inputs = (facts, small, resid, valid, norms)
    return call(
        functools.partial(loss_kernel, dim, classes, proj),
        "losses",
        (clip, *inputs),
        (
            shaped(1, 1),
            shaped(count, dim, dtype=LOWER),
            shaped(count, dim, dtype=LOWER),
            shaped(ROWS, dim),
            shaped(ROWS, dim, dtype=LOWER),
            shaped(2, dim),
        ),
        [((count, dim), SINGLE)],
        1,
        1,
        [pl.BlockSpec(memory_space=pltpu.SMEM)] + [whole(value.shape) for value in inputs],
    )


def optimizer(total, masters, firsts, seconds, parts, classes, proj):
    inputs = (total, *masters, *firsts, *seconds, *parts)
    outputs = [shaped(1, 1)] + [shaped(*value.shape) for value in masters for _ in range(3)]
    return pl.pallas_call(
        functools.partial(adam_kernel, classes, proj),
        grid=(1,),
        in_specs=[whole(value.shape) for value in inputs],
        out_specs=[whole(value.shape) for value in outputs],
        out_shape=outputs,
        compiler_params=pltpu.CompilerParams(vmem_limit_bytes=GRANT),
        name="optimizer",
    )(*inputs)


def finish_kernel(count, token_ref, *refs):
    squares = jnp.zeros((1, 1), SINGLE)
    ins, outs = list(refs[: -count - 2]), refs[-count - 2 :]
    per = len(ins) // count
    for i in range(count):
        value = functools.reduce(
            jnp.add, (ref[...].astype(SINGLE) for ref in ins[per * i : per * (i + 1)])
        )
        outs[i][...] = value
        squares = squares + jnp.sum(
            jnp.sum(value * value, axis=1, keepdims=True), axis=0, keepdims=True
        )
    outs[count][...] = squares
    outs[count + 1][...] = token_ref[...]


def finish(token, lists):
    inputs = (token, *(term for terms in lists for term in terms))
    outputs = [shaped(*terms[0].shape) for terms in lists]
    outputs += [shaped(1, 1), shaped(*token.shape)]
    return call(
        functools.partial(finish_kernel, len(lists)),
        "finish",
        inputs,
        outputs,
        (),
        30,
        1,
        [whole(value.shape) for value in inputs],
    )


def pace_kernel(token_ref, out_ref):
    out_ref[...] = token_ref[...]


def pace(token):
    return call(pace_kernel, "pace", (token,), (shaped(*token.shape),), (), 30, 1)[0]


def tick(*values):
    return lax.optimization_barrier(values)


def summed(terms):
    return functools.reduce(jnp.add, (term.astype(SINGLE) for term in terms))


class Cube:
    def __init__(self, sizes):
        self.count = sizes["batch"] * sizes["head"]
        self.mine = lax.axis_index(ALL)
        batch_bits = sizes["batch"].bit_length() - 1
        self.batch_masks = [4 << k for k in reversed(range(batch_bits))]

    def swap(self, value, mask):
        return lax.ppermute(value, ALL, [(i, i ^ mask) for i in range(self.count)])

    def has(self, mask):
        return (self.mine & mask) != 0

    def join(self, value, *masks):
        for mask in masks:
            value = self.merge(value, self.swap(value, mask), mask)
        return value

    def fork(self, value):
        return self.stack(value, self.swap(value, 2), 2)

    def step(self, token, sends, late=(), work=None, hold=None, beside=None):
        values = [value for value, _ in (*sends, *late)]
        count = len(values)
        *values, token = tick(*values, *(hold or ()), token)
        if hold is not None:
            hold[:] = values[count:]
        values = values[:count]
        extra = beside(*hold) if beside is not None else []
        masks = [mask for _, mask in (*sends, *late)]
        received = [self.swap(value, mask) for value, mask in zip(values, masks)]
        count = len(sends)
        if work is not None:
            *done, paced = finish(token, work)
            *ended, token = tick(*received[:count], paced)
            return token, done, *ended, *received[count:]
        results = tick(*received[:count], *extra, pace(token))
        if extra:
            hold[:] = results[count:-1]
        return results[-1], *results[:count], *received[count:]


    def quads(self):
        *_, high, near, _ = self.batch_masks
        return [near, high, near | high]

    def gathered(self, value, others):
        near, high, _ = (self.has(mask) for mask in self.quads())
        p = [value, *others]
        p = [jnp.where(near, p[i ^ 1], p[i]) for i in range(4)]
        p = [jnp.where(high, p[i ^ 2], p[i]) for i in range(4)]
        shape = value.shape
        return jnp.stack(p, axis=-3).reshape(*shape[:-3], 4 * shape[-3], *shape[-2:])

    def quarter(self, terms):
        near, high, _ = (self.has(mask).astype(jnp.int32) for mask in self.quads())
        place = near + 2 * high
        views = [term.reshape(-1, 4, *term.shape[-2:]) for term in terms]
        part = lambda view, r: lax.dynamic_index_in_dim(view, place ^ r, 1, False)
        sends = [low(summed([part(view, r) for view in views])) for r in range(1, 4)]
        return sends, [part(view, 0) for view in views]

    def fourfold(self, sends):
        return list(zip(sends, self.quads()))

    def merge(self, value, other, mask):
        has = self.has(mask)
        both = jnp.stack([jnp.where(has, other, value), jnp.where(has, value, other)], axis=-3)
        shape = value.shape
        return both.reshape(*shape[:-3], 2 * shape[-3], *shape[-2:])

    def stack(self, value, other, mask):
        has = self.has(mask)
        return jnp.stack([jnp.where(has, other, value), jnp.where(has, value, other)])


    def cut(self, terms, mask):
        shape = terms[0].shape
        mine = self.has(mask).astype(jnp.int32)
        pairs = [
            term.reshape(*shape[:-3], shape[-3] // 2, 2, *shape[-2:]) for term in terms
        ]
        half = lambda pair, which: lax.dynamic_index_in_dim(pair, which, pair.ndim - 3, False)
        return low(summed([half(pair, 1 - mine) for pair in pairs])), [
            half(pair, mine) for pair in pairs
        ]

    def shed(self, terms, *masks):
        for mask in masks:
            send, keep = self.cut(terms, mask)
            terms = keep + [self.swap(send, mask)]
        return terms

    def cut_row(self, terms):
        mine = self.has(2).astype(jnp.int32)
        half = lambda term, which: lax.dynamic_index_in_dim(term, which, 0, False)
        return low(summed([half(term, 1 - mine) for term in terms])), [
            half(term, mine) for term in terms
        ]

    def meet(self, terms):
        send, keep = self.cut_row(terms)
        return keep + [self.swap(send, 2)]

    def total(self, value):
        for mask in [1, 2, *self.batch_masks[::-1]]:
            value = value + self.swap(value, mask)
        return value

    def swap_frames(self, parts):
        return [parts[0]] + [self.swap(parts[r], r) for r in range(1, FRAMES)]


def body(sizes, *args):
    patches, bucket, labels, partner = args[:4]
    views = [lambda v: v] * 4 + [
        lambda v: v.transpose(0, 2, 1, 3), lambda v: v, lambda v: v, lambda v: v.T
    ]
    masters, firsts, seconds = (
        [view(value) for view, value in zip(views, args[4 + 8 * i : 12 + 8 * i])] for i in range(3)
    )
    patch_weight, norm_params, head_weight, proj_weight, attn_in, attn_out, up, down = masters
    cube = Cube(sizes)
    dim = norm_params.shape[1] * cube.count
    classes, proj = head_weight.shape[1], proj_weight.shape[1]
    rows_wide, rows_small = attn_in.shape[2], patch_weight.shape[0]
    place = lax.axis_index(HEAD)

    *first, near, last = cube.batch_masks
    middle = dim // 2
    blocked = lambda value: value.reshape(*value.shape[:-2], -1, rows_wide, value.shape[-1])
    pack = lambda w_in, w_out: jnp.concatenate(
        [low(w_in[0]), low(w_in[1]), low(w_in[2]), low(w_out).T], axis=1
    )[None]
    patch_count = jnp.where(bucket == 1, PMAX, PSMALL)
    offset = jnp.arange(SLOTS)[None, :]
    number = (place ^ jnp.arange(FRAMES))[:, None]
    frame_valid = ((number * SLOTS + offset) < patch_count).reshape(ROWS, 1).astype(SINGLE)
    slot_valid = (jnp.broadcast_to(place * SLOTS + offset, (FRAMES, SLOTS)) < patch_count).reshape(
        ROWS, 1
    ).astype(SINGLE)
    lane = jnp.arange(HD)[None, :]
    key_extra = low(
        jnp.where(lane == 0, jnp.where(frame_valid > 0, 0.0, -1e30), (lane < 4).astype(SINGLE))
    )

    extra = -(-(rows_small + 1) // 16) * 16
    norm_row = low(norm_params).reshape(1, -1)
    first_w = jnp.concatenate(
        [
            pack(attn_in[0], attn_out[0])[0],
            low(patch_weight),
            jnp.pad(norm_row, ((0, extra - rows_small - 1), (0, dim - norm_row.shape[1]))),
        ]
    )[None]
    token = jnp.zeros((8, 128), SINGLE)
    clip, w_in, w_out, w_up, w_down = patches[0], attn_in[1], attn_out[1], up, down
    for mask in first:
        first_w, clip, w_in, w_out, w_up, w_down = tick(first_w, clip, w_in, w_out, w_up, w_down)
        token, other = cube.step(token, [(first_w, mask)])
        first_w = cube.merge(first_w, other, mask)
    blocks = jnp.pad(clip, ((0, ROWS - PMAX), (0, 0))).reshape(FRAMES, SLOTS, -1)
    blocks = jnp.where((place & 1) != 0, blocks[jnp.array([1, 0, 3, 2])], blocks)
    blocks = jnp.where((place & 2) != 0, blocks[jnp.array([2, 3, 0, 1])], blocks)
    blocks, token = tick(blocks, token)
    second_w = jnp.concatenate([pack(w_in, w_out)[0], low(w_up)])[None]
    small = jnp.concatenate([low(head_weight), low(proj_weight)], axis=1)
    small = jnp.pad(small, ((0, -rows_small % 16), (0, dim - small.shape[1])))
    down_w = jnp.concatenate([low(w_down), small])[None]

    token, other, *slots = cube.step(
        token, [(first_w, near)] + [(blocks[r], r) for r in range(1, FRAMES)]
    )
    first_w = cube.merge(first_w, other, near)
    by_frame = blocks.reshape(ROWS, -1)

    left, right = first_w[..., :middle], first_w[..., middle:]
    second_w = cube.join(second_w, *first[:-1])
    token, other_left, other_right, *others = cube.step(
        token, [(left, last), (right, 2)], cube.fourfold([second_w] * 3)
    )
    left, right = cube.merge(left, other_left, last), cube.stack(right, other_right, 2)

    left, right, *slots = tick(left, right, *slots)
    by_slot = jnp.concatenate([blocks[0], *slots])
    token, other_left, other_right = cube.step(token, [(left, 2), (right, last)])
    by_slot, slot_valid, token, *others = tick(by_slot, slot_valid, token, *others)
    own_first = (cube.stack(left, other_left, 2), cube.merge(right, other_right, last))

    second_w = cube.gathered(second_w, others)
    token, *other_first, other_left, other_right, other = cube.step(
        token,
        [(own_first[0], 1), (own_first[1], 1)],
        [(second_w[..., :middle], last), (second_w[..., middle:], 2)]
        + [(down_w, mask) for mask in first[:1]],
    )
    other_down = other
    joined = lambda parts, at: jnp.concatenate([part[:, :, at] for part in parts], axis=-1)
    early = [joined(parts, slice(rows_wide, None)) for parts in (own_first, other_first)]
    early = cube.stack(*early, 1).transpose(2, 1, 0, 3, 4)
    patch_copy = early[..., :rows_small, :].reshape(dim, dim)
    norms = early[..., rows_small, : norm_row.shape[1]].reshape(-1, 8, rows_small)
    norms = norms.transpose(1, 0, 2).reshape(8, dim).astype(SINGLE)
    start_slot, normed_t = embed(by_slot, patch_copy, slot_valid, norms)
    normed_t, other_left, other_right = tick(normed_t, other_left, other_right)
    left = cube.merge(second_w[..., :middle], other_left, last)
    right = cube.stack(second_w[..., middle:], other_right, 2)
    ours, theirs = slice(0, rows_wide), slice(rows_wide, None)
    other_left, other_right = (
        cube.swap(left[..., ours, :], 2), cube.swap(right[..., ours, :], last)
    )
    first_w = tuple([(part, None) for part in parts] for parts in (own_first, other_first))
    qkv_t, mixed_t = temporal_forward(normed_t, *first_w, rows_wide)
    mixed_t, other_left, other_right, other_down = tick(
        mixed_t, other_left, other_right, other_down
    )
    parts = [
        jnp.concatenate(
            [mixed_t[2 * (c ^ (r & 1)) + y][frame_rows(r)] for c in range(2) for y in range(2)],
            axis=1,
        )
        for r in range(FRAMES)
    ]
    down_w = cube.join(cube.merge(down_w, other_down, first[0]), *first[1:])

    hold = [other_left, other_right, patch_copy]
    token, *received, other = cube.step(
        token, [(parts[r], r) for r in range(1, FRAMES)] + [(down_w, near)], hold=hold
    )
    other_left, other_right, patch_copy = hold
    outs = [
        part[y, :, :rows_wide, GROUP:].reshape(dim, GROUP)
        for part in (own_first[1], other_first[1])
        for y in range(2)
    ]
    out_first = jnp.concatenate(outs, axis=1)
    start_frame = dot(by_frame, patch_copy) * frame_valid
    own_second = jnp.concatenate(
        [
            cube.stack(left[..., ours, :], other_left, 2),
            cube.merge(right[..., ours, :], other_right, last),
        ],
        axis=-1,
    )
    down_w = cube.merge(down_w, other, near)
    key_extra, own_second, down_w, out_first, start_frame = tick(
        key_extra, own_second, down_w, out_first, start_frame
    )

    resid_one, normed_s = enter_frame(start_frame, [parts[0], *received], out_first, norms)
    other_second = cube.swap(own_second, 1)
    other_left = cube.swap(left[..., theirs, :], 2)
    other_right = cube.swap(right[..., theirs, :], last)
    left_down, right_down = cube.join(down_w[..., :middle], last), cube.fork(down_w[..., middle:])
    qkv_s, mixed_s, extra_s = ([None, None] for _ in range(3))
    halves = lambda value: [(value, 0), (value, 1)]
    qkv_s[0], mixed_s[0], extra_s[0], branch = spatial_forward(
        normed_s, halves(own_second), rows_wide, key_extra
    )
    branch, normed_s, other_second, other_left, other_right, left_down, right_down = tick(
        branch, normed_s, other_second, other_left, other_right, left_down, right_down
    )
    own_up = (
        cube.stack(left[..., theirs, :], other_left, 2),
        cube.merge(right[..., theirs, :], other_right, last),
    )
    other_up = [cube.swap(part, 1) for part in own_up]
    left, right = cube.fork(left_down), cube.join(right_down, last)
    qkv_s[1], mixed_s[1], extra_s[1], resid_two, normed_m = spatial_forward(
        normed_s, halves(other_second), rows_wide, key_extra, (resid_one, branch, norms)
    )
    normed_m, left, right, *other_up = tick(normed_m, left, right, *other_up)

    own_down, other_down = (left, right), (cube.swap(left, 1), cube.swap(right, 1))
    own_feed = [(part, None) for part in (*own_up, *own_down)]
    other_feed = [(part, None) for part in (*other_up, *other_down)]
    act, slope = ([None, None] for _ in range(2))
    act[0], slope[0], branch = feed_forward(normed_m, own_feed, rows_wide)
    act[1], slope[1], resid_three, sums = feed_forward(
        normed_m, other_feed, rows_wide, (resid_two, branch, norms, frame_valid)
    )
    small = [
        joined(parts, slice(rows_wide, rows_wide + rows_small)) for parts in (own_down, other_down)
    ]
    small = cube.stack(*small, 1).transpose(2, 1, 0, 3, 4).reshape(dim, dim)

    for mask in (1, 2):
        sums = sums + cube.swap(sums, mask)
    facts = jnp.stack([labels[0], partner[0], FRAMES * patch_count[0]]).astype(SINGLE)
    gathered = jnp.concatenate([sums, jnp.pad(facts, (0, 125))[None]], axis=1)[None]
    gathered = cube.join(gathered, *first[:-1])
    others = [cube.swap(gathered, mask) for mask in cube.quads()]
    gathered = cube.join(cube.gathered(gathered, others), last)[:, 0]
    clip = lax.axis_index("batch").reshape(1)
    loss_sum, d_small, pooled_low, d_resid, d_rows, d_norms_f = all_losses(
        clip, gathered, small, resid_three, frame_valid, norms, classes, proj
    )

    d_up, d_down = [None, None], [None, None]
    d_up[1], d_down[1], d_normed = feed_backward(
        normed_m, d_rows, other_feed, rows_wide, act[1], slope[1]
    )
    up_other, down_other, d_normed, d_rows, normed_m = tick(
        d_up[1], d_down[1], d_normed, d_rows, normed_m
    )
    core_up, core_down = cube.swap(up_other, 1), cube.swap(down_other, 1)
    d_up[0], d_down[0], d_resid, d_rows, d_norms_m = feed_backward(
        normed_m,
        d_rows,
        own_feed,
        rows_wide,
        act[0],
        slope[0],
        (resid_two, d_resid, d_normed, norms),
    )
    d_resid, d_rows, up_own, down_own, core_up, core_down = tick(
        d_resid, d_rows, d_up[0], d_down[0], core_up, core_down
    )

    sum_up = cube.meet([blocked(up_own), blocked(core_up)])
    sum_down = cube.shed([blocked(down_own), blocked(core_down)], last)
    d_second = [None, None]
    d_second[1], d_normed = spatial_backward(
        normed_s, d_rows, halves(other_second), rows_wide, qkv_s[1], mixed_s[1], extra_s[1], key_extra
    )
    d_small = lax.dynamic_slice_in_dim(
        dot(pooled_low, d_small, TN), cube.mine * rows_small, rows_small, 0
    )
    second_other, d_normed, d_rows, normed_s, sum_up[-1], sum_down[-1], d_small = tick(
        d_second[1], d_normed, d_rows, normed_s, sum_up[-1], sum_down[-1], d_small
    )
    core_second = cube.swap(second_other, 1)
    sum_up, sum_down = cube.shed(sum_up, last), cube.meet(sum_down)
    d_second[0], d_rows, d_norms_s = spatial_backward(
        normed_s,
        d_rows,
        halves(own_second),
        rows_wide,
        qkv_s[0],
        mixed_s[0],
        extra_s[0],
        key_extra,
        (resid_one, d_resid, d_normed, norms),
    )
    d_rows, second_own, sum_up[-1], sum_down[-1], core_second = tick(
        d_rows, d_second[0], sum_up[-1], sum_down[-1], core_second
    )

    parts = split_frames(d_rows)
    send, sum_second = cube.cut([blocked(second_own), blocked(core_second)], last)
    def to_quarters(up_last, down_last):
        up, down = sum_up[:-1] + [up_last], sum_down[:-1] + [down_last]
        up, down = cube.shed(up, *first[-2::-1]), cube.shed(down, *first[-2::-1])
        kept.extend([cube.quarter(up)[1], cube.quarter(down)[1]])
        pairs = zip(cube.quarter(up)[0], cube.quarter(down)[0])
        return [jnp.concatenate(pair, axis=-2) for pair in pairs]

    kept, hold = [], [sum_up[-1], sum_down[-1]]
    token, *received, other = cube.step(
        token,
        [(parts[r], r) for r in range(1, FRAMES)],
        [(send, last)],
        hold=hold,
        beside=to_quarters,
    )
    sends, (sum_up, sum_down) = hold, kept
    d_rows = jnp.concatenate([parts[0], *received])
    sum_second.append(other)

    others = [cube.swap(send, mask) for send, mask in cube.fourfold(sends)]
    d_first, d_normed = [None, None], [None, None]
    d_first[1], d_normed[1] = temporal_backward(
        normed_t, d_rows, first_w[1], rows_wide, qkv_t, mixed_t, 2
    )
    first_other, d_normed[1], d_rows, normed_t, sum_second[-1] = tick(
        d_first[1], d_normed[1], d_rows, normed_t, sum_second[-1]
    )
    core_first = cube.swap(first_other, 1)
    sum_second = cube.meet(sum_second)
    d_first[0], d_normed[0] = temporal_backward(
        normed_t, d_rows, first_w[0], rows_wide, qkv_t, mixed_t, 0
    )
    d_rows, first_own, d_normed[0], core_first, sum_second[-1], *others = tick(
        d_rows, d_first[0], d_normed[0], core_first, sum_second[-1], *others
    )
    sum_up += [other[..., :rows_wide, :] for other in others]
    sum_down += [other[..., rows_wide:, :] for other in others]

    sum_first = [blocked(first_own), blocked(core_first)]
    send_left, left = cube.cut_row([term[..., :middle] for term in sum_first])
    send_right, right = cube.cut([term[..., middle:] for term in sum_first], last)
    sum_second = cube.shed(sum_second, *first[-2::-1])
    send_left, send_right, d_normed[0], d_norms_f, d_small, sum_second[-1] = tick(
        send_left, send_right, d_normed[0], d_norms_f, d_small, sum_second[-1]
    )
    other_left, other_right = cube.swap(send_left, 2), cube.swap(send_right, last)
    sends, sum_second = cube.quarter(sum_second)
    others = [cube.swap(send, mask) for send, mask in cube.fourfold(sends)]
    d_norms = jnp.concatenate([d_norms_s, d_norms_m, d_norms_f])
    d_early = embed_backward(
        by_slot, start_slot, slot_valid, d_rows, d_normed[0], d_normed[1], norms, d_norms
    )
    send, sum_early = cube.cut([d_early.reshape(-1, rows_small, dim + 128)], 1)
    other_left, other_right, send, token = tick(other_left, other_right, send, token)
    other = cube.swap(send, 1)
    left.append(other_left)
    right.append(other_right)
    sum_early.append(other)

    send_left, left = cube.cut(left, last)
    send_right, right = cube.cut_row(right)
    send, sum_early = cube.cut(sum_early, 2)
    flat = lambda terms: [summed(terms)[0]]
    token, other_left, other_right, other = cube.step(
        token, [(send_left, last), (send_right, 2), (send, 2)]
    )
    *others, token = tick(*others, token)
    sum_second += others
    sum_first = [jnp.concatenate([summed(left + [other_left]), summed(right + [other_right])], -1)]
    sum_early.append(other)

    sum_first = cube.shed(sum_first, *first[-2::-1])
    sends, sum_first = cube.quarter(sum_first)
    send, sum_early = cube.cut(sum_early, last)
    token, (d_second, d_up, d_down, squares), *others, other = cube.step(
        token,
        [*cube.fourfold(sends), (send, last)],
        work=[flat(terms) for terms in (sum_second, sum_up, sum_down)],
    )
    sum_first += others
    sum_early.append(other)

    sum_early = cube.shed(sum_early, *first[-2::-1])
    sends, sum_early = cube.quarter(sum_early)
    square = lambda value: jnp.sum(value * value)
    d_first = summed(sum_first)[0]
    token, *others = cube.step(token, cube.fourfold(sends))
    d_early = summed(sum_early + others)[0]
    squares = squares[0, 0] + square(d_small) + square(d_first)

    total = cube.total((squares + square(d_early)).reshape(1, 1))
    parts = (d_early, d_small, d_first, d_second, d_up, d_down)
    grad_norm, *updates = optimizer(total, masters, firsts, seconds, parts, classes, proj)
    updates = [views[i // 3](update) for i, update in enumerate(updates)]
    return (loss_sum[0, 0], grad_norm[0, 0], *updates)


def solution(mesh):
    sizes = dict(mesh.shape)
    split = Mesh(mesh.devices.reshape(sizes["batch"], 2, sizes["head"] // 2), ALL)
    placed = (
        P("batch", HEAD, None),
        P("batch"),
        P("batch"),
        P("batch"),
        P(ALL, None),
        P(None, ALL),
        P(ALL, None),
        P(ALL, None),
        P(None, "batch", None, HEAD),
        P(None, HEAD, "batch"),
        P("batch", HEAD),
        P(HEAD, "batch"),
        P(ALL, None),
        P(None, ALL),
        P(ALL, None),
        P(ALL, None),
        P(None, "batch", None, HEAD),
        P(None, HEAD, "batch"),
        P("batch", HEAD),
        P(HEAD, "batch"),
        P(ALL, None),
        P(None, ALL),
        P(ALL, None),
        P(ALL, None),
        P(None, "batch", None, HEAD),
        P(None, HEAD, "batch"),
        P("batch", HEAD),
        P(HEAD, "batch"),
    )
    return jax.shard_map(
        functools.partial(body, sizes),
        mesh=split,
        in_specs=placed,
        out_specs=(
            P(),
            P(),
            P(ALL, None),
            P(ALL, None),
            P(ALL, None),
            P(None, ALL),
            P(None, ALL),
            P(None, ALL),
            P(ALL, None),
            P(ALL, None),
            P(ALL, None),
            P(ALL, None),
            P(ALL, None),
            P(ALL, None),
            P(None, "batch", None, HEAD),
            P(None, "batch", None, HEAD),
            P(None, "batch", None, HEAD),
            P(None, HEAD, "batch"),
            P(None, HEAD, "batch"),
            P(None, HEAD, "batch"),
            P("batch", HEAD),
            P("batch", HEAD),
            P("batch", HEAD),
            P(HEAD, "batch"),
            P(HEAD, "batch"),
            P(HEAD, "batch"),
        ),
        check_vma=False,
    )
```

```python
import functools

import jax
import jax.numpy as jnp
from jax import lax
from jax.experimental import pallas as pl
from jax.experimental.pallas import tpu as pltpu
from jax.sharding import Mesh
from jax.sharding import PartitionSpec as P

HD = 64
FRAMES = 4
PMAX = 784
PSMALL = 196
STEP = 5
SLOTS = 208
ROWS = FRAMES * SLOTS
GROUP = 192
QKV = 3 * GROUP


EXACT = lax.Precision.HIGHEST
TEMPER = 0.05
BETA_ONE = 0.5
BETA_TWO = 0.5
RATE = 0.04
NORM_RATE = 0.3
DECAY = 0.05
ADAM_EPS = 1e-08
CLIP_AT = 1.0
LOWER = jnp.bfloat16
SINGLE = jnp.float32
ALL = ("batch", "row", "core")
HEAD = ("row", "core")
GRANT = 56 << 20

NN = (((1,), (0,)), ((), ()))
NT = (((1,), (1,)), ((), ()))
TN = (((0,), (0,)), ((), ()))


def dot(left, right, dims=NN):
    return lax.dot_general(left, right, dims, preferred_element_type=SINGLE)


def low(value):
    return value.astype(LOWER)


def layer_norm(value, gain, bias):
    center = value - jnp.mean(value, axis=-1, keepdims=True)
    spread = jnp.mean(center * center, axis=-1, keepdims=True)
    return center * lax.rsqrt(spread + 1e-06) * gain + bias


def wide(*refs):
    return jnp.concatenate([ref[0].reshape(-1, ref.shape[-1]) for ref in refs], axis=1)


def three_parts(value):
    high = low(value)
    rest = value - high.astype(SINGLE)
    middle = low(rest)
    return high, middle, low(rest - middle.astype(SINGLE))


def frame_probs(query, keys):
    scores = [jnp.sum(query * key, axis=0, keepdims=True) * HD ** (-0.5) for key in keys]
    top = functools.reduce(jnp.maximum, scores)
    raised = [jnp.exp(score - top) for score in scores]
    total = functools.reduce(jnp.add, raised)
    return [value / total for value in raised]


def rounded(value):
    return low(value).astype(SINGLE)


def frame_rows(f):
    return slice(SLOTS * f, SLOTS * (f + 1))


def split_frames(rows):
    return [rows[frame_rows(f)] for f in range(FRAMES)]


def head_features(which, head):
    return slice(GROUP * which + HD * head, GROUP * which + HD * (head + 1))


def temporal_fwd_kernel(
    normed_ref, own_left, own_right, other_left, other_right, qkv_ref, mixed_ref, out, left, right
):
    for chosen, parts in (
        (pl.program_id(0) < 2, (own_left, own_right)),
        (pl.program_id(0) >= 2, (other_left, other_right)),
    ):

        @pl.when(chosen)
        def _(parts=parts):
            left[...], right[...] = wide(parts[0]), wide(parts[1])

    for f in range(FRAMES):
        rows = normed_ref[frame_rows(f), :]
        qkv_ref[0, f, : 2 * GROUP, :] = low(dot(rows, left[...])).T
        qkv_ref[0, f, 2 * GROUP :, :] = low(dot(rows, right[:, :GROUP])).T
    for head in range(GROUP // HD):
        query, keys, values = (
            [qkv_ref[0, f, head_features(i, head), :].astype(SINGLE) for f in range(FRAMES)]
            for i in range(3)
        )
        for f in range(FRAMES):
            probs = frame_probs(query[f], keys)
            mixed = sum(rounded(prob) * value for prob, value in zip(probs, values))
            out[f, head_features(0, head), :] = low(mixed)
    for f in range(FRAMES):
        mixed_ref[0, frame_rows(f), :] = out[f].T


def temporal_bwd_kernel(
    normed_ref,
    grad_ref,
    left_ref,
    right_ref,
    qkv_ref,
    mixed_ref,
    dweight_ref,
    dnormed_ref,
    dqkv,
    dmix,
    dcol,
):
    scale = HD ** (-0.5)
    for f in range(FRAMES):
        dmix[f] = low(dot(grad_ref[frame_rows(f), :], wide(right_ref)[:, GROUP:])).T
    for head in range(GROUP // HD):
        query, keys, values = (
            [qkv_ref[0, f, head_features(i, head), :].astype(SINGLE) for f in range(FRAMES)]
            for i in range(3)
        )
        d_keys = [jnp.zeros((HD, SLOTS), SINGLE) for _ in range(FRAMES)]
        d_values = [jnp.zeros((HD, SLOTS), SINGLE) for _ in range(FRAMES)]
        for f in range(FRAMES):
            d_mixed = dmix[f, head_features(0, head), :].astype(SINGLE)
            probs = frame_probs(query[f], keys)
            d_probs = [jnp.sum(d_mixed * value, axis=0, keepdims=True) for value in values]
            row = sum(prob * d_prob for prob, d_prob in zip(probs, d_probs))
            d_query = jnp.zeros((HD, SLOTS), SINGLE)
            for g in range(FRAMES):
                d_score = rounded(probs[g] * (d_probs[g] - row))
                d_query = d_query + d_score * keys[g]
                d_keys[g] = d_keys[g] + d_score * query[f]
                d_values[g] = d_values[g] + rounded(probs[g]) * d_mixed
            dcol[f, head_features(0, head), :] = low(d_query * scale)
        for g in range(FRAMES):
            dcol[g, head_features(1, head), :] = low(d_keys[g] * scale)
            dcol[g, head_features(2, head), :] = low(d_values[g])
    for f in range(FRAMES):
        dqkv[frame_rows(f), :] = dcol[f].T
    finish_backward(normed_ref, grad_ref, left_ref, right_ref, mixed_ref, dweight_ref, dnormed_ref, dqkv)


def finish_backward(
    normed_ref, grad_ref, left_ref, right_ref, mixed_ref, dweight_ref, dnormed_ref, dqkv
):
    dweight_ref[0, :, :QKV] = low(dot(normed_ref[...], dqkv[...], TN))
    dweight_ref[0, :, QKV:] = low(dot(grad_ref[...], mixed_ref[0], TN))
    d_normed = dot(dqkv[:, : 2 * GROUP], wide(left_ref), NT) + dot(
        dqkv[:, 2 * GROUP :], wide(right_ref)[:, :GROUP], NT
    )

    accumulate(dnormed_ref, d_normed)


def lane_pieces(pieces, rows):
    lane = lax.broadcasted_iota(jnp.int32, (rows, HD), 1)
    result = jnp.zeros((rows, HD), SINGLE)
    for number, piece in enumerate(pieces):
        result = jnp.where(lane == number, piece.astype(SINGLE), result)
    return low(result)


def spatial_fwd_kernel(
    normed_ref, left_ref, right_ref, key_extra_ref, qkv_ref, mixed_ref, extra_ref, branch_ref
):
    qkv_ref[0, :, : 2 * GROUP] = low(dot(normed_ref[...], wide(left_ref)))
    qkv_ref[0, :, 2 * GROUP :] = low(dot(normed_ref[...], wide(right_ref)[:, :GROUP]))
    one = jnp.ones((ROWS, 1), SINGLE)
    for head in range(GROUP // HD):
        at = HD * head
        query = qkv_ref[0, :, at : at + HD] * jnp.asarray(HD ** (-0.5), LOWER)
        query = jnp.concatenate([query, lane_pieces([one], ROWS)], axis=1)
        keys = jnp.concatenate(
            [qkv_ref[0, :, GROUP + at : GROUP + at + HD], key_extra_ref[...]], axis=1
        )
        values = jnp.concatenate(
            [qkv_ref[0, :, 2 * GROUP + at : 2 * GROUP + at + HD], lane_pieces([one], ROWS)], axis=1
        )
        score = dot(query, keys, NT)
        top = jnp.max(score, axis=1, keepdims=True)
        mixed = dot(low(jnp.exp(score - top)), values)
        total = mixed[:, HD : HD + 1]
        mixed_ref[0, :, at : at + HD] = low(mixed[:, :HD] / total)
        logsum = -(top + jnp.log(total))
        extra_ref[0, :, at : at + HD] = lane_pieces([one, *three_parts(logsum)], ROWS)
    branch = dot(mixed_ref[0], wide(right_ref)[:, GROUP:], NT)

    accumulate(branch_ref, branch)


def spatial_fwd_last_kernel(
    normed_ref,
    left_ref,
    right_ref,
    key_extra_ref,
    resid_ref,
    branch_ref,
    norms_ref,
    qkv_ref,
    mixed_ref,
    extra_ref,
    out_ref,
    out_normed_ref,
    branch,
):
    spatial_fwd_kernel(
        normed_ref, left_ref, right_ref, key_extra_ref, qkv_ref, mixed_ref, extra_ref, branch
    )

    @pl.when(pl.program_id(0) == 1)
    def _():
        for f in range(FRAMES):
            rows = frame_rows(f)
            value = resid_ref[rows, :] + (branch_ref[rows, :] + branch[rows, :])
            out_ref[rows, :] = value
            out_normed_ref[rows, :] = low(layer_norm(value, norms_ref[4:5, :], norms_ref[5:6, :]))


def spatial_bwd_kernel(
    normed_ref,
    grad_ref,
    left_ref,
    right_ref,
    qkv_ref,
    mixed_ref,
    extra_ref,
    key_extra_ref,
    dweight_ref,
    dnormed_ref,
    dqkv,
):
    scale = HD ** (-0.5)
    d_mixed_all = low(dot(grad_ref[...], wide(right_ref)[:, GROUP:]))
    one = jnp.ones((ROWS, 1), SINGLE)
    for head in range(GROUP // HD):
        at = HD * head
        query = qkv_ref[0, :, at : at + HD]
        query_long = jnp.concatenate(
            [query * jnp.asarray(scale, LOWER), extra_ref[0, :, at : at + HD]], axis=1
        )
        d_mixed = d_mixed_all[:, at : at + HD]
        delta = -jnp.sum(
            d_mixed.astype(SINGLE) * mixed_ref[0, :, at : at + HD].astype(SINGLE),
            axis=1,
            keepdims=True,
        )
        d_mixed_long = jnp.concatenate([d_mixed, lane_pieces(three_parts(delta), ROWS)], axis=1)
        keys = qkv_ref[0, :, GROUP + at : GROUP + at + HD]
        values = qkv_ref[0, :, 2 * GROUP + at : 2 * GROUP + at + HD]
        keys_long = jnp.concatenate([keys, key_extra_ref[...]], axis=1)
        values_long = jnp.concatenate([values, lane_pieces([one] * 3, ROWS)], axis=1)
        prob = jnp.exp(dot(keys_long, query_long, NT))
        d_score = low(prob * dot(values_long, d_mixed_long, NT))
        dqkv[:, 2 * GROUP + at : 2 * GROUP + at + HD] = low(dot(low(prob), d_mixed))
        dqkv[:, GROUP + at : GROUP + at + HD] = low(dot(d_score, query) * scale)
        dqkv[:, at : at + HD] = low(dot(d_score, keys, TN) * scale)
    finish_backward(normed_ref, grad_ref, left_ref, right_ref, mixed_ref, dweight_ref, dnormed_ref, dqkv)


def spatial_bwd_last_kernel(
    normed_ref,
    grad_ref,
    left_ref,
    right_ref,
    qkv_ref,
    mixed_ref,
    extra_ref,
    key_extra_ref,
    resid_ref,
    dresid_ref,
    dother_ref,
    norms_ref,
    dweight_ref,
    drows_ref,
    dnorms_ref,
    dqkv,
    dnormed,
):
    spatial_bwd_kernel(
        normed_ref,
        grad_ref,
        left_ref,
    right_ref,
        qkv_ref,
        mixed_ref,
        extra_ref,
        key_extra_ref,
        dweight_ref,
        dnormed,
        dqkv,
    )

    @pl.when(pl.program_id(0) == 1)
    def _():
        norm_rows_back(
            resid_ref, norms_ref, 2, dother_ref, dnormed, dresid_ref, None, drows_ref, dnorms_ref
        )


def norm_back(value, gain, grad):
    center = value - jnp.mean(value, axis=-1, keepdims=True)
    inverse = lax.rsqrt(jnp.mean(center * center, axis=-1, keepdims=True) + 1e-06)
    hat = center * inverse
    scaled = grad * gain
    d_value = inverse * (
        scaled
        - jnp.mean(scaled, axis=-1, keepdims=True)
        - hat * jnp.mean(scaled * hat, axis=-1, keepdims=True)
    )
    return (
        d_value,
        jnp.sum(grad * hat, axis=0, keepdims=True),
        jnp.sum(grad, axis=0, keepdims=True),
    )


def norm_rows_back(
    resid_ref, norms_ref, at, dother_ref, dnormed_ref, dresid_ref, out_ref, rows_ref, dnorms_ref
):
    d_gain = jnp.zeros((1, resid_ref.shape[1]), SINGLE)
    d_bias = jnp.zeros((1, resid_ref.shape[1]), SINGLE)
    for f in range(FRAMES):
        rows = frame_rows(f)
        d_value, gain, bias = norm_back(
            resid_ref[rows, :],
            norms_ref[at : at + 1, :],
            dother_ref[rows, :] + dnormed_ref[rows, :],
        )
        d_value = d_value + dresid_ref[rows, :]
        if out_ref is not None:
            out_ref[rows, :] = d_value
        rows_ref[rows, :] = low(d_value)
        d_gain, d_bias = d_gain + gain, d_bias + bias
    dnorms_ref[0:1, :] = d_gain
    dnorms_ref[1:2, :] = d_bias


def accumulate(ref, value):
    first = pl.program_id(0) == 0
    ref[...] = jnp.where(first, value, ref[...] + value)


def feed_fwd_kernel(normed_ref, *refs):
    up_refs, down_refs = refs[:2], refs[2:4]
    act_ref, slope_ref, branch_ref = refs[4:]
    hidden = dot(normed_ref[...], wide(*up_refs))
    root = 0.7978845608028654
    square = hidden * hidden
    bend = jnp.tanh(hidden * (root + root * 0.044715 * square))
    half = 0.5 + 0.5 * bend
    act_ref[0] = low(hidden * half)
    slope_ref[0] = low(
        half + hidden * (0.5 - 0.5 * bend * bend) * (root + 3.0 * root * 0.044715 * square)
    )
    accumulate(branch_ref, dot(act_ref[0], wide(*down_refs), NT))


def feed_fwd_last_kernel(normed_ref, *refs):
    resid_ref, branch_ref, norms_ref, valid_ref = refs[4:8]
    act_ref, slope_ref, out_ref, sums_ref, branch = refs[8:]
    feed_fwd_kernel(normed_ref, *refs[:4], act_ref, slope_ref, branch)

    @pl.when(pl.program_id(0) == 1)
    def _():
        sums = jnp.zeros(sums_ref.shape, SINGLE)
        for f in range(FRAMES):
            rows = frame_rows(f)
            value = resid_ref[rows, :] + (branch_ref[rows, :] + branch[rows, :])
            out_ref[rows, :] = value
            normed = layer_norm(value, norms_ref[6:7, :], norms_ref[7:8, :])
            sums = sums + jnp.sum(normed * valid_ref[rows, :], axis=0, keepdims=True)
        sums_ref[...] = sums


def feed_bwd_kernel(normed_ref, grad_ref, *refs):
    up_refs, down_refs = refs[:2], refs[2:4]
    act_ref, slope_ref, dup_ref, ddown_ref, dnormed_ref, dhid = refs[4:]
    dhid[...] = low(dot(grad_ref[...], wide(*down_refs)) * slope_ref[0].astype(SINGLE))
    ddown_ref[0] = low(dot(grad_ref[...], act_ref[0], TN))
    dup_ref[0] = low(dot(normed_ref[...], dhid[...], TN))
    accumulate(dnormed_ref, dot(dhid[...], wide(*up_refs), NT))


def feed_bwd_last_kernel(normed_ref, grad_ref, *refs):
    act_ref, slope_ref, resid_ref, dresid_ref, dother_ref, norms_ref = refs[4:10]
    dup_ref, ddown_ref, out_ref, drows_ref, dnorms_ref, dhid, dnormed = refs[10:]
    feed_bwd_kernel(
        normed_ref, grad_ref, *refs[:4], act_ref, slope_ref, dup_ref, ddown_ref, dnormed, dhid
    )

    @pl.when(pl.program_id(0) == 1)
    def _():
        norm_rows_back(
            resid_ref, norms_ref, 4, dother_ref, dnormed, dresid_ref, out_ref, drows_ref, dnorms_ref
        )


def embed_kernel(patches_ref, weight_ref, valid_ref, norms_ref, start_ref, normed_ref):
    start_ref[...] = dot(patches_ref[...], weight_ref[...]) * valid_ref[...]
    for f in range(FRAMES):
        rows = frame_rows(f)
        normed_ref[rows, :] = low(
            layer_norm(start_ref[rows, :], norms_ref[0:1, :], norms_ref[1:2, :])
        )


def embed_bwd_kernel(
    patches_ref, start_ref, valid_ref, drows_ref, da_ref, db_ref, norms_ref, dnorms_ref, out_ref, dstart
):
    dim = start_ref.shape[1]
    d_gain, d_bias = jnp.zeros((1, dim), SINGLE), jnp.zeros((1, dim), SINGLE)
    for f in range(FRAMES):
        rows = frame_rows(f)
        d_value, gain, bias = norm_back(
            start_ref[rows, :], norms_ref[0:1, :], da_ref[rows, :] + db_ref[rows, :]
        )
        dstart[rows, :] = low((drows_ref[rows, :].astype(SINGLE) + d_value) * valid_ref[rows, :])
        d_gain, d_bias = d_gain + gain, d_bias + bias
    out_ref[:, :dim] = low(dot(patches_ref[...], dstart[...], TN))
    padded = jnp.concatenate(
        [d_gain, d_bias, dnorms_ref[...], jnp.zeros((120, dim), SINGLE)], axis=0
    )
    out_ref[:, dim : dim + 128] = low(padded.T)


def enter_frame_kernel(start_ref, *refs):
    parts, (weight_ref, norms_ref, out_ref, normed_ref, mixed) = refs[:FRAMES], refs[FRAMES:]
    for f in range(FRAMES):
        mixed[frame_rows(f), :] = parts[f][...]
    out_ref[...] = start_ref[...] + dot(mixed[...], weight_ref[...], NT)
    for f in range(FRAMES):
        rows = frame_rows(f)
        normed_ref[rows, :] = low(
            layer_norm(out_ref[rows, :], norms_ref[2:3, :], norms_ref[3:4, :])
        )


def loss_kernel(
    dim,
    classes,
    proj,
    clip_ref,
    facts_ref,
    small_ref,
    resid_ref,
    valid_ref,
    norms_ref,
    loss_ref,
    dsmall_ref,
    pooled_ref,
    dresid_ref,
    drows_ref,
    dnorms_ref,
    dpool,
):
    facts = facts_ref[...]
    count = facts.shape[0]
    label, mate = (facts[:, dim + i : dim + i + 1].astype(jnp.int32) for i in range(2))
    pooled = low(facts[:, :dim] / facts[:, dim + 2 : dim + 3])
    pooled_ref[...] = pooled
    both = dot(pooled, small_ref[...])
    lane = lax.broadcasted_iota(jnp.int32, both.shape, 1)
    logits = jnp.where(lane < classes, both, -1e30)
    hot = (lane == label).astype(SINGLE)
    top = jnp.max(logits, axis=1, keepdims=True)
    raised = jnp.exp(logits - top)
    total = jnp.sum(raised, axis=1, keepdims=True)
    cross = top + jnp.log(total) - jnp.sum(both * hot, axis=1, keepdims=True)
    d_logits = raised / total - hot
    embedding = jnp.where((lane >= classes) & (lane < classes + proj), both, 0.0)
    inverse = lax.rsqrt(jnp.sum(embedding * embedding, axis=1, keepdims=True) + 1e-06)
    unit = embedding * inverse
    exact = functools.partial(
        lax.dot_general, precision=EXACT, preferred_element_type=SINGLE
    )
    similar = exact(unit, unit, NT) / TEMPER
    row = lax.broadcasted_iota(jnp.int32, (count, count), 0)
    col = lax.broadcasted_iota(jnp.int32, (count, count), 1)
    mate_hot = (col == mate).astype(SINGLE)
    masked = jnp.where(row == col, -1e30, similar)
    top = jnp.max(masked, axis=1, keepdims=True)
    raised = jnp.exp(masked - top)
    total = jnp.sum(raised, axis=1, keepdims=True)
    contrast = top + jnp.log(total) - jnp.sum(similar * mate_hot, axis=1, keepdims=True)
    loss_ref[...] = jnp.sum(cross + contrast, axis=0, keepdims=True)
    d_similar = (raised / total - mate_hot) / TEMPER
    d_unit = exact(d_similar, unit, NN) + exact(d_similar, unit, TN)
    d_embed = inverse * d_unit - embedding * (inverse * inverse * inverse) * jnp.sum(
        embedding * d_unit, axis=1, keepdims=True
    )
    dsmall_ref[...] = low(jnp.where(lane < classes, d_logits, d_embed))
    dpool[...] = dot(dsmall_ref[...], small_ref[...], NT) / facts[:, dim + 2 : dim + 3]
    d_pooled = dpool[pl.ds(clip_ref[0], 1), :]
    d_gain, d_bias = jnp.zeros((1, dim), SINGLE), jnp.zeros((1, dim), SINGLE)
    for f in range(FRAMES):
        rows = frame_rows(f)
        d_value, gain, bias = norm_back(
            resid_ref[rows, :], norms_ref[6:7, :], valid_ref[rows, :] * d_pooled
        )
        dresid_ref[rows, :] = d_value
        drows_ref[rows, :] = low(d_value)
        d_gain, d_bias = d_gain + gain, d_bias + bias
    dnorms_ref[0:1, :] = d_gain
    dnorms_ref[1:2, :] = d_bias


def adam_step(master, first, second, clipped, rate):
    first_new = BETA_ONE * first + (1.0 - BETA_ONE) * clipped
    second_new = BETA_TWO * second + (1.0 - BETA_TWO) * clipped * clipped
    first_hat = first_new / (1.0 - BETA_ONE**STEP)
    second_hat = second_new / (1.0 - BETA_TWO**STEP)
    master_new = master - rate * (first_hat / (jnp.sqrt(second_hat) + ADAM_EPS) + DECAY * master)
    return (master_new, first_new, second_new)


def adam_kernel(classes, proj, total_ref, *refs):
    masters, firsts, seconds, parts, outs = (
        refs[0:8], refs[8:16], refs[16:24], refs[24:30], refs[31:]
    )
    norm = jnp.sqrt(total_ref[...])
    refs[30][...] = norm
    factor = jnp.minimum(1.0, CLIP_AT / (norm + 1e-06))
    early, small, first, second, up, down = (ref[...] * factor for ref in parts)
    dim = masters[0].shape[1]
    columns = lambda k: slice(GROUP * k, GROUP * (k + 1))
    todo = [
        (0, ..., early[:, :dim]),
        (1, ..., early[:, dim : dim + 128].T[:8]),
        (2, ..., small[:, :classes]),
        (3, ..., small[:, classes : classes + proj]),
        (6, ..., up),
        (7, ..., down),
    ]
    for layer, grad in enumerate((first, second)):
        todo += [(4, (layer, k), grad[:, columns(k)]) for k in range(3)]
        todo.append((5, layer, grad[:, columns(3)].T))
    for i, at, grad in todo:
        results = adam_step(
            masters[i][at], firsts[i][at], seconds[i][at], grad, NORM_RATE if i == 1 else RATE
        )
        for j, result in enumerate(results):
            outs[3 * i + j][at] = result


def whole(shape):
    return pl.BlockSpec(shape, lambda g: (0,) * len(shape))


def per_group(rows, width):
    return pl.BlockSpec((1, rows, width), lambda g: (g, 0, 0))


def columns_of(width):
    return pl.BlockSpec((1, FRAMES, width, SLOTS), lambda g: (g, 0, 0, 0))


def shaped(*shape, dtype=SINGLE):
    return jax.ShapeDtypeStruct(shape, dtype)


def spec_of(value):
    shape = value.shape
    if len(shape) == 4:
        return columns_of(shape[2])
    return per_group(*shape[1:]) if len(shape) == 3 else whole(shape)


def call(kernel, name, inputs, outputs, scratch=(), gflops=1, steps=2, in_specs=None):
    return pl.pallas_call(
        kernel,
        grid=(steps,),
        in_specs=in_specs or [spec_of(value) for value in inputs],
        out_specs=[spec_of(value) for value in outputs],
        out_shape=list(outputs),
        scratch_shapes=[pltpu.VMEM(shape, dtype) for shape, dtype in scratch],
        compiler_params=pltpu.CompilerParams(vmem_limit_bytes=GRANT),
        cost_estimate=pl.CostEstimate(
            flops=gflops * 10**9, bytes_accessed=8 << 20, transcendentals=0
        ),
        name=name,
    )(*inputs)


def by_group(width, rows=ROWS):
    return shaped(2, rows, width, dtype=LOWER)


def weight_specs(parts, rows):
    inputs, specs = [], []
    for value, half in parts:
        taken = rows
        if rows % 16 != 0:
            value = value[:, :, :rows].reshape(2, 1, -1, value.shape[-1])
            taken = value.shape[2]
        width = value.shape[3] if half is None else value.shape[3] // 2
        inputs.append(value)
        specs.append(
            pl.BlockSpec((1, value.shape[1], taken, width), lambda g, h=half or 0: (g, 0, 0, h))
        )
    return inputs, specs


def with_fetches(kernel, places):
    def wrapped(*refs):
        *refs, sems = refs
        buffers = refs[len(refs) - len(places) :]
        refs = list(refs[: len(refs) - len(places)])
        copies = [
            pltpu.make_async_copy(refs[at], buffer, sems.at[i])
            for i, (at, buffer) in enumerate(zip(places, buffers))
        ]

        @pl.when(pl.program_id(0) == 0)
        def _():
            for copy in copies:
                copy.start()

        @pl.when(pl.program_id(0) == 1)
        def _():
            for copy in copies:
                copy.wait()

        for at, buffer in zip(places, buffers):
            refs[at] = buffer
        kernel(*refs)

    return wrapped


def block_call(kernel, name, before, parts, rows, rest, outputs, scratch, gflops, later=False):
    parts, specs = weight_specs(parts, rows)
    specs = [spec_of(v) for v in before] + specs + [spec_of(v) for v in rest]
    inputs = (*before, *parts, *rest)
    if not later:
        return call(kernel, name, inputs, outputs, scratch, gflops, in_specs=specs)
    places = [
        i
        for i, value in enumerate(inputs)
        if value.dtype == SINGLE and value.shape == (ROWS, inputs[0].shape[1])
    ]
    for at in places:
        specs[at] = pl.BlockSpec(memory_space=pl.ANY)
    scratch = [pltpu.VMEM(shape, dtype) for shape, dtype in scratch]
    scratch += [pltpu.VMEM(inputs[at].shape, SINGLE) for at in places]
    return pl.pallas_call(
        with_fetches(kernel, places),
        grid=(2,),
        in_specs=specs,
        out_specs=[spec_of(value) for value in outputs],
        out_shape=list(outputs),
        scratch_shapes=scratch + [pltpu.SemaphoreType.DMA((len(places),))],
        compiler_params=pltpu.CompilerParams(vmem_limit_bytes=GRANT),
        cost_estimate=pl.CostEstimate(
            flops=gflops * 10**9, bytes_accessed=8 << 20, transcendentals=0
        ),
        name=name,
    )(*inputs)


def temporal_forward(normed, own, other, rows):
    dim = normed.shape[1]
    parts, specs = weight_specs([*own, *other], rows)
    place = [lambda g: jnp.minimum(g, 1)] * 2 + [lambda g: jnp.maximum(g - 2, 0)] * 2
    specs = [
        pl.BlockSpec(spec.block_shape, lambda g, at=at: (at(g), 0, 0, 0))
        for spec, at in zip(specs, place)
    ]
    width = parts[0].shape[3]
    return call(
        temporal_fwd_kernel,
        "temporal_forward",
        (normed, *parts),
        (shaped(4, FRAMES, QKV, SLOTS, dtype=LOWER), shaped(4, ROWS, GROUP, dtype=LOWER)),
        [((FRAMES, GROUP, SLOTS), LOWER), ((dim, width), LOWER), ((dim, width), LOWER)],
        40,
        4,
        [spec_of(normed), *specs],
    )


def temporal_backward(normed, grad, parts, rows, qkv, mixed, skip):
    dim = normed.shape[1]
    parts, specs = weight_specs(parts, rows)
    specs = [spec_of(normed), spec_of(grad), *specs]
    specs += [
        pl.BlockSpec((1, FRAMES, QKV, SLOTS), lambda g: (g + skip, 0, 0, 0)),
        pl.BlockSpec((1, ROWS, GROUP), lambda g: (g + skip, 0, 0)),
    ]
    return call(
        temporal_bwd_kernel,
        "temporal_backward",
        (normed, grad, *parts, qkv, mixed),
        (by_group(dim, dim), shaped(ROWS, dim)),
        [((ROWS, QKV), LOWER), ((FRAMES, GROUP, SLOTS), LOWER), ((FRAMES, QKV, SLOTS), LOWER)],
        14,
        2,
        specs,
    )


def spatial_forward(normed, parts, rows, key_extra, last=None):
    dim = normed.shape[1]
    outputs = (by_group(QKV), by_group(GROUP), by_group(GROUP), shaped(ROWS, dim))
    kernel, scratch = spatial_fwd_kernel, []
    if last is not None:
        kernel, scratch = spatial_fwd_last_kernel, [((ROWS, dim), SINGLE)]
        outputs += (shaped(ROWS, dim, dtype=LOWER),)
    rest = (key_extra, *(last or ()))
    return block_call(
        kernel, "spatial_forward", (normed,), parts, rows, rest, outputs, scratch, 15, last is not None
    )


def spatial_backward(normed, grad, parts, rows, qkv, mixed, extra, key_extra, last=None):
    dim = normed.shape[1]
    kernel, scratch = spatial_bwd_kernel, [((ROWS, QKV), LOWER)]
    outputs = (by_group(dim, dim), shaped(ROWS, dim))
    if last is not None:
        kernel, scratch = spatial_bwd_last_kernel, scratch + [((ROWS, dim), SINGLE)]
        outputs = (by_group(dim, dim), shaped(ROWS, dim, dtype=LOWER), shaped(2, dim))
    rest = (qkv, mixed, extra, key_extra, *(last or ()))
    return block_call(
        kernel, "spatial_backward", (normed, grad), parts, rows, rest, outputs, scratch, 30, last is not None
    )


def feed_forward(normed, parts, rows, last=None):
    dim, width = normed.shape[1], 2 * parts[0][0].shape[3]
    outputs = (by_group(width), by_group(width), shaped(ROWS, dim))
    kernel, scratch = feed_fwd_kernel, []
    if last is not None:
        kernel, scratch = feed_fwd_last_kernel, [((ROWS, dim), SINGLE)]
        outputs += (shaped(1, dim),)
    return block_call(
        kernel, "feed_forward", (normed,), parts, rows, last or (), outputs, scratch, 10, last is not None
    )


def feed_backward(normed, grad, parts, rows, act, slope, last=None):
    dim, width = normed.shape[1], 2 * parts[0][0].shape[3]
    kernel, scratch = feed_bwd_kernel, [((ROWS, width), LOWER)]
    outputs = (by_group(width, dim), by_group(width, dim), shaped(ROWS, dim))
    if last is not None:
        kernel, scratch = feed_bwd_last_kernel, scratch + [((ROWS, dim), SINGLE)]
        outputs += (shaped(ROWS, dim, dtype=LOWER), shaped(2, dim))
    rest = (act, slope, *(last or ()))
    return block_call(
        kernel, "feed_backward", (normed, grad), parts, rows, rest, outputs, scratch, 15, last is not None
    )


def embed(patches, weight, valid, norms):
    dim = patches.shape[1]
    outputs = (shaped(ROWS, dim), shaped(ROWS, dim, dtype=LOWER))
    return call(embed_kernel, "embed", (patches, weight, valid, norms), outputs, (), 15, 1)


def embed_backward(patches, start, valid, d_rows, d_a, d_b, norms, d_norms):
    dim = patches.shape[1]
    return call(
        embed_bwd_kernel,
        "embed_backward",
        (patches, start, valid, d_rows, d_a, d_b, norms, d_norms),
        (shaped(dim, dim + 128, dtype=LOWER),),
        [((ROWS, dim), LOWER)],
        30,
        1,
    )[0]


def enter_frame(start, parts, weight, norms):
    dim = start.shape[1]
    return call(
        enter_frame_kernel,
        "enter_frame",
        (start, *parts, weight, norms),
        (shaped(ROWS, dim), shaped(ROWS, dim, dtype=LOWER)),
        [((ROWS, dim), LOWER)],
        2,
        1,
    )


def all_losses(clip, facts, small, resid, valid, norms, classes, proj):
    count, dim = facts.shape[0], resid.shape[1]
    inputs = (facts, small, resid, valid, norms)
    return call(
        functools.partial(loss_kernel, dim, classes, proj),
        "losses",
        (clip, *inputs),
        (
            shaped(1, 1),
            shaped(count, dim, dtype=LOWER),
            shaped(count, dim, dtype=LOWER),
            shaped(ROWS, dim),
            shaped(ROWS, dim, dtype=LOWER),
            shaped(2, dim),
        ),
        [((count, dim), SINGLE)],
        1,
        1,
        [pl.BlockSpec(memory_space=pltpu.SMEM)] + [whole(value.shape) for value in inputs],
    )


def optimizer(total, masters, firsts, seconds, parts, classes, proj):
    inputs = (total, *masters, *firsts, *seconds, *parts)
    outputs = [shaped(1, 1)] + [shaped(*value.shape) for value in masters for _ in range(3)]
    return pl.pallas_call(
        functools.partial(adam_kernel, classes, proj),
        grid=(1,),
        in_specs=[whole(value.shape) for value in inputs],
        out_specs=[whole(value.shape) for value in outputs],
        out_shape=outputs,
        compiler_params=pltpu.CompilerParams(vmem_limit_bytes=GRANT),
        name="optimizer",
    )(*inputs)


def finish_kernel(count, token_ref, *refs):
    squares = jnp.zeros((1, 1), SINGLE)
    ins, outs = list(refs[: -count - 2]), refs[-count - 2 :]
    per = len(ins) // count
    for i in range(count):
        value = functools.reduce(
            jnp.add, (ref[...].astype(SINGLE) for ref in ins[per * i : per * (i + 1)])
        )
        outs[i][...] = value
        squares = squares + jnp.sum(
            jnp.sum(value * value, axis=1, keepdims=True), axis=0, keepdims=True
        )
    outs[count][...] = squares
    outs[count + 1][...] = token_ref[...]


def finish(token, lists):
    inputs = (token, *(term for terms in lists for term in terms))
    outputs = [shaped(*terms[0].shape) for terms in lists]
    outputs += [shaped(1, 1), shaped(*token.shape)]
    return call(
        functools.partial(finish_kernel, len(lists)),
        "finish",
        inputs,
        outputs,
        (),
        30,
        1,
        [whole(value.shape) for value in inputs],
    )


def pace_kernel(token_ref, out_ref):
    out_ref[...] = token_ref[...]


def pace(token):
    return call(pace_kernel, "pace", (token,), (shaped(*token.shape),), (), 30, 1)[0]


def tick(*values):
    return lax.optimization_barrier(values)


def summed(terms):
    return functools.reduce(jnp.add, (term.astype(SINGLE) for term in terms))


class Cube:
    def __init__(self, sizes):
        self.count = sizes["batch"] * sizes["head"]
        self.mine = lax.axis_index(ALL)
        batch_bits = sizes["batch"].bit_length() - 1
        self.batch_masks = [4 << k for k in reversed(range(batch_bits))]

    def swap(self, value, mask):
        return lax.ppermute(value, ALL, [(i, i ^ mask) for i in range(self.count)])

    def has(self, mask):
        return (self.mine & mask) != 0

    def join(self, value, *masks):
        for mask in masks:
            value = self.merge(value, self.swap(value, mask), mask)
        return value

    def fork(self, value):
        return self.stack(value, self.swap(value, 2), 2)

    def step(self, token, sends, late=(), work=None, hold=None, beside=None):
        values = [value for value, _ in (*sends, *late)]
        count = len(values)
        *values, token = tick(*values, *(hold or ()), token)
        if hold is not None:
            hold[:] = values[count:]
        values = values[:count]
        extra = beside(*hold) if beside is not None else []
        masks = [mask for _, mask in (*sends, *late)]
        received = [self.swap(value, mask) for value, mask in zip(values, masks)]
        count = len(sends)
        if work is not None:
            *done, paced = finish(token, work)
            *ended, token = tick(*received[:count], paced)
            return token, done, *ended, *received[count:]
        results = tick(*received[:count], *extra, pace(token))
        if extra:
            hold[:] = results[count:-1]
        return results[-1], *results[:count], *received[count:]


    def quads(self):
        *_, high, near, _ = self.batch_masks
        return [near, high, near | high]

    def gathered(self, value, others):
        near, high, _ = (self.has(mask) for mask in self.quads())
        p = [value, *others]
        p = [jnp.where(near, p[i ^ 1], p[i]) for i in range(4)]
        p = [jnp.where(high, p[i ^ 2], p[i]) for i in range(4)]
        shape = value.shape
        return jnp.stack(p, axis=-3).reshape(*shape[:-3], 4 * shape[-3], *shape[-2:])

    def quarter(self, terms):
        near, high, _ = (self.has(mask).astype(jnp.int32) for mask in self.quads())
        place = near + 2 * high
        views = [term.reshape(-1, 4, *term.shape[-2:]) for term in terms]
        part = lambda view, r: lax.dynamic_index_in_dim(view, place ^ r, 1, False)
        sends = [low(summed([part(view, r) for view in views])) for r in range(1, 4)]
        return sends, [part(view, 0) for view in views]

    def fourfold(self, sends):
        return list(zip(sends, self.quads()))

    def merge(self, value, other, mask):
        has = self.has(mask)
        both = jnp.stack([jnp.where(has, other, value), jnp.where(has, value, other)], axis=-3)
        shape = value.shape
        return both.reshape(*shape[:-3], 2 * shape[-3], *shape[-2:])

    def stack(self, value, other, mask):
        has = self.has(mask)
        return jnp.stack([jnp.where(has, other, value), jnp.where(has, value, other)])


    def cut(self, terms, mask):
        shape = terms[0].shape
        mine = self.has(mask).astype(jnp.int32)
        pairs = [
            term.reshape(*shape[:-3], shape[-3] // 2, 2, *shape[-2:]) for term in terms
        ]
        half = lambda pair, which: lax.dynamic_index_in_dim(pair, which, pair.ndim - 3, False)
        return low(summed([half(pair, 1 - mine) for pair in pairs])), [
            half(pair, mine) for pair in pairs
        ]

    def shed(self, terms, *masks):
        for mask in masks:
            send, keep = self.cut(terms, mask)
            terms = keep + [self.swap(send, mask)]
        return terms

    def cut_row(self, terms):
        mine = self.has(2).astype(jnp.int32)
        half = lambda term, which: lax.dynamic_index_in_dim(term, which, 0, False)
        return low(summed([half(term, 1 - mine) for term in terms])), [
            half(term, mine) for term in terms
        ]

    def meet(self, terms):
        send, keep = self.cut_row(terms)
        return keep + [self.swap(send, 2)]

    def total(self, value):
        for mask in [1, 2, *self.batch_masks[::-1]]:
            value = value + self.swap(value, mask)
        return value

    def swap_frames(self, parts):
        return [parts[0]] + [self.swap(parts[r], r) for r in range(1, FRAMES)]


def body(sizes, *args):
    patches, bucket, labels, partner = args[:4]
    views = [lambda v: v] * 4 + [
        lambda v: v.transpose(0, 2, 1, 3), lambda v: v, lambda v: v, lambda v: v.T
    ]
    masters, firsts, seconds = (
        [view(value) for view, value in zip(views, args[4 + 8 * i : 12 + 8 * i])] for i in range(3)
    )
    patch_weight, norm_params, head_weight, proj_weight, attn_in, attn_out, up, down = masters
    cube = Cube(sizes)
    dim = norm_params.shape[1] * cube.count
    classes, proj = head_weight.shape[1], proj_weight.shape[1]
    rows_wide, rows_small = attn_in.shape[2], patch_weight.shape[0]
    place = lax.axis_index(HEAD)

    *first, near, last = cube.batch_masks
    middle = dim // 2
    blocked = lambda value: value.reshape(*value.shape[:-2], -1, rows_wide, value.shape[-1])
    pack = lambda w_in, w_out: jnp.concatenate(
        [low(w_in[0]), low(w_in[1]), low(w_in[2]), low(w_out).T], axis=1
    )[None]
    patch_count = jnp.where(bucket == 1, PMAX, PSMALL)
    offset = jnp.arange(SLOTS)[None, :]
    number = (place ^ jnp.arange(FRAMES))[:, None]
    frame_valid = ((number * SLOTS + offset) < patch_count).reshape(ROWS, 1).astype(SINGLE)
    slot_valid = (jnp.broadcast_to(place * SLOTS + offset, (FRAMES, SLOTS)) < patch_count).reshape(
        ROWS, 1
    ).astype(SINGLE)
    lane = jnp.arange(HD)[None, :]
    key_extra = low(
        jnp.where(lane == 0, jnp.where(frame_valid > 0, 0.0, -1e30), (lane < 4).astype(SINGLE))
    )

    extra = -(-(rows_small + 1) // 16) * 16
    norm_row = low(norm_params).reshape(1, -1)
    first_w = jnp.concatenate(
        [
            pack(attn_in[0], attn_out[0])[0],
            low(patch_weight),
            jnp.pad(norm_row, ((0, extra - rows_small - 1), (0, dim - norm_row.shape[1]))),
        ]
    )[None]
    token = jnp.zeros((8, 128), SINGLE)
    clip, w_in, w_out, w_up, w_down = patches[0], attn_in[1], attn_out[1], up, down
    for mask in first:
        first_w, clip, w_in, w_out, w_up, w_down = tick(first_w, clip, w_in, w_out, w_up, w_down)
        token, other = cube.step(token, [(first_w, mask)])
        first_w = cube.merge(first_w, other, mask)
    blocks = jnp.pad(clip, ((0, ROWS - PMAX), (0, 0))).reshape(FRAMES, SLOTS, -1)
    blocks = jnp.where((place & 1) != 0, blocks[jnp.array([1, 0, 3, 2])], blocks)
    blocks = jnp.where((place & 2) != 0, blocks[jnp.array([2, 3, 0, 1])], blocks)
    blocks, token = tick(blocks, token)
    second_w = jnp.concatenate([pack(w_in, w_out)[0], low(w_up)])[None]
    small = jnp.concatenate([low(head_weight), low(proj_weight)], axis=1)
    small = jnp.pad(small, ((0, -rows_small % 16), (0, dim - small.shape[1])))
    down_w = jnp.concatenate([low(w_down), small])[None]

    token, other, *slots = cube.step(
        token, [(first_w, near)] + [(blocks[r], r) for r in range(1, FRAMES)]
    )
    first_w = cube.merge(first_w, other, near)
    by_frame = blocks.reshape(ROWS, -1)

    left, right = first_w[..., :middle], first_w[..., middle:]
    second_w = cube.join(second_w, *first[:-1])
    token, other_left, other_right, *others = cube.step(
        token, [(left, last), (right, 2)], cube.fourfold([second_w] * 3)
    )
    left, right = cube.merge(left, other_left, last), cube.stack(right, other_right, 2)

    left, right, *slots = tick(left, right, *slots)
    by_slot = jnp.concatenate([blocks[0], *slots])
    token, other_left, other_right = cube.step(token, [(left, 2), (right, last)])
    by_slot, slot_valid, token, *others = tick(by_slot, slot_valid, token, *others)
    own_first = (cube.stack(left, other_left, 2), cube.merge(right, other_right, last))

    second_w = cube.gathered(second_w, others)
    token, *other_first, other_left, other_right, other = cube.step(
        token,
        [(own_first[0], 1), (own_first[1], 1)],
        [(second_w[..., :middle], last), (second_w[..., middle:], 2)]
        + [(down_w, mask) for mask in first[:1]],
    )
    other_down = other
    joined = lambda parts, at: jnp.concatenate([part[:, :, at] for part in parts], axis=-1)
    early = [joined(parts, slice(rows_wide, None)) for parts in (own_first, other_first)]
    early = cube.stack(*early, 1).transpose(2, 1, 0, 3, 4)
    patch_copy = early[..., :rows_small, :].reshape(dim, dim)
    norms = early[..., rows_small, : norm_row.shape[1]].reshape(-1, 8, rows_small)
    norms = norms.transpose(1, 0, 2).reshape(8, dim).astype(SINGLE)
    start_slot, normed_t = embed(by_slot, patch_copy, slot_valid, norms)
    normed_t, other_left, other_right = tick(normed_t, other_left, other_right)
    left = cube.merge(second_w[..., :middle], other_left, last)
    right = cube.stack(second_w[..., middle:], other_right, 2)
    ours, theirs = slice(0, rows_wide), slice(rows_wide, None)
    other_left, other_right = (
        cube.swap(left[..., ours, :], 2), cube.swap(right[..., ours, :], last)
    )
    first_w = tuple([(part, None) for part in parts] for parts in (own_first, other_first))
    qkv_t, mixed_t = temporal_forward(normed_t, *first_w, rows_wide)
    mixed_t, other_left, other_right, other_down = tick(
        mixed_t, other_left, other_right, other_down
    )
    parts = [
        jnp.concatenate(
            [mixed_t[2 * (c ^ (r & 1)) + y][frame_rows(r)] for c in range(2) for y in range(2)],
            axis=1,
        )
        for r in range(FRAMES)
    ]
    down_w = cube.join(cube.merge(down_w, other_down, first[0]), *first[1:])

    hold = [other_left, other_right, patch_copy]
    token, *received, other = cube.step(
        token, [(parts[r], r) for r in range(1, FRAMES)] + [(down_w, near)], hold=hold
    )
    other_left, other_right, patch_copy = hold
    outs = [
        part[y, :, :rows_wide, GROUP:].reshape(dim, GROUP)
        for part in (own_first[1], other_first[1])
        for y in range(2)
    ]
    out_first = jnp.concatenate(outs, axis=1)
    start_frame = dot(by_frame, patch_copy) * frame_valid
    own_second = jnp.concatenate(
        [
            cube.stack(left[..., ours, :], other_left, 2),
            cube.merge(right[..., ours, :], other_right, last),
        ],
        axis=-1,
    )
    down_w = cube.merge(down_w, other, near)
    key_extra, own_second, down_w, out_first, start_frame = tick(
        key_extra, own_second, down_w, out_first, start_frame
    )

    resid_one, normed_s = enter_frame(start_frame, [parts[0], *received], out_first, norms)
    other_second = cube.swap(own_second, 1)
    other_left = cube.swap(left[..., theirs, :], 2)
    other_right = cube.swap(right[..., theirs, :], last)
    left_down, right_down = cube.join(down_w[..., :middle], last), cube.fork(down_w[..., middle:])
    qkv_s, mixed_s, extra_s = ([None, None] for _ in range(3))
    halves = lambda value: [(value, 0), (value, 1)]
    qkv_s[0], mixed_s[0], extra_s[0], branch = spatial_forward(
        normed_s, halves(own_second), rows_wide, key_extra
    )
    branch, normed_s, other_second, other_left, other_right, left_down, right_down = tick(
        branch, normed_s, other_second, other_left, other_right, left_down, right_down
    )
    own_up = (
        cube.stack(left[..., theirs, :], other_left, 2),
        cube.merge(right[..., theirs, :], other_right, last),
    )
    other_up = [cube.swap(part, 1) for part in own_up]
    left, right = cube.fork(left_down), cube.join(right_down, last)
    qkv_s[1], mixed_s[1], extra_s[1], resid_two, normed_m = spatial_forward(
        normed_s, halves(other_second), rows_wide, key_extra, (resid_one, branch, norms)
    )
    normed_m, left, right, *other_up = tick(normed_m, left, right, *other_up)

    own_down, other_down = (left, right), (cube.swap(left, 1), cube.swap(right, 1))
    own_feed = [(part, None) for part in (*own_up, *own_down)]
    other_feed = [(part, None) for part in (*other_up, *other_down)]
    act, slope = ([None, None] for _ in range(2))
    act[0], slope[0], branch = feed_forward(normed_m, own_feed, rows_wide)
    act[1], slope[1], resid_three, sums = feed_forward(
        normed_m, other_feed, rows_wide, (resid_two, branch, norms, frame_valid)
    )
    small = [
        joined(parts, slice(rows_wide, rows_wide + rows_small)) for parts in (own_down, other_down)
    ]
    small = cube.stack(*small, 1).transpose(2, 1, 0, 3, 4).reshape(dim, dim)

    for mask in (1, 2):
        sums = sums + cube.swap(sums, mask)
    facts = jnp.stack([labels[0], partner[0], FRAMES * patch_count[0]]).astype(SINGLE)
    gathered = jnp.concatenate([sums, jnp.pad(facts, (0, 125))[None]], axis=1)[None]
    gathered = cube.join(gathered, *first[:-1])
    others = [cube.swap(gathered, mask) for mask in cube.quads()]
    gathered = cube.join(cube.gathered(gathered, others), last)[:, 0]
    clip = lax.axis_index("batch").reshape(1)
    loss_sum, d_small, pooled_low, d_resid, d_rows, d_norms_f = all_losses(
        clip, gathered, small, resid_three, frame_valid, norms, classes, proj
    )

    d_up, d_down = [None, None], [None, None]
    d_up[1], d_down[1], d_normed = feed_backward(
        normed_m, d_rows, other_feed, rows_wide, act[1], slope[1]
    )
    up_other, down_other, d_normed, d_rows, normed_m = tick(
        d_up[1], d_down[1], d_normed, d_rows, normed_m
    )
    core_up, core_down = cube.swap(up_other, 1), cube.swap(down_other, 1)
    d_up[0], d_down[0], d_resid, d_rows, d_norms_m = feed_backward(
        normed_m,
        d_rows,
        own_feed,
        rows_wide,
        act[0],
        slope[0],
        (resid_two, d_resid, d_normed, norms),
    )
    d_resid, d_rows, up_own, down_own, core_up, core_down = tick(
        d_resid, d_rows, d_up[0], d_down[0], core_up, core_down
    )

    sum_up = cube.meet([blocked(up_own), blocked(core_up)])
    sum_down = cube.shed([blocked(down_own), blocked(core_down)], last)
    d_second = [None, None]
    d_second[1], d_normed = spatial_backward(
        normed_s, d_rows, halves(other_second), rows_wide, qkv_s[1], mixed_s[1], extra_s[1], key_extra
    )
    d_small = lax.dynamic_slice_in_dim(
        dot(pooled_low, d_small, TN), cube.mine * rows_small, rows_small, 0
    )
    second_other, d_normed, d_rows, normed_s, sum_up[-1], sum_down[-1], d_small = tick(
        d_second[1], d_normed, d_rows, normed_s, sum_up[-1], sum_down[-1], d_small
    )
    core_second = cube.swap(second_other, 1)
    sum_up, sum_down = cube.shed(sum_up, last), cube.meet(sum_down)
    d_second[0], d_rows, d_norms_s = spatial_backward(
        normed_s,
        d_rows,
        halves(own_second),
        rows_wide,
        qkv_s[0],
        mixed_s[0],
        extra_s[0],
        key_extra,
        (resid_one, d_resid, d_normed, norms),
    )
    d_rows, second_own, sum_up[-1], sum_down[-1], core_second = tick(
        d_rows, d_second[0], sum_up[-1], sum_down[-1], core_second
    )

    parts = split_frames(d_rows)
    send, sum_second = cube.cut([blocked(second_own), blocked(core_second)], last)
    def to_quarters(up_last, down_last):
        up, down = sum_up[:-1] + [up_last], sum_down[:-1] + [down_last]
        up, down = cube.shed(up, *first[-2::-1]), cube.shed(down, *first[-2::-1])
        kept.extend([cube.quarter(up)[1], cube.quarter(down)[1]])
        pairs = zip(cube.quarter(up)[0], cube.quarter(down)[0])
        return [jnp.concatenate(pair, axis=-2) for pair in pairs]

    kept, hold = [], [sum_up[-1], sum_down[-1]]
    token, *received, other = cube.step(
        token,
        [(parts[r], r) for r in range(1, FRAMES)],
        [(send, last)],
        hold=hold,
        beside=to_quarters,
    )
    sends, (sum_up, sum_down) = hold, kept
    d_rows = jnp.concatenate([parts[0], *received])
    sum_second.append(other)

    others = [cube.swap(send, mask) for send, mask in cube.fourfold(sends)]
    d_first, d_normed = [None, None], [None, None]
    d_first[1], d_normed[1] = temporal_backward(
        normed_t, d_rows, first_w[1], rows_wide, qkv_t, mixed_t, 2
    )
    first_other, d_normed[1], d_rows, normed_t, sum_second[-1] = tick(
        d_first[1], d_normed[1], d_rows, normed_t, sum_second[-1]
    )
    core_first = cube.swap(first_other, 1)
    sum_second = cube.meet(sum_second)
    d_first[0], d_normed[0] = temporal_backward(
        normed_t, d_rows, first_w[0], rows_wide, qkv_t, mixed_t, 0
    )
    d_rows, first_own, d_normed[0], core_first, sum_second[-1], *others = tick(
        d_rows, d_first[0], d_normed[0], core_first, sum_second[-1], *others
    )
    sum_up += [other[..., :rows_wide, :] for other in others]
    sum_down += [other[..., rows_wide:, :] for other in others]

    sum_first = [blocked(first_own), blocked(core_first)]
    send_left, left = cube.cut_row([term[..., :middle] for term in sum_first])
    send_right, right = cube.cut([term[..., middle:] for term in sum_first], last)
    sum_second = cube.shed(sum_second, *first[-2::-1])
    send_left, send_right, d_normed[0], d_norms_f, d_small, sum_second[-1] = tick(
        send_left, send_right, d_normed[0], d_norms_f, d_small, sum_second[-1]
    )
    other_left, other_right = cube.swap(send_left, 2), cube.swap(send_right, last)
    sends, sum_second = cube.quarter(sum_second)
    others = [cube.swap(send, mask) for send, mask in cube.fourfold(sends)]
    d_norms = jnp.concatenate([d_norms_s, d_norms_m, d_norms_f])
    d_early = embed_backward(
        by_slot, start_slot, slot_valid, d_rows, d_normed[0], d_normed[1], norms, d_norms
    )
    send, sum_early = cube.cut([d_early.reshape(-1, rows_small, dim + 128)], 1)
    other_left, other_right, send, token = tick(other_left, other_right, send, token)
    other = cube.swap(send, 1)
    left.append(other_left)
    right.append(other_right)
    sum_early.append(other)

    send_left, left = cube.cut(left, last)
    send_right, right = cube.cut_row(right)
    send, sum_early = cube.cut(sum_early, 2)
    flat = lambda terms: [summed(terms)[0]]
    token, other_left, other_right, other = cube.step(
        token, [(send_left, last), (send_right, 2), (send, 2)]
    )
    *others, token = tick(*others, token)
    sum_second += others
    sum_first = [jnp.concatenate([summed(left + [other_left]), summed(right + [other_right])], -1)]
    sum_early.append(other)

    sum_first = cube.shed(sum_first, *first[-2::-1])
    sends, sum_first = cube.quarter(sum_first)
    send, sum_early = cube.cut(sum_early, last)
    token, (d_second, d_up, d_down, squares), *others, other = cube.step(
        token,
        [*cube.fourfold(sends), (send, last)],
        work=[flat(terms) for terms in (sum_second, sum_up, sum_down)],
    )
    sum_first += others
    sum_early.append(other)

    sum_early = cube.shed(sum_early, *first[-2::-1])
    sends, sum_early = cube.quarter(sum_early)
    square = lambda value: jnp.sum(value * value)
    d_first = summed(sum_first)[0]
    token, *others = cube.step(token, cube.fourfold(sends))
    d_early = summed(sum_early + others)[0]
    squares = squares[0, 0] + square(d_small) + square(d_first)

    total = cube.total((squares + square(d_early)).reshape(1, 1))
    parts = (d_early, d_small, d_first, d_second, d_up, d_down)
    grad_norm, *updates = optimizer(total, masters, firsts, seconds, parts, classes, proj)
    updates = [views[i // 3](update) for i, update in enumerate(updates)]
    return (loss_sum[0, 0], grad_norm[0, 0], *updates)


def solution(mesh):
    sizes = dict(mesh.shape)
    split = Mesh(mesh.devices.reshape(sizes["batch"], 2, sizes["head"] // 2), ALL)
    placed = (
        P("batch", HEAD, None),
        P("batch"),
        P("batch"),
        P("batch"),
        P(ALL, None),
        P(None, ALL),
        P(ALL, None),
        P(ALL, None),
        P(None, "batch", None, HEAD),
        P(None, HEAD, "batch"),
        P("batch", HEAD),
        P(HEAD, "batch"),
        P(ALL, None),
        P(None, ALL),
        P(ALL, None),
        P(ALL, None),
        P(None, "batch", None, HEAD),
        P(None, HEAD, "batch"),
        P("batch", HEAD),
        P(HEAD, "batch"),
        P(ALL, None),
        P(None, ALL),
        P(ALL, None),
        P(ALL, None),
        P(None, "batch", None, HEAD),
        P(None, HEAD, "batch"),
        P("batch", HEAD),
        P(HEAD, "batch"),
    )
    return jax.shard_map(
        functools.partial(body, sizes),
        mesh=split,
        in_specs=placed,
        out_specs=(
            P(),
            P(),
            P(ALL, None),
            P(ALL, None),
            P(ALL, None),
            P(None, ALL),
            P(None, ALL),
            P(None, ALL),
            P(ALL, None),
            P(ALL, None),
            P(ALL, None),
            P(ALL, None),
            P(ALL, None),
            P(ALL, None),
            P(None, "batch", None, HEAD),
            P(None, "batch", None, HEAD),
            P(None, "batch", None, HEAD),
            P(None, HEAD, "batch"),
            P(None, HEAD, "batch"),
            P(None, HEAD, "batch"),
            P("batch", HEAD),
            P("batch", HEAD),
            P("batch", HEAD),
            P(HEAD, "batch"),
            P(HEAD, "batch"),
            P(HEAD, "batch"),
        ),
        check_vma=False,
    )
```

```python
import functools

import jax
import jax.numpy as jnp
from jax import lax
from jax.experimental import pallas as pl
from jax.experimental.pallas import tpu as pltpu
from jax.sharding import Mesh
from jax.sharding import PartitionSpec as P

HD = 64
FRAMES = 4
PMAX = 784
PSMALL = 196
STEP = 5
SLOTS = 208
ROWS = FRAMES * SLOTS
GROUP = 192
QKV = 3 * GROUP


EXACT = lax.Precision.HIGHEST
TEMPER = 0.05
BETA_ONE = 0.5
BETA_TWO = 0.5
RATE = 0.04
NORM_RATE = 0.3
DECAY = 0.05
ADAM_EPS = 1e-08
CLIP_AT = 1.0
LOWER = jnp.bfloat16
SINGLE = jnp.float32
ALL = ("batch", "row", "core")
HEAD = ("row", "core")
GRANT = 56 << 20

NN = (((1,), (0,)), ((), ()))
NT = (((1,), (1,)), ((), ()))
TN = (((0,), (0,)), ((), ()))


def dot(left, right, dims=NN):
    return lax.dot_general(left, right, dims, preferred_element_type=SINGLE)


def low(value):
    return value.astype(LOWER)


def layer_norm(value, gain, bias):
    center = value - jnp.mean(value, axis=-1, keepdims=True)
    spread = jnp.mean(center * center, axis=-1, keepdims=True)
    return center * lax.rsqrt(spread + 1e-06) * gain + bias


def wide(*refs):
    return jnp.concatenate([ref[0].reshape(-1, ref.shape[-1]) for ref in refs], axis=1)


def three_parts(value):
    high = low(value)
    rest = value - high.astype(SINGLE)
    middle = low(rest)
    return high, middle, low(rest - middle.astype(SINGLE))


def frame_probs(query, keys):
    scores = [jnp.sum(query * key, axis=0, keepdims=True) * HD ** (-0.5) for key in keys]
    top = functools.reduce(jnp.maximum, scores)
    raised = [jnp.exp(score - top) for score in scores]
    total = functools.reduce(jnp.add, raised)
    return [value / total for value in raised]


def rounded(value):
    return low(value).astype(SINGLE)


def frame_rows(f):
    return slice(SLOTS * f, SLOTS * (f + 1))


def split_frames(rows):
    return [rows[frame_rows(f)] for f in range(FRAMES)]


def head_features(which, head):
    return slice(GROUP * which + HD * head, GROUP * which + HD * (head + 1))


def temporal_fwd_kernel(
    normed_ref, own_left, own_right, other_left, other_right, qkv_ref, mixed_ref, out, left, right
):
    for chosen, parts in (
        (pl.program_id(0) < 2, (own_left, own_right)),
        (pl.program_id(0) >= 2, (other_left, other_right)),
    ):

        @pl.when(chosen)
        def _(parts=parts):
            left[...], right[...] = wide(parts[0]), wide(parts[1])

    for f in range(FRAMES):
        rows = normed_ref[frame_rows(f), :]
        qkv_ref[0, f, : 2 * GROUP, :] = low(dot(rows, left[...])).T
        qkv_ref[0, f, 2 * GROUP :, :] = low(dot(rows, right[:, :GROUP])).T
    for head in range(GROUP // HD):
        query, keys, values = (
            [qkv_ref[0, f, head_features(i, head), :].astype(SINGLE) for f in range(FRAMES)]
            for i in range(3)
        )
        for f in range(FRAMES):
            probs = frame_probs(query[f], keys)
            mixed = sum(rounded(prob) * value for prob, value in zip(probs, values))
            out[f, head_features(0, head), :] = low(mixed)
    for f in range(FRAMES):
        mixed_ref[0, frame_rows(f), :] = out[f].T


def temporal_bwd_kernel(
    normed_ref,
    grad_ref,
    left_ref,
    right_ref,
    qkv_ref,
    mixed_ref,
    dweight_ref,
    dnormed_ref,
    dqkv,
    dmix,
    dcol,
):
    scale = HD ** (-0.5)
    for f in range(FRAMES):
        dmix[f] = low(dot(grad_ref[frame_rows(f), :], wide(right_ref)[:, GROUP:])).T
    for head in range(GROUP // HD):
        query, keys, values = (
            [qkv_ref[0, f, head_features(i, head), :].astype(SINGLE) for f in range(FRAMES)]
            for i in range(3)
        )
        d_keys = [jnp.zeros((HD, SLOTS), SINGLE) for _ in range(FRAMES)]
        d_values = [jnp.zeros((HD, SLOTS), SINGLE) for _ in range(FRAMES)]
        for f in range(FRAMES):
            d_mixed = dmix[f, head_features(0, head), :].astype(SINGLE)
            probs = frame_probs(query[f], keys)
            d_probs = [jnp.sum(d_mixed * value, axis=0, keepdims=True) for value in values]
            row = sum(prob * d_prob for prob, d_prob in zip(probs, d_probs))
            d_query = jnp.zeros((HD, SLOTS), SINGLE)
            for g in range(FRAMES):
                d_score = rounded(probs[g] * (d_probs[g] - row))
                d_query = d_query + d_score * keys[g]
                d_keys[g] = d_keys[g] + d_score * query[f]
                d_values[g] = d_values[g] + rounded(probs[g]) * d_mixed
            dcol[f, head_features(0, head), :] = low(d_query * scale)
        for g in range(FRAMES):
            dcol[g, head_features(1, head), :] = low(d_keys[g] * scale)
            dcol[g, head_features(2, head), :] = low(d_values[g])
    for f in range(FRAMES):
        dqkv[frame_rows(f), :] = dcol[f].T
    finish_backward(normed_ref, grad_ref, left_ref, right_ref, mixed_ref, dweight_ref, dnormed_ref, dqkv)


def finish_backward(
    normed_ref, grad_ref, left_ref, right_ref, mixed_ref, dweight_ref, dnormed_ref, dqkv
):
    dweight_ref[0, :, :QKV] = low(dot(normed_ref[...], dqkv[...], TN))
    dweight_ref[0, :, QKV:] = low(dot(grad_ref[...], mixed_ref[0], TN))
    d_normed = dot(dqkv[:, : 2 * GROUP], wide(left_ref), NT) + dot(
        dqkv[:, 2 * GROUP :], wide(right_ref)[:, :GROUP], NT
    )

    accumulate(dnormed_ref, d_normed)


def lane_pieces(pieces, rows):
    lane = lax.broadcasted_iota(jnp.int32, (rows, HD), 1)
    result = jnp.zeros((rows, HD), SINGLE)
    for number, piece in enumerate(pieces):
        result = jnp.where(lane == number, piece.astype(SINGLE), result)
    return low(result)


def spatial_fwd_kernel(
    normed_ref, left_ref, right_ref, key_extra_ref, qkv_ref, mixed_ref, extra_ref, branch_ref
):
    qkv_ref[0, :, : 2 * GROUP] = low(dot(normed_ref[...], wide(left_ref)))
    qkv_ref[0, :, 2 * GROUP :] = low(dot(normed_ref[...], wide(right_ref)[:, :GROUP]))
    one = jnp.ones((ROWS, 1), SINGLE)
    for head in range(GROUP // HD):
        at = HD * head
        query = qkv_ref[0, :, at : at + HD] * jnp.asarray(HD ** (-0.5), LOWER)
        query = jnp.concatenate([query, lane_pieces([one], ROWS)], axis=1)
        keys = jnp.concatenate(
            [qkv_ref[0, :, GROUP + at : GROUP + at + HD], key_extra_ref[...]], axis=1
        )
        values = jnp.concatenate(
            [qkv_ref[0, :, 2 * GROUP + at : 2 * GROUP + at + HD], lane_pieces([one], ROWS)], axis=1
        )
        score = dot(query, keys, NT)
        top = jnp.max(score, axis=1, keepdims=True)
        mixed = dot(low(jnp.exp(score - top)), values)
        total = mixed[:, HD : HD + 1]
        mixed_ref[0, :, at : at + HD] = low(mixed[:, :HD] / total)
        logsum = -(top + jnp.log(total))
        extra_ref[0, :, at : at + HD] = lane_pieces([one, *three_parts(logsum)], ROWS)
    branch = dot(mixed_ref[0], wide(right_ref)[:, GROUP:], NT)

    accumulate(branch_ref, branch)


def spatial_fwd_last_kernel(
    normed_ref,
    left_ref,
    right_ref,
    key_extra_ref,
    resid_ref,
    branch_ref,
    norms_ref,
    qkv_ref,
    mixed_ref,
    extra_ref,
    out_ref,
    out_normed_ref,
    branch,
):
    spatial_fwd_kernel(
        normed_ref, left_ref, right_ref, key_extra_ref, qkv_ref, mixed_ref, extra_ref, branch
    )

    @pl.when(pl.program_id(0) == 1)
    def _():
        for f in range(FRAMES):
            rows = frame_rows(f)
            value = resid_ref[rows, :] + (branch_ref[rows, :] + branch[rows, :])
            out_ref[rows, :] = value
            out_normed_ref[rows, :] = low(layer_norm(value, norms_ref[4:5, :], norms_ref[5:6, :]))


def spatial_bwd_kernel(
    normed_ref,
    grad_ref,
    left_ref,
    right_ref,
    qkv_ref,
    mixed_ref,
    extra_ref,
    key_extra_ref,
    dweight_ref,
    dnormed_ref,
    dqkv,
):
    scale = HD ** (-0.5)
    d_mixed_all = low(dot(grad_ref[...], wide(right_ref)[:, GROUP:]))
    one = jnp.ones((ROWS, 1), SINGLE)
    for head in range(GROUP // HD):
        at = HD * head
        query = qkv_ref[0, :, at : at + HD]
        query_long = jnp.concatenate(
            [query * jnp.asarray(scale, LOWER), extra_ref[0, :, at : at + HD]], axis=1
        )
        d_mixed = d_mixed_all[:, at : at + HD]
        delta = -jnp.sum(
            d_mixed.astype(SINGLE) * mixed_ref[0, :, at : at + HD].astype(SINGLE),
            axis=1,
            keepdims=True,
        )
        d_mixed_long = jnp.concatenate([d_mixed, lane_pieces(three_parts(delta), ROWS)], axis=1)
        keys = qkv_ref[0, :, GROUP + at : GROUP + at + HD]
        values = qkv_ref[0, :, 2 * GROUP + at : 2 * GROUP + at + HD]
        keys_long = jnp.concatenate([keys, key_extra_ref[...]], axis=1)
        values_long = jnp.concatenate([values, lane_pieces([one] * 3, ROWS)], axis=1)
        prob = jnp.exp(dot(keys_long, query_long, NT))
        d_score = low(prob * dot(values_long, d_mixed_long, NT))
        dqkv[:, 2 * GROUP + at : 2 * GROUP + at + HD] = low(dot(low(prob), d_mixed))
        dqkv[:, GROUP + at : GROUP + at + HD] = low(dot(d_score, query) * scale)
        dqkv[:, at : at + HD] = low(dot(d_score, keys, TN) * scale)
    finish_backward(normed_ref, grad_ref, left_ref, right_ref, mixed_ref, dweight_ref, dnormed_ref, dqkv)


def spatial_bwd_last_kernel(
    normed_ref,
    grad_ref,
    left_ref,
    right_ref,
    qkv_ref,
    mixed_ref,
    extra_ref,
    key_extra_ref,
    resid_ref,
    dresid_ref,
    dother_ref,
    norms_ref,
    dweight_ref,
    drows_ref,
    dnorms_ref,
    dqkv,
    dnormed,
):
    spatial_bwd_kernel(
        normed_ref,
        grad_ref,
        left_ref,
    right_ref,
        qkv_ref,
        mixed_ref,
        extra_ref,
        key_extra_ref,
        dweight_ref,
        dnormed,
        dqkv,
    )

    @pl.when(pl.program_id(0) == 1)
    def _():
        norm_rows_back(
            resid_ref, norms_ref, 2, dother_ref, dnormed, dresid_ref, None, drows_ref, dnorms_ref
        )


def norm_back(value, gain, grad):
    center = value - jnp.mean(value, axis=-1, keepdims=True)
    inverse = lax.rsqrt(jnp.mean(center * center, axis=-1, keepdims=True) + 1e-06)
    hat = center * inverse
    scaled = grad * gain
    d_value = inverse * (
        scaled
        - jnp.mean(scaled, axis=-1, keepdims=True)
        - hat * jnp.mean(scaled * hat, axis=-1, keepdims=True)
    )
    return (
        d_value,
        jnp.sum(grad * hat, axis=0, keepdims=True),
        jnp.sum(grad, axis=0, keepdims=True),
    )


def norm_rows_back(
    resid_ref, norms_ref, at, dother_ref, dnormed_ref, dresid_ref, out_ref, rows_ref, dnorms_ref
):
    d_gain = jnp.zeros((1, resid_ref.shape[1]), SINGLE)
    d_bias = jnp.zeros((1, resid_ref.shape[1]), SINGLE)
    for f in range(FRAMES):
        rows = frame_rows(f)
        d_value, gain, bias = norm_back(
            resid_ref[rows, :],
            norms_ref[at : at + 1, :],
            dother_ref[rows, :] + dnormed_ref[rows, :],
        )
        d_value = d_value + dresid_ref[rows, :]
        if out_ref is not None:
            out_ref[rows, :] = d_value
        rows_ref[rows, :] = low(d_value)
        d_gain, d_bias = d_gain + gain, d_bias + bias
    dnorms_ref[0:1, :] = d_gain
    dnorms_ref[1:2, :] = d_bias


def accumulate(ref, value):
    first = pl.program_id(0) == 0
    ref[...] = jnp.where(first, value, ref[...] + value)


def feed_fwd_kernel(normed_ref, *refs):
    up_refs, down_refs = refs[:2], refs[2:4]
    act_ref, slope_ref, branch_ref = refs[4:]
    hidden = dot(normed_ref[...], wide(*up_refs))
    root = 0.7978845608028654
    square = hidden * hidden
    bend = jnp.tanh(hidden * (root + root * 0.044715 * square))
    half = 0.5 + 0.5 * bend
    act_ref[0] = low(hidden * half)
    slope_ref[0] = low(
        half + hidden * (0.5 - 0.5 * bend * bend) * (root + 3.0 * root * 0.044715 * square)
    )
    accumulate(branch_ref, dot(act_ref[0], wide(*down_refs), NT))


def feed_fwd_last_kernel(normed_ref, *refs):
    resid_ref, branch_ref, norms_ref, valid_ref = refs[4:8]
    act_ref, slope_ref, out_ref, sums_ref, branch = refs[8:]
    feed_fwd_kernel(normed_ref, *refs[:4], act_ref, slope_ref, branch)

    @pl.when(pl.program_id(0) == 1)
    def _():
        sums = jnp.zeros(sums_ref.shape, SINGLE)
        for f in range(FRAMES):
            rows = frame_rows(f)
            value = resid_ref[rows, :] + (branch_ref[rows, :] + branch[rows, :])
            out_ref[rows, :] = value
            normed = layer_norm(value, norms_ref[6:7, :], norms_ref[7:8, :])
            sums = sums + jnp.sum(normed * valid_ref[rows, :], axis=0, keepdims=True)
        sums_ref[...] = sums


def feed_bwd_kernel(normed_ref, grad_ref, *refs):
    up_refs, down_refs = refs[:2], refs[2:4]
    act_ref, slope_ref, dup_ref, ddown_ref, dnormed_ref, dhid = refs[4:]
    dhid[...] = low(dot(grad_ref[...], wide(*down_refs)) * slope_ref[0].astype(SINGLE))
    ddown_ref[0] = low(dot(grad_ref[...], act_ref[0], TN))
    dup_ref[0] = low(dot(normed_ref[...], dhid[...], TN))
    accumulate(dnormed_ref, dot(dhid[...], wide(*up_refs), NT))


def feed_bwd_last_kernel(normed_ref, grad_ref, *refs):
    act_ref, slope_ref, resid_ref, dresid_ref, dother_ref, norms_ref = refs[4:10]
    dup_ref, ddown_ref, out_ref, drows_ref, dnorms_ref, dhid, dnormed = refs[10:]
    feed_bwd_kernel(
        normed_ref, grad_ref, *refs[:4], act_ref, slope_ref, dup_ref, ddown_ref, dnormed, dhid
    )

    @pl.when(pl.program_id(0) == 1)
    def _():
        norm_rows_back(
            resid_ref, norms_ref, 4, dother_ref, dnormed, dresid_ref, out_ref, drows_ref, dnorms_ref
        )


def embed_kernel(patches_ref, weight_ref, valid_ref, norms_ref, start_ref, normed_ref):
    start_ref[...] = dot(patches_ref[...], weight_ref[...]) * valid_ref[...]
    for f in range(FRAMES):
        rows = frame_rows(f)
        normed_ref[rows, :] = low(
            layer_norm(start_ref[rows, :], norms_ref[0:1, :], norms_ref[1:2, :])
        )


def embed_bwd_kernel(
    patches_ref, start_ref, valid_ref, drows_ref, da_ref, db_ref, norms_ref, dnorms_ref, out_ref, dstart
):
    dim = start_ref.shape[1]
    d_gain, d_bias = jnp.zeros((1, dim), SINGLE), jnp.zeros((1, dim), SINGLE)
    for f in range(FRAMES):
        rows = frame_rows(f)
        d_value, gain, bias = norm_back(
            start_ref[rows, :], norms_ref[0:1, :], da_ref[rows, :] + db_ref[rows, :]
        )
        dstart[rows, :] = low((drows_ref[rows, :].astype(SINGLE) + d_value) * valid_ref[rows, :])
        d_gain, d_bias = d_gain + gain, d_bias + bias
    out_ref[:, :dim] = low(dot(patches_ref[...], dstart[...], TN))
    padded = jnp.concatenate(
        [d_gain, d_bias, dnorms_ref[...], jnp.zeros((120, dim), SINGLE)], axis=0
    )
    out_ref[:, dim : dim + 128] = low(padded.T)


def enter_frame_kernel(start_ref, *refs):
    parts, (weight_ref, norms_ref, out_ref, normed_ref, mixed) = refs[:FRAMES], refs[FRAMES:]
    for f in range(FRAMES):
        mixed[frame_rows(f), :] = parts[f][...]
    out_ref[...] = start_ref[...] + dot(mixed[...], weight_ref[...], NT)
    for f in range(FRAMES):
        rows = frame_rows(f)
        normed_ref[rows, :] = low(
            layer_norm(out_ref[rows, :], norms_ref[2:3, :], norms_ref[3:4, :])
        )


def loss_kernel(
    dim,
    classes,
    proj,
    clip_ref,
    facts_ref,
    small_ref,
    resid_ref,
    valid_ref,
    norms_ref,
    loss_ref,
    dsmall_ref,
    pooled_ref,
    dresid_ref,
    drows_ref,
    dnorms_ref,
    dpool,
):
    facts = facts_ref[...]
    count = facts.shape[0]
    label, mate = (facts[:, dim + i : dim + i + 1].astype(jnp.int32) for i in range(2))
    pooled = low(facts[:, :dim] / facts[:, dim + 2 : dim + 3])
    pooled_ref[...] = pooled
    both = dot(pooled, small_ref[...])
    lane = lax.broadcasted_iota(jnp.int32, both.shape, 1)
    logits = jnp.where(lane < classes, both, -1e30)
    hot = (lane == label).astype(SINGLE)
    top = jnp.max(logits, axis=1, keepdims=True)
    raised = jnp.exp(logits - top)
    total = jnp.sum(raised, axis=1, keepdims=True)
    cross = top + jnp.log(total) - jnp.sum(both * hot, axis=1, keepdims=True)
    d_logits = raised / total - hot
    embedding = jnp.where((lane >= classes) & (lane < classes + proj), both, 0.0)
    inverse = lax.rsqrt(jnp.sum(embedding * embedding, axis=1, keepdims=True) + 1e-06)
    unit = embedding * inverse
    exact = functools.partial(
        lax.dot_general, precision=EXACT, preferred_element_type=SINGLE
    )
    similar = exact(unit, unit, NT) / TEMPER
    row = lax.broadcasted_iota(jnp.int32, (count, count), 0)
    col = lax.broadcasted_iota(jnp.int32, (count, count), 1)
    mate_hot = (col == mate).astype(SINGLE)
    masked = jnp.where(row == col, -1e30, similar)
    top = jnp.max(masked, axis=1, keepdims=True)
    raised = jnp.exp(masked - top)
    total = jnp.sum(raised, axis=1, keepdims=True)
    contrast = top + jnp.log(total) - jnp.sum(similar * mate_hot, axis=1, keepdims=True)
    loss_ref[...] = jnp.sum(cross + contrast, axis=0, keepdims=True)
    d_similar = (raised / total - mate_hot) / TEMPER
    d_unit = exact(d_similar, unit, NN) + exact(d_similar, unit, TN)
    d_embed = inverse * d_unit - embedding * (inverse * inverse * inverse) * jnp.sum(
        embedding * d_unit, axis=1, keepdims=True
    )
    dsmall_ref[...] = low(jnp.where(lane < classes, d_logits, d_embed))
    dpool[...] = dot(dsmall_ref[...], small_ref[...], NT) / facts[:, dim + 2 : dim + 3]
    d_pooled = dpool[pl.ds(clip_ref[0], 1), :]
    d_gain, d_bias = jnp.zeros((1, dim), SINGLE), jnp.zeros((1, dim), SINGLE)
    for f in range(FRAMES):
        rows = frame_rows(f)
        d_value, gain, bias = norm_back(
            resid_ref[rows, :], norms_ref[6:7, :], valid_ref[rows, :] * d_pooled
        )
        dresid_ref[rows, :] = d_value
        drows_ref[rows, :] = low(d_value)
        d_gain, d_bias = d_gain + gain, d_bias + bias
    dnorms_ref[0:1, :] = d_gain
    dnorms_ref[1:2, :] = d_bias


def adam_step(master, first, second, clipped, rate):
    first_new = BETA_ONE * first + (1.0 - BETA_ONE) * clipped
    second_new = BETA_TWO * second + (1.0 - BETA_TWO) * clipped * clipped
    first_hat = first_new / (1.0 - BETA_ONE**STEP)
    second_hat = second_new / (1.0 - BETA_TWO**STEP)
    master_new = master - rate * (first_hat / (jnp.sqrt(second_hat) + ADAM_EPS) + DECAY * master)
    return (master_new, first_new, second_new)


def adam_kernel(classes, proj, total_ref, *refs):
    masters, firsts, seconds, parts, outs = (
        refs[0:8], refs[8:16], refs[16:24], refs[24:30], refs[31:]
    )
    norm = jnp.sqrt(total_ref[...])
    refs[30][...] = norm
    factor = jnp.minimum(1.0, CLIP_AT / (norm + 1e-06))
    early, small, first, second, up, down = (ref[...] * factor for ref in parts)
    dim = masters[0].shape[1]
    columns = lambda k: slice(GROUP * k, GROUP * (k + 1))
    todo = [
        (0, ..., early[:, :dim]),
        (1, ..., early[:, dim : dim + 128].T[:8]),
        (2, ..., small[:, :classes]),
        (3, ..., small[:, classes : classes + proj]),
        (6, ..., up),
        (7, ..., down),
    ]
    for layer, grad in enumerate((first, second)):
        todo += [(4, (layer, k), grad[:, columns(k)]) for k in range(3)]
        todo.append((5, layer, grad[:, columns(3)].T))
    for i, at, grad in todo:
        results = adam_step(
            masters[i][at], firsts[i][at], seconds[i][at], grad, NORM_RATE if i == 1 else RATE
        )
        for j, result in enumerate(results):
            outs[3 * i + j][at] = result


def whole(shape):
    return pl.BlockSpec(shape, lambda g: (0,) * len(shape))


def per_group(rows, width):
    return pl.BlockSpec((1, rows, width), lambda g: (g, 0, 0))


def columns_of(width):
    return pl.BlockSpec((1, FRAMES, width, SLOTS), lambda g: (g, 0, 0, 0))


def shaped(*shape, dtype=SINGLE):
    return jax.ShapeDtypeStruct(shape, dtype)


def spec_of(value):
    shape = value.shape
    if len(shape) == 4:
        return columns_of(shape[2])
    return per_group(*shape[1:]) if len(shape) == 3 else whole(shape)


def call(kernel, name, inputs, outputs, scratch=(), gflops=1, steps=2, in_specs=None):
    return pl.pallas_call(
        kernel,
        grid=(steps,),
        in_specs=in_specs or [spec_of(value) for value in inputs],
        out_specs=[spec_of(value) for value in outputs],
        out_shape=list(outputs),
        scratch_shapes=[pltpu.VMEM(shape, dtype) for shape, dtype in scratch],
        compiler_params=pltpu.CompilerParams(vmem_limit_bytes=GRANT),
        cost_estimate=pl.CostEstimate(
            flops=gflops * 10**9, bytes_accessed=8 << 20, transcendentals=0
        ),
        name=name,
    )(*inputs)


def by_group(width, rows=ROWS):
    return shaped(2, rows, width, dtype=LOWER)


def weight_specs(parts, rows):
    inputs, specs = [], []
    for value, half in parts:
        taken = rows
        if rows % 16 != 0:
            value = value[:, :, :rows].reshape(2, 1, -1, value.shape[-1])
            taken = value.shape[2]
        width = value.shape[3] if half is None else value.shape[3] // 2
        inputs.append(value)
        specs.append(
            pl.BlockSpec((1, value.shape[1], taken, width), lambda g, h=half or 0: (g, 0, 0, h))
        )
    return inputs, specs


def with_fetches(kernel, places):
    def wrapped(*refs):
        *refs, sems = refs
        buffers = refs[len(refs) - len(places) :]
        refs = list(refs[: len(refs) - len(places)])
        copies = [
            pltpu.make_async_copy(refs[at], buffer, sems.at[i])
            for i, (at, buffer) in enumerate(zip(places, buffers))
        ]

        @pl.when(pl.program_id(0) == 0)
        def _():
            for copy in copies:
                copy.start()

        @pl.when(pl.program_id(0) == 1)
        def _():
            for copy in copies:
                copy.wait()

        for at, buffer in zip(places, buffers):
            refs[at] = buffer
        kernel(*refs)

    return wrapped


def block_call(kernel, name, before, parts, rows, rest, outputs, scratch, gflops, later=False):
    parts, specs = weight_specs(parts, rows)
    specs = [spec_of(v) for v in before] + specs + [spec_of(v) for v in rest]
    inputs = (*before, *parts, *rest)
    if not later:
        return call(kernel, name, inputs, outputs, scratch, gflops, in_specs=specs)
    places = [
        i
        for i, value in enumerate(inputs)
        if value.dtype == SINGLE and value.shape == (ROWS, inputs[0].shape[1])
    ]
    for at in places:
        specs[at] = pl.BlockSpec(memory_space=pl.ANY)
    scratch = [pltpu.VMEM(shape, dtype) for shape, dtype in scratch]
    scratch += [pltpu.VMEM(inputs[at].shape, SINGLE) for at in places]
    return pl.pallas_call(
        with_fetches(kernel, places),
        grid=(2,),
        in_specs=specs,
        out_specs=[spec_of(value) for value in outputs],
        out_shape=list(outputs),
        scratch_shapes=scratch + [pltpu.SemaphoreType.DMA((len(places),))],
        compiler_params=pltpu.CompilerParams(vmem_limit_bytes=GRANT),
        cost_estimate=pl.CostEstimate(
            flops=gflops * 10**9, bytes_accessed=8 << 20, transcendentals=0
        ),
        name=name,
    )(*inputs)


def temporal_forward(normed, own, other, rows):
    dim = normed.shape[1]
    parts, specs = weight_specs([*own, *other], rows)
    place = [lambda g: jnp.minimum(g, 1)] * 2 + [lambda g: jnp.maximum(g - 2, 0)] * 2
    specs = [
        pl.BlockSpec(spec.block_shape, lambda g, at=at: (at(g), 0, 0, 0))
        for spec, at in zip(specs, place)
    ]
    width = parts[0].shape[3]
    return call(
        temporal_fwd_kernel,
        "temporal_forward",
        (normed, *parts),
        (shaped(4, FRAMES, QKV, SLOTS, dtype=LOWER), shaped(4, ROWS, GROUP, dtype=LOWER)),
        [((FRAMES, GROUP, SLOTS), LOWER), ((dim, width), LOWER), ((dim, width), LOWER)],
        40,
        4,
        [spec_of(normed), *specs],
    )


def temporal_backward(normed, grad, parts, rows, qkv, mixed, skip):
    dim = normed.shape[1]
    parts, specs = weight_specs(parts, rows)
    specs = [spec_of(normed), spec_of(grad), *specs]
    specs += [
        pl.BlockSpec((1, FRAMES, QKV, SLOTS), lambda g: (g + skip, 0, 0, 0)),
        pl.BlockSpec((1, ROWS, GROUP), lambda g: (g + skip, 0, 0)),
    ]
    return call(
        temporal_bwd_kernel,
        "temporal_backward",
        (normed, grad, *parts, qkv, mixed),
        (by_group(dim, dim), shaped(ROWS, dim)),
        [((ROWS, QKV), LOWER), ((FRAMES, GROUP, SLOTS), LOWER), ((FRAMES, QKV, SLOTS), LOWER)],
        14,
        2,
        specs,
    )


def spatial_forward(normed, parts, rows, key_extra, last=None):
    dim = normed.shape[1]
    outputs = (by_group(QKV), by_group(GROUP), by_group(GROUP), shaped(ROWS, dim))
    kernel, scratch = spatial_fwd_kernel, []
    if last is not None:
        kernel, scratch = spatial_fwd_last_kernel, [((ROWS, dim), SINGLE)]
        outputs += (shaped(ROWS, dim, dtype=LOWER),)
    rest = (key_extra, *(last or ()))
    return block_call(
        kernel, "spatial_forward", (normed,), parts, rows, rest, outputs, scratch, 15, last is not None
    )


def spatial_backward(normed, grad, parts, rows, qkv, mixed, extra, key_extra, last=None):
    dim = normed.shape[1]
    kernel, scratch = spatial_bwd_kernel, [((ROWS, QKV), LOWER)]
    outputs = (by_group(dim, dim), shaped(ROWS, dim))
    if last is not None:
        kernel, scratch = spatial_bwd_last_kernel, scratch + [((ROWS, dim), SINGLE)]
        outputs = (by_group(dim, dim), shaped(ROWS, dim, dtype=LOWER), shaped(2, dim))
    rest = (qkv, mixed, extra, key_extra, *(last or ()))
    return block_call(
        kernel, "spatial_backward", (normed, grad), parts, rows, rest, outputs, scratch, 30, last is not None
    )


def feed_forward(normed, parts, rows, last=None):
    dim, width = normed.shape[1], 2 * parts[0][0].shape[3]
    outputs = (by_group(width), by_group(width), shaped(ROWS, dim))
    kernel, scratch = feed_fwd_kernel, []
    if last is not None:
        kernel, scratch = feed_fwd_last_kernel, [((ROWS, dim), SINGLE)]
        outputs += (shaped(1, dim),)
    return block_call(
        kernel, "feed_forward", (normed,), parts, rows, last or (), outputs, scratch, 10, last is not None
    )


def feed_backward(normed, grad, parts, rows, act, slope, last=None):
    dim, width = normed.shape[1], 2 * parts[0][0].shape[3]
    kernel, scratch = feed_bwd_kernel, [((ROWS, width), LOWER)]
    outputs = (by_group(width, dim), by_group(width, dim), shaped(ROWS, dim))
    if last is not None:
        kernel, scratch = feed_bwd_last_kernel, scratch + [((ROWS, dim), SINGLE)]
        outputs += (shaped(ROWS, dim, dtype=LOWER), shaped(2, dim))
    rest = (act, slope, *(last or ()))
    return block_call(
        kernel, "feed_backward", (normed, grad), parts, rows, rest, outputs, scratch, 15, last is not None
    )


def embed(patches, weight, valid, norms):
    dim = patches.shape[1]
    outputs = (shaped(ROWS, dim), shaped(ROWS, dim, dtype=LOWER))
    return call(embed_kernel, "embed", (patches, weight, valid, norms), outputs, (), 15, 1)


def embed_backward(patches, start, valid, d_rows, d_a, d_b, norms, d_norms):
    dim = patches.shape[1]
    return call(
        embed_bwd_kernel,
        "embed_backward",
        (patches, start, valid, d_rows, d_a, d_b, norms, d_norms),
        (shaped(dim, dim + 128, dtype=LOWER),),
        [((ROWS, dim), LOWER)],
        30,
        1,
    )[0]


def enter_frame(start, parts, weight, norms):
    dim = start.shape[1]
    return call(
        enter_frame_kernel,
        "enter_frame",
        (start, *parts, weight, norms),
        (shaped(ROWS, dim), shaped(ROWS, dim, dtype=LOWER)),
        [((ROWS, dim), LOWER)],
        2,
        1,
    )


def all_losses(clip, facts, small, resid, valid, norms, classes, proj):
    count, dim = facts.shape[0], resid.shape[1]
    inputs = (facts, small, resid, valid, norms)
    return call(
        functools.partial(loss_kernel, dim, classes, proj),
        "losses",
        (clip, *inputs),
        (
            shaped(1, 1),
            shaped(count, dim, dtype=LOWER),
            shaped(count, dim, dtype=LOWER),
            shaped(ROWS, dim),
            shaped(ROWS, dim, dtype=LOWER),
            shaped(2, dim),
        ),
        [((count, dim), SINGLE)],
        1,
        1,
        [pl.BlockSpec(memory_space=pltpu.SMEM)] + [whole(value.shape) for value in inputs],
    )


def optimizer(total, masters, firsts, seconds, parts, classes, proj):
    inputs = (total, *masters, *firsts, *seconds, *parts)
    outputs = [shaped(1, 1)] + [shaped(*value.shape) for value in masters for _ in range(3)]
    return pl.pallas_call(
        functools.partial(adam_kernel, classes, proj),
        grid=(1,),
        in_specs=[whole(value.shape) for value in inputs],
        out_specs=[whole(value.shape) for value in outputs],
        out_shape=outputs,
        compiler_params=pltpu.CompilerParams(vmem_limit_bytes=GRANT),
        name="optimizer",
    )(*inputs)


def finish_kernel(count, token_ref, *refs):
    squares = jnp.zeros((1, 1), SINGLE)
    ins, outs = list(refs[: -count - 2]), refs[-count - 2 :]
    per = len(ins) // count
    for i in range(count):
        value = functools.reduce(
            jnp.add, (ref[...].astype(SINGLE) for ref in ins[per * i : per * (i + 1)])
        )
        outs[i][...] = value
        squares = squares + jnp.sum(
            jnp.sum(value * value, axis=1, keepdims=True), axis=0, keepdims=True
        )
    outs[count][...] = squares
    outs[count + 1][...] = token_ref[...]


def finish(token, lists):
    inputs = (token, *(term for terms in lists for term in terms))
    outputs = [shaped(*terms[0].shape) for terms in lists]
    outputs += [shaped(1, 1), shaped(*token.shape)]
    return call(
        functools.partial(finish_kernel, len(lists)),
        "finish",
        inputs,
        outputs,
        (),
        30,
        1,
        [whole(value.shape) for value in inputs],
    )


def pace_kernel(token_ref, out_ref):
    out_ref[...] = token_ref[...]


def pace(token):
    return call(pace_kernel, "pace", (token,), (shaped(*token.shape),), (), 30, 1)[0]


def tick(*values):
    return lax.optimization_barrier(values)


def summed(terms):
    return functools.reduce(jnp.add, (term.astype(SINGLE) for term in terms))


class Cube:
    def __init__(self, sizes):
        self.count = sizes["batch"] * sizes["head"]
        self.mine = lax.axis_index(ALL)
        batch_bits = sizes["batch"].bit_length() - 1
        self.batch_masks = [4 << k for k in reversed(range(batch_bits))]

    def swap(self, value, mask):
        return lax.ppermute(value, ALL, [(i, i ^ mask) for i in range(self.count)])

    def has(self, mask):
        return (self.mine & mask) != 0

    def join(self, value, *masks):
        for mask in masks:
            value = self.merge(value, self.swap(value, mask), mask)
        return value

    def fork(self, value):
        return self.stack(value, self.swap(value, 2), 2)

    def step(self, token, sends, late=(), work=None, hold=None, beside=None):
        values = [value for value, _ in (*sends, *late)]
        count = len(values)
        *values, token = tick(*values, *(hold or ()), token)
        if hold is not None:
            hold[:] = values[count:]
        values = values[:count]
        extra = beside(*hold) if beside is not None else []
        masks = [mask for _, mask in (*sends, *late)]
        received = [self.swap(value, mask) for value, mask in zip(values, masks)]
        count = len(sends)
        if work is not None:
            *done, paced = finish(token, work)
            *ended, token = tick(*received[:count], paced)
            return token, done, *ended, *received[count:]
        results = tick(*received[:count], *extra, pace(token))
        if extra:
            hold[:] = results[count:-1]
        return results[-1], *results[:count], *received[count:]


    def quads(self):
        *_, high, near, _ = self.batch_masks
        return [near, high, near | high]

    def gathered(self, value, others):
        near, high, _ = (self.has(mask) for mask in self.quads())
        p = [value, *others]
        p = [jnp.where(near, p[i ^ 1], p[i]) for i in range(4)]
        p = [jnp.where(high, p[i ^ 2], p[i]) for i in range(4)]
        shape = value.shape
        return jnp.stack(p, axis=-3).reshape(*shape[:-3], 4 * shape[-3], *shape[-2:])

    def quarter(self, terms):
        near, high, _ = (self.has(mask).astype(jnp.int32) for mask in self.quads())
        place = near + 2 * high
        views = [term.reshape(-1, 4, *term.shape[-2:]) for term in terms]
        part = lambda view, r: lax.dynamic_index_in_dim(view, place ^ r, 1, False)
        sends = [low(summed([part(view, r) for view in views])) for r in range(1, 4)]
        return sends, [part(view, 0) for view in views]

    def fourfold(self, sends):
        return list(zip(sends, self.quads()))

    def merge(self, value, other, mask):
        has = self.has(mask)
        both = jnp.stack([jnp.where(has, other, value), jnp.where(has, value, other)], axis=-3)
        shape = value.shape
        return both.reshape(*shape[:-3], 2 * shape[-3], *shape[-2:])

    def stack(self, value, other, mask):
        has = self.has(mask)
        return jnp.stack([jnp.where(has, other, value), jnp.where(has, value, other)])


    def cut(self, terms, mask):
        shape = terms[0].shape
        mine = self.has(mask).astype(jnp.int32)
        pairs = [
            term.reshape(*shape[:-3], shape[-3] // 2, 2, *shape[-2:]) for term in terms
        ]
        half = lambda pair, which: lax.dynamic_index_in_dim(pair, which, pair.ndim - 3, False)
        return low(summed([half(pair, 1 - mine) for pair in pairs])), [
            half(pair, mine) for pair in pairs
        ]

    def shed(self, terms, *masks):
        for mask in masks:
            send, keep = self.cut(terms, mask)
            terms = keep + [self.swap(send, mask)]
        return terms

    def cut_row(self, terms):
        mine = self.has(2).astype(jnp.int32)
        half = lambda term, which: lax.dynamic_index_in_dim(term, which, 0, False)
        return low(summed([half(term, 1 - mine) for term in terms])), [
            half(term, mine) for term in terms
        ]

    def meet(self, terms):
        send, keep = self.cut_row(terms)
        return keep + [self.swap(send, 2)]

    def total(self, value):
        for mask in [1, 2, *self.batch_masks[::-1]]:
            value = value + self.swap(value, mask)
        return value

    def swap_frames(self, parts):
        return [parts[0]] + [self.swap(parts[r], r) for r in range(1, FRAMES)]


def body(sizes, *args):
    patches, bucket, labels, partner = args[:4]
    views = [lambda v: v] * 4 + [
        lambda v: v.transpose(0, 2, 1, 3), lambda v: v, lambda v: v, lambda v: v.T
    ]
    masters, firsts, seconds = (
        [view(value) for view, value in zip(views, args[4 + 8 * i : 12 + 8 * i])] for i in range(3)
    )
    patch_weight, norm_params, head_weight, proj_weight, attn_in, attn_out, up, down = masters
    cube = Cube(sizes)
    dim = norm_params.shape[1] * cube.count
    classes, proj = head_weight.shape[1], proj_weight.shape[1]
    rows_wide, rows_small = attn_in.shape[2], patch_weight.shape[0]
    place = lax.axis_index(HEAD)

    *first, near, last = cube.batch_masks
    middle = dim // 2
    blocked = lambda value: value.reshape(*value.shape[:-2], -1, rows_wide, value.shape[-1])
    pack = lambda w_in, w_out: jnp.concatenate(
        [low(w_in[0]), low(w_in[1]), low(w_in[2]), low(w_out).T], axis=1
    )[None]
    patch_count = jnp.where(bucket == 1, PMAX, PSMALL)
    offset = jnp.arange(SLOTS)[None, :]
    number = (place ^ jnp.arange(FRAMES))[:, None]
    frame_valid = ((number * SLOTS + offset) < patch_count).reshape(ROWS, 1).astype(SINGLE)
    slot_valid = (jnp.broadcast_to(place * SLOTS + offset, (FRAMES, SLOTS)) < patch_count).reshape(
        ROWS, 1
    ).astype(SINGLE)
    lane = jnp.arange(HD)[None, :]
    key_extra = low(
        jnp.where(lane == 0, jnp.where(frame_valid > 0, 0.0, -1e30), (lane < 4).astype(SINGLE))
    )

    extra = -(-(rows_small + 1) // 16) * 16
    norm_row = low(norm_params).reshape(1, -1)
    first_w = jnp.concatenate(
        [
            pack(attn_in[0], attn_out[0])[0],
            low(patch_weight),
            jnp.pad(norm_row, ((0, extra - rows_small - 1), (0, dim - norm_row.shape[1]))),
        ]
    )[None]
    token = jnp.zeros((8, 128), SINGLE)
    clip, w_in, w_out, w_up, w_down = patches[0], attn_in[1], attn_out[1], up, down
    for mask in first:
        first_w, clip, w_in, w_out, w_up, w_down = tick(first_w, clip, w_in, w_out, w_up, w_down)
        token, other = cube.step(token, [(first_w, mask)])
        first_w = cube.merge(first_w, other, mask)
    blocks = jnp.pad(clip, ((0, ROWS - PMAX), (0, 0))).reshape(FRAMES, SLOTS, -1)
    blocks = jnp.where((place & 1) != 0, blocks[jnp.array([1, 0, 3, 2])], blocks)
    blocks = jnp.where((place & 2) != 0, blocks[jnp.array([2, 3, 0, 1])], blocks)
    blocks, token = tick(blocks, token)
    second_w = jnp.concatenate([pack(w_in, w_out)[0], low(w_up)])[None]
    small = jnp.concatenate([low(head_weight), low(proj_weight)], axis=1)
    small = jnp.pad(small, ((0, -rows_small % 16), (0, dim - small.shape[1])))
    down_w = jnp.concatenate([low(w_down), small])[None]

    token, other, *slots = cube.step(
        token, [(first_w, near)] + [(blocks[r], r) for r in range(1, FRAMES)]
    )
    first_w = cube.merge(first_w, other, near)
    by_frame = blocks.reshape(ROWS, -1)

    left, right = first_w[..., :middle], first_w[..., middle:]
    second_w = cube.join(second_w, *first[:-1])
    token, other_left, other_right, *others = cube.step(
        token, [(left, last), (right, 2)], cube.fourfold([second_w] * 3)
    )
    left, right = cube.merge(left, other_left, last), cube.stack(right, other_right, 2)

    left, right, *slots = tick(left, right, *slots)
    by_slot = jnp.concatenate([blocks[0], *slots])
    token, other_left, other_right = cube.step(token, [(left, 2), (right, last)])
    by_slot, slot_valid, token, *others = tick(by_slot, slot_valid, token, *others)
    own_first = (cube.stack(left, other_left, 2), cube.merge(right, other_right, last))

    second_w = cube.gathered(second_w, others)
    token, *other_first, other_left, other_right, other = cube.step(
        token,
        [(own_first[0], 1), (own_first[1], 1)],
        [(second_w[..., :middle], last), (second_w[..., middle:], 2)]
        + [(down_w, mask) for mask in first[:1]],
    )
    other_down = other
    joined = lambda parts, at: jnp.concatenate([part[:, :, at] for part in parts], axis=-1)
    early = [joined(parts, slice(rows_wide, None)) for parts in (own_first, other_first)]
    early = cube.stack(*early, 1).transpose(2, 1, 0, 3, 4)
    patch_copy = early[..., :rows_small, :].reshape(dim, dim)
    norms = early[..., rows_small, : norm_row.shape[1]].reshape(-1, 8, rows_small)
    norms = norms.transpose(1, 0, 2).reshape(8, dim).astype(SINGLE)
    start_slot, normed_t = embed(by_slot, patch_copy, slot_valid, norms)
    normed_t, other_left, other_right = tick(normed_t, other_left, other_right)
    left = cube.merge(second_w[..., :middle], other_left, last)
    right = cube.stack(second_w[..., middle:], other_right, 2)
    ours, theirs = slice(0, rows_wide), slice(rows_wide, None)
    other_left, other_right = (
        cube.swap(left[..., ours, :], 2), cube.swap(right[..., ours, :], last)
    )
    first_w = tuple([(part, None) for part in parts] for parts in (own_first, other_first))
    qkv_t, mixed_t = temporal_forward(normed_t, *first_w, rows_wide)
    mixed_t, other_left, other_right, other_down = tick(
        mixed_t, other_left, other_right, other_down
    )
    parts = [
        jnp.concatenate(
            [mixed_t[2 * (c ^ (r & 1)) + y][frame_rows(r)] for c in range(2) for y in range(2)],
            axis=1,
        )
        for r in range(FRAMES)
    ]
    down_w = cube.join(cube.merge(down_w, other_down, first[0]), *first[1:])

    hold = [other_left, other_right, patch_copy]
    token, *received, other = cube.step(
        token, [(parts[r], r) for r in range(1, FRAMES)] + [(down_w, near)], hold=hold
    )
    other_left, other_right, patch_copy = hold
    outs = [
        part[y, :, :rows_wide, GROUP:].reshape(dim, GROUP)
        for part in (own_first[1], other_first[1])
        for y in range(2)
    ]
    out_first = jnp.concatenate(outs, axis=1)
    start_frame = dot(by_frame, patch_copy) * frame_valid
    own_second = jnp.concatenate(
        [
            cube.stack(left[..., ours, :], other_left, 2),
            cube.merge(right[..., ours, :], other_right, last),
        ],
        axis=-1,
    )
    down_w = cube.merge(down_w, other, near)
    key_extra, own_second, down_w, out_first, start_frame = tick(
        key_extra, own_second, down_w, out_first, start_frame
    )

    resid_one, normed_s = enter_frame(start_frame, [parts[0], *received], out_first, norms)
    other_second = cube.swap(own_second, 1)
    other_left = cube.swap(left[..., theirs, :], 2)
    other_right = cube.swap(right[..., theirs, :], last)
    left_down, right_down = cube.join(down_w[..., :middle], last), cube.fork(down_w[..., middle:])
    qkv_s, mixed_s, extra_s = ([None, None] for _ in range(3))
    halves = lambda value: [(value, 0), (value, 1)]
    qkv_s[0], mixed_s[0], extra_s[0], branch = spatial_forward(
        normed_s, halves(own_second), rows_wide, key_extra
    )
    branch, normed_s, other_second, other_left, other_right, left_down, right_down = tick(
        branch, normed_s, other_second, other_left, other_right, left_down, right_down
    )
    own_up = (
        cube.stack(left[..., theirs, :], other_left, 2),
        cube.merge(right[..., theirs, :], other_right, last),
    )
    other_up = [cube.swap(part, 1) for part in own_up]
    left, right = cube.fork(left_down), cube.join(right_down, last)
    qkv_s[1], mixed_s[1], extra_s[1], resid_two, normed_m = spatial_forward(
        normed_s, halves(other_second), rows_wide, key_extra, (resid_one, branch, norms)
    )
    normed_m, left, right, *other_up = tick(normed_m, left, right, *other_up)

    own_down, other_down = (left, right), (cube.swap(left, 1), cube.swap(right, 1))
    own_feed = [(part, None) for part in (*own_up, *own_down)]
    other_feed = [(part, None) for part in (*other_up, *other_down)]
    act, slope = ([None, None] for _ in range(2))
    act[0], slope[0], branch = feed_forward(normed_m, own_feed, rows_wide)
    act[1], slope[1], resid_three, sums = feed_forward(
        normed_m, other_feed, rows_wide, (resid_two, branch, norms, frame_valid)
    )
    small = [
        joined(parts, slice(rows_wide, rows_wide + rows_small)) for parts in (own_down, other_down)
    ]
    small = cube.stack(*small, 1).transpose(2, 1, 0, 3, 4).reshape(dim, dim)

    for mask in (1, 2):
        sums = sums + cube.swap(sums, mask)
    facts = jnp.stack([labels[0], partner[0], FRAMES * patch_count[0]]).astype(SINGLE)
    gathered = jnp.concatenate([sums, jnp.pad(facts, (0, 125))[None]], axis=1)[None]
    gathered = cube.join(gathered, *first[:-1])
    others = [cube.swap(gathered, mask) for mask in cube.quads()]
    gathered = cube.join(cube.gathered(gathered, others), last)[:, 0]
    clip = lax.axis_index("batch").reshape(1)
    loss_sum, d_small, pooled_low, d_resid, d_rows, d_norms_f = all_losses(
        clip, gathered, small, resid_three, frame_valid, norms, classes, proj
    )

    d_up, d_down = [None, None], [None, None]
    d_up[1], d_down[1], d_normed = feed_backward(
        normed_m, d_rows, other_feed, rows_wide, act[1], slope[1]
    )
    up_other, down_other, d_normed, d_rows, normed_m = tick(
        d_up[1], d_down[1], d_normed, d_rows, normed_m
    )
    core_up, core_down = cube.swap(up_other, 1), cube.swap(down_other, 1)
    d_up[0], d_down[0], d_resid, d_rows, d_norms_m = feed_backward(
        normed_m,
        d_rows,
        own_feed,
        rows_wide,
        act[0],
        slope[0],
        (resid_two, d_resid, d_normed, norms),
    )
    d_resid, d_rows, up_own, down_own, core_up, core_down = tick(
        d_resid, d_rows, d_up[0], d_down[0], core_up, core_down
    )

    sum_up = cube.meet([blocked(up_own), blocked(core_up)])
    sum_down = cube.shed([blocked(down_own), blocked(core_down)], last)
    d_second = [None, None]
    d_second[1], d_normed = spatial_backward(
        normed_s, d_rows, halves(other_second), rows_wide, qkv_s[1], mixed_s[1], extra_s[1], key_extra
    )
    d_small = lax.dynamic_slice_in_dim(
        dot(pooled_low, d_small, TN), cube.mine * rows_small, rows_small, 0
    )
    second_other, d_normed, d_rows, normed_s, sum_up[-1], sum_down[-1], d_small = tick(
        d_second[1], d_normed, d_rows, normed_s, sum_up[-1], sum_down[-1], d_small
    )
    core_second = cube.swap(second_other, 1)
    sum_up, sum_down = cube.shed(sum_up, last), cube.meet(sum_down)
    d_second[0], d_rows, d_norms_s = spatial_backward(
        normed_s,
        d_rows,
        halves(own_second),
        rows_wide,
        qkv_s[0],
        mixed_s[0],
        extra_s[0],
        key_extra,
        (resid_one, d_resid, d_normed, norms),
    )
    d_rows, second_own, sum_up[-1], sum_down[-1], core_second = tick(
        d_rows, d_second[0], sum_up[-1], sum_down[-1], core_second
    )

    parts = split_frames(d_rows)
    send, sum_second = cube.cut([blocked(second_own), blocked(core_second)], last)
    def to_quarters(up_last, down_last):
        up, down = sum_up[:-1] + [up_last], sum_down[:-1] + [down_last]
        up, down = cube.shed(up, *first[-2::-1]), cube.shed(down, *first[-2::-1])
        kept.extend([cube.quarter(up)[1], cube.quarter(down)[1]])
        pairs = zip(cube.quarter(up)[0], cube.quarter(down)[0])
        return [jnp.concatenate(pair, axis=-2) for pair in pairs]

    kept, hold = [], [sum_up[-1], sum_down[-1]]
    token, *received, other = cube.step(
        token,
        [(parts[r], r) for r in range(1, FRAMES)],
        [(send, last)],
        hold=hold,
        beside=to_quarters,
    )
    sends, (sum_up, sum_down) = hold, kept
    d_rows = jnp.concatenate([parts[0], *received])
    sum_second.append(other)

    others = [cube.swap(send, mask) for send, mask in cube.fourfold(sends)]
    d_first, d_normed = [None, None], [None, None]
    d_first[1], d_normed[1] = temporal_backward(
        normed_t, d_rows, first_w[1], rows_wide, qkv_t, mixed_t, 2
    )
    first_other, d_normed[1], d_rows, normed_t, sum_second[-1] = tick(
        d_first[1], d_normed[1], d_rows, normed_t, sum_second[-1]
    )
    core_first = cube.swap(first_other, 1)
    sum_second = cube.meet(sum_second)
    d_first[0], d_normed[0] = temporal_backward(
        normed_t, d_rows, first_w[0], rows_wide, qkv_t, mixed_t, 0
    )
    d_rows, first_own, d_normed[0], core_first, sum_second[-1] = tick(
        d_rows, d_first[0], d_normed[0], core_first, sum_second[-1]
    )
    wide_parts = others

    sum_first = [blocked(first_own), blocked(core_first)]
    send_left, left = cube.cut_row([term[..., :middle] for term in sum_first])
    send_right, right = cube.cut([term[..., middle:] for term in sum_first], last)
    sum_second = cube.shed(sum_second, *first[-2::-1])
    send_left, send_right, d_normed[0], d_norms_f, d_small, sum_second[-1] = tick(
        send_left, send_right, d_normed[0], d_norms_f, d_small, sum_second[-1]
    )
    other_left, other_right = cube.swap(send_left, 2), cube.swap(send_right, last)
    sends, sum_second = cube.quarter(sum_second)
    others = [cube.swap(send, mask) for send, mask in cube.fourfold(sends)]
    d_norms = jnp.concatenate([d_norms_s, d_norms_m, d_norms_f])
    d_early = embed_backward(
        by_slot, start_slot, slot_valid, d_rows, d_normed[0], d_normed[1], norms, d_norms
    )
    send, sum_early = cube.cut([d_early.reshape(-1, rows_small, dim + 128)], 1)
    other_left, other_right, send, token, *wide_parts = tick(
        other_left, other_right, send, token, *wide_parts
    )
    sum_up += [other[..., :rows_wide, :] for other in wide_parts]
    sum_down += [other[..., rows_wide:, :] for other in wide_parts]
    other = cube.swap(send, 1)
    left.append(other_left)
    right.append(other_right)
    sum_early.append(other)

    send_left, left = cube.cut(left, last)
    send_right, right = cube.cut_row(right)
    send, sum_early = cube.cut(sum_early, 2)
    flat = lambda terms: [summed(terms)[0]]
    token, other_left, other_right, other = cube.step(
        token, [(send_left, last), (send_right, 2), (send, 2)]
    )
    *others, token = tick(*others, token)
    sum_second += others
    sum_first = [jnp.concatenate([summed(left + [other_left]), summed(right + [other_right])], -1)]
    sum_early.append(other)

    sum_first = cube.shed(sum_first, *first[-2::-1])
    sends, sum_first = cube.quarter(sum_first)
    send, sum_early = cube.cut(sum_early, last)
    token, (d_second, d_up, d_down, squares), *others, other = cube.step(
        token,
        [*cube.fourfold(sends), (send, last)],
        work=[flat(terms) for terms in (sum_second, sum_up, sum_down)],
    )
    sum_first += others
    sum_early.append(other)

    sum_early = cube.shed(sum_early, *first[-2::-1])
    sends, sum_early = cube.quarter(sum_early)
    square = lambda value: jnp.sum(value * value)
    d_first = summed(sum_first)[0]
    token, *others = cube.step(token, cube.fourfold(sends))
    d_early = summed(sum_early + others)[0]
    squares = squares[0, 0] + square(d_small) + square(d_first)

    total = cube.total((squares + square(d_early)).reshape(1, 1))
    parts = (d_early, d_small, d_first, d_second, d_up, d_down)
    grad_norm, *updates = optimizer(total, masters, firsts, seconds, parts, classes, proj)
    updates = [views[i // 3](update) for i, update in enumerate(updates)]
    return (loss_sum[0, 0], grad_norm[0, 0], *updates)


def solution(mesh):
    sizes = dict(mesh.shape)
    split = Mesh(mesh.devices.reshape(sizes["batch"], 2, sizes["head"] // 2), ALL)
    placed = (
        P("batch", HEAD, None),
        P("batch"),
        P("batch"),
        P("batch"),
        P(ALL, None),
        P(None, ALL),
        P(ALL, None),
        P(ALL, None),
        P(None, "batch", None, HEAD),
        P(None, HEAD, "batch"),
        P("batch", HEAD),
        P(HEAD, "batch"),
        P(ALL, None),
        P(None, ALL),
        P(ALL, None),
        P(ALL, None),
        P(None, "batch", None, HEAD),
        P(None, HEAD, "batch"),
        P("batch", HEAD),
        P(HEAD, "batch"),
        P(ALL, None),
        P(None, ALL),
        P(ALL, None),
        P(ALL, None),
        P(None, "batch", None, HEAD),
        P(None, HEAD, "batch"),
        P("batch", HEAD),
        P(HEAD, "batch"),
    )
    return jax.shard_map(
        functools.partial(body, sizes),
        mesh=split,
        in_specs=placed,
        out_specs=(
            P(),
            P(),
            P(ALL, None),
            P(ALL, None),
            P(ALL, None),
            P(None, ALL),
            P(None, ALL),
            P(None, ALL),
            P(ALL, None),
            P(ALL, None),
            P(ALL, None),
            P(ALL, None),
            P(ALL, None),
            P(ALL, None),
            P(None, "batch", None, HEAD),
            P(None, "batch", None, HEAD),
            P(None, "batch", None, HEAD),
            P(None, HEAD, "batch"),
            P(None, HEAD, "batch"),
            P(None, HEAD, "batch"),
            P("batch", HEAD),
            P("batch", HEAD),
            P("batch", HEAD),
            P(HEAD, "batch"),
            P(HEAD, "batch"),
            P(HEAD, "batch"),
        ),
        check_vma=False,
    )
```
